32 devices in a mesh: blk: 16 (over z, y, core), wa: 2 (over x).
Axes of the slice: x: 2, y: 2, z: 4, core: 2. Of those that a mesh axis runs over, the one named last changes fastest.
Arguments:
- features: bfloat16 [53248, 2048], P(('blk', 'wa')), may hold values from -6 to 6
- weight: bfloat16 [2048, 2048], P(('blk', 'wa')), may hold values from -0.375 to 0.375
- bias: bfloat16 [2048], P(('blk', 'wa')), may hold values from -3 to 3
- neighbours: int32 [16, 53248], P(None, ('blk', 'wa')), may hold values from 0 to 3199, as said below
- degrees: int32 [53248], P(('blk', 'wa')), may hold values from 4 to 16
- cluster_sizes: int32 [16], P('blk'), may hold values from 603 to 3016
- cotangent: bfloat16 [53248, 2048], P(('blk', 'wa')), may hold values from -6 to 6
Outputs:
- output: float32 [53248, 2048], P(('blk', 'wa'))
- grad_features: float32 [53248, 2048], P(('blk', 'wa'))
- grad_weight: float32 [2048, 2048], P(('blk', 'wa'))
- grad_bias: float32 [2048], P(('blk', 'wa'))
The draws below stay inside these ranges and needn't reach their ends.
Inputs may be any that keep to these rules, and one draw needn't show every extreme that they name: `neighbours`: an entry below 1664 names a live row of the same part; larger entries name leading rows of the cluster itself and of the two clusters beside it on the cycle. Slots past a node's degree hold entries of the same law.
All inputs are finite; a program needn't handle non-finite values.
Results may differ from the reference program's by a relative error of at most 0.0049.
Values may be sent and summed in bfloat16 or wider, within the bound.
No kernel may reach another device: no remote copies, remote signals or barrier semaphores. Data moves between devices by JAX's collectives and lax.ppermute only.
A program may use at most 192 MiB of HBM per device.

```python
import jax
import jax.numpy as jnp
from jax import lax

H = 2048
FANOUT = 16
NODES_DEV = 1664
BOUND = 256
CMAX = 3016
CMIN = 603
CLUSTERS = 16
HALVES = 2
NODES = 53248
TABLE = 3200
N_BLK = 16
N_WA = 2


def cluster_lengths(key):
    key = jax.random.fold_in(key, 11)
    first_key, second_key, third_key = jax.random.split(key, 3)
    lengths = jax.random.randint(first_key, (CLUSTERS,), CMIN, CMAX + 1)
    largest_at = jax.random.randint(second_key, (), 0, CLUSTERS)
    smallest_at = (largest_at + 1 + jax.random.randint(third_key, (), 0, CLUSTERS - 1)) % CLUSTERS
    indices = jnp.arange(CLUSTERS)
    lengths = jnp.where(indices == largest_at, CMAX, lengths)
    lengths = jnp.where(indices == smallest_at, CMIN, lengths)
    return lengths.astype(jnp.int32)


def draw_cluster_sizes(key, part):
    return cluster_lengths(key)


def draw_neighbours(key, part):
    lengths = cluster_lengths(key)
    key = jax.random.fold_in(key, 5)
    seg_key, local_key, remote_key, top_key, low_key = jax.random.split(key, 5)
    node_ids = jnp.arange(NODES, dtype=jnp.int32)
    device = node_ids // NODES_DEV
    cluster = device // HALVES
    halfway = device % HALVES
    live_count = (jnp.take(lengths, cluster) - halfway + HALVES - 1) // HALVES
    segment = jax.random.randint(seg_key, (FANOUT, NODES), 0, 5)
    local_pick = jax.random.randint(local_key, (FANOUT, NODES), 0, live_count[None, :])
    remote_pick = jax.random.randint(remote_key, (FANOUT, NODES), 0, HALVES * BOUND)
    remote_entry = NODES_DEV + (segment - 2) * HALVES * BOUND + remote_pick
    values = jnp.where(segment < 2, local_pick, remote_entry)
    flat_ids = jnp.arange(FANOUT * NODES, dtype=jnp.int32).reshape(FANOUT, NODES)
    top_place = jax.random.randint(top_key, (), 0, FANOUT * NODES)
    low_place = (top_place + 1 + jax.random.randint(low_key, (), 0, FANOUT * NODES - 1)) % (FANOUT * NODES)
    values = jnp.where(flat_ids == top_place, TABLE - 1, values)
    values = jnp.where(flat_ids == low_place, 0, values)
    return values.astype(jnp.int32)


def place_ends(array, stream_key, smallest, high):
    longest = array.shape.index(max(array.shape))
    spots = []
    for shift in (0, 1):
        where = [jax.random.randint(jax.random.fold_in(stream_key, axis), (), 0, length) for axis, length in enumerate(array.shape)]
        where[longest] = (where[longest] + shift) % array.shape[longest]
        spots.append(tuple(where))
    return array.at[spots[0]].set(smallest).at[spots[1]].set(high)


def with_spikes(array, rng, source, target, shards_of, factor):
    owner, partner = [(jnp.arange(array.shape[axis_at]) // (array.shape[axis_at] // shards_of)).reshape([-1 if axis == axis_at else 1 for axis in range(array.ndim)]) for axis_at in (source, target)]
    chosen = jax.random.permutation(rng, shards_of)[partner]
    strong = (owner == chosen) | (owner == (partner + shards_of // 2) % shards_of)
    return jnp.where(strong, factor * array, array)


def block_scale(stream_key, shape, cuts, low, top_value):
    loudness, own = 1.0, jax.random.fold_in(stream_key, 6)
    for dim, shards_of in cuts:
        draws = jnp.exp(jax.random.uniform(jax.random.fold_in(own, dim), (shards_of,), jnp.float32, low / len(cuts), top_value / len(cuts)))
        loudness = loudness * jnp.repeat(draws, shape[dim] // shards_of).reshape([-1 if axis == dim else 1 for axis in range(len(shape))])
    return loudness


def centred(own_key, shape, spread, most, cuts=(), kind=jnp.bfloat16):
    array = spread * jax.random.normal(own_key, shape, jnp.float32)
    if cuts:
        array = array * block_scale(own_key, shape, cuts, -0.22, 0.18)
    return jnp.clip(array, -most, most).astype(kind)


def bell_draw_with(rng, extent, width, limit, pieces, heavy, held_as=jnp.bfloat16):
    values = width * jax.random.normal(rng, extent, jnp.float32)
    if pieces:
        values = values * block_scale(rng, extent, pieces, -0.22, 0.18)
    return jnp.clip(with_spikes(values, jax.random.fold_in(rng, 3), *heavy), -limit, limit).astype(held_as)


def setup_inputs(seed: int = 0) -> dict:
    key_list = jax.random.split(jax.random.key(seed), 8)
    features = bell_draw_with(key_list[0], (NODES, H), 1.0, 6.0, ((0, 32),), (0, 1, 32, 2.75))
    weight = centred(key_list[1], (H, H), (H // 8) ** -0.5, 0.375, ((0, 32),))
    bias = centred(key_list[2], (H,), 0.5, 3.0, ((0, 32),))
    neighbours = draw_neighbours(jax.random.fold_in(key_list[7], 71), 0)
    degrees = place_ends(jax.random.randint(key_list[4], (NODES,), 4, FANOUT + 1), jax.random.fold_in(key_list[4], 1), 4, FANOUT).astype(jnp.int32)
    cluster_sizes = draw_cluster_sizes(jax.random.fold_in(key_list[7], 71), 0)
    cotangent = centred(key_list[6], (NODES, H), 1.0, 6.0, ((0, 32),))
    return {"features": features, "weight": weight, "bias": bias, "neighbours": neighbours, "degrees": degrees, "cluster_sizes": cluster_sizes, "cotangent": cotangent}


@jax.custom_vjp
def low(v):
    return lax.optimization_barrier(v.astype(jnp.bfloat16)).astype(jnp.float32)

@jax.custom_vjp
def low_back(v):
    return v

def low_keep(v):
    return (low(v), None)

def low_pass(kept, grad):
    return (grad,)

def back_keep(v):
    return (v, None)

def back_low(kept, grad):
    return (low(grad),)
low.defvjp(low_keep, low_pass)
low_back.defvjp(back_keep, back_low)

def table_targets(neighbours):
    node_ids = jnp.arange(NODES, dtype=jnp.int32)
    device = node_ids // NODES_DEV
    cluster = device // N_WA
    block = N_WA * BOUND
    beyond = neighbours - NODES_DEV
    segment = jnp.clip(beyond // block, 0, 2)
    within = beyond % block
    cycle_step = jnp.where(segment == 1, -1, jnp.where(segment == 2, 1, 0))
    source = (cluster[None, :] + cycle_step + N_BLK) % N_BLK
    remote = (source * N_WA + within // BOUND) * NODES_DEV + within % BOUND
    on_device = device[None, :] * NODES_DEV + neighbours
    return jnp.where(neighbours < NODES_DEV, on_device, remote).astype(jnp.int32)

def reference(features, weight, bias, neighbours, degrees, cluster_sizes, cotangent):
    targets = table_targets(neighbours)
    columns = jnp.arange(FANOUT, dtype=jnp.int32)[:, None]
    in_range = columns < degrees[None, :]
    inverse = 1.0 / (degrees.astype(jnp.float32) + 1.0)
    node_ids = jnp.arange(NODES, dtype=jnp.int32)
    position = N_WA * (node_ids % NODES_DEV) + node_ids // NODES_DEV % N_WA
    owner = (node_ids // (NODES_DEV * N_WA)).astype(jnp.int32)
    live_mask = (position < jnp.take(cluster_sizes, owner)).astype(jnp.float32)

    def forward(inputs, matrix, offset):
        summed = 2.0 * inputs
        for column in range(FANOUT):
            picked = jnp.take(inputs, targets[column], axis=0)
            summed = summed + jnp.where(in_range[column][:, None], picked, 0.0)
        blended = low(summed * inverse[:, None])
        product = low_back(jnp.dot(blended, matrix, precision=lax.Precision.HIGHEST, preferred_element_type=jnp.float32))
        return live_mask[:, None] * jax.nn.gelu(product + offset[None, :], approximate=True)
    output, pullback = jax.vjp(forward, features.astype(jnp.float32), weight.astype(jnp.float32), bias.astype(jnp.float32))
    gradients = pullback(cotangent.astype(jnp.float32))
    return (output, gradients[0], gradients[1], gradients[2])
```

```python
import functools
import math

import jax
import jax.numpy as jnp
from jax import lax
from jax.experimental import pallas as pl
from jax.experimental.pallas import tpu as pltpu
from jax.sharding import PartitionSpec as P

FANOUT = 16
BOUND = 256
CMAX = 3016
TILE = 256
F32 = jnp.float32
BF16 = jnp.bfloat16
VMEM = 60 * 1024 * 1024
GELU_A = math.sqrt(2 / math.pi)
GELU_B = 0.044715


def params():
    return pltpu.CompilerParams(vmem_limit_bytes=VMEM)


def cost(flops, nbytes):
    return pl.CostEstimate(flops=int(flops), bytes_accessed=int(nbytes), transcendentals=0)


def dot(a, b, ca, cb):
    return lax.dot_general(a, b, (((ca,), (cb,)), ((), ())), preferred_element_type=F32)


def small(value):
    return value.astype(F32).astype(BF16)


def counts_kernel(index_ref, out_ref):
    base = pl.program_id(0) * TILE
    rows = small(lax.broadcasted_iota(jnp.int32, (TILE, 128), 0))
    lanes = lax.broadcasted_iota(jnp.int32, (FANOUT, 128), 1)
    zero, one, two = (jnp.array(v, BF16) for v in (0, 1, 2))
    for c in range(0, out_ref.shape[1], 128):
        entry = small(jnp.clip(index_ref[:, c : c + 128] - base, -1, TILE))
        own = small(jnp.clip(lanes + (c - base), -1, TILE))
        total = jnp.where(own[0:1, :] == rows, two, zero)
        for s in range(FANOUT):
            total = total + jnp.where(entry[s : s + 1, :] == rows, one, zero)
        out_ref[:, c : c + 128] = total


def counts(index, tiles):
    n = index.shape[1]
    return pl.pallas_call(
        counts_kernel,
        grid=(tiles,),
        in_specs=[pl.BlockSpec((FANOUT, n), lambda i: (0, 0))],
        out_specs=pl.BlockSpec((TILE, n), lambda i: (i, 0)),
        out_shape=jax.ShapeDtypeStruct((tiles * TILE, n), BF16),
        compiler_params=params(),
        cost_estimate=cost(0, tiles * TILE * n * 16),
        name="counts",
    )(index)


def gather_own_kernel(c_ref, t_ref, o_ref):
    o_ref[...] = dot(c_ref[...], t_ref[...], 0, 0)


def gather_own(adjacency, features, live):
    h = features.shape[1]
    return pl.pallas_call(
        gather_own_kernel,
        grid=(live // TILE,),
        in_specs=[pl.BlockSpec((live, TILE), lambda i: (0, i)), pl.BlockSpec((live, h), lambda i: (0, 0))],
        out_specs=pl.BlockSpec((TILE, h), lambda i: (i, 0)),
        out_shape=jax.ShapeDtypeStruct((live, h), F32),
        compiler_params=params(),
        cost_estimate=cost(2 * live * live * h, live * h * 6),
        name="gather_own",
    )(adjacency, features)


def gather_bound_kernel(c_ref, part_ref, inv_ref, *refs):
    o_ref = refs[-1]
    total = part_ref[...]
    for k, ref in enumerate(refs[:-1]):
        total = total + dot(c_ref[k * BOUND : (k + 1) * BOUND, :], ref[...], 0, 0)
    o_ref[...] = (total * inv_ref[...]).astype(BF16)


def gather_bound(adjacency, part, inverse, blocks):
    live, h = part.shape
    rest = adjacency.shape[0] - live
    return pl.pallas_call(
        gather_bound_kernel,
        grid=(live // TILE,),
        in_specs=[
            pl.BlockSpec((pl.Element(rest), pl.Element(TILE)), lambda i: (live, i * TILE)),
            pl.BlockSpec((TILE, h), lambda i: (i, 0)),
            pl.BlockSpec((TILE, 1), lambda i: (i, 0)),
        ]
        + [pl.BlockSpec((BOUND, h), lambda i: (0, 0))] * len(blocks),
        out_specs=pl.BlockSpec((TILE, h), lambda i: (i, 0)),
        out_shape=jax.ShapeDtypeStruct((live, h), BF16),
        compiler_params=params(),
        cost_estimate=cost(2 * live * rest * h, live * h * 6),
        name="gather_bound",
    )(adjacency, part, inverse, *blocks)


def layer_kernel(live_ref, m_ref, w_ref, b_ref, ct_ref, o_ref, gl_ref, gb_ref, *, tiles):
    i = pl.program_id(0)

    @pl.when(i == 0)
    def _():
        gb_ref[...] = jnp.zeros_like(gb_ref)

    @pl.when(i == tiles)
    def _():
        o_ref[...] = jnp.zeros_like(o_ref)

    @pl.when(i < tiles)
    def _():
        live = i * TILE + lax.broadcasted_iota(jnp.int32, (TILE, 256), 0) < live_ref[0]
        for j in range(0, w_ref.shape[1], 256):
            at = slice(j, j + 256)
            v = dot(m_ref[...], w_ref[:, at], 1, 0) + b_ref[:, at]
            square = v * v
            t = jnp.tanh(v * (GELU_A + (GELU_A * GELU_B) * square))
            half = 0.5 + 0.5 * t
            o_ref[:, at] = jnp.where(live, v * half, 0.0)
            slope = half + (0.5 * v) * (1 - t * t) * (GELU_A + (3 * GELU_A * GELU_B) * square)
            grad = jnp.where(live, ct_ref[:, at].astype(F32) * slope, 0.0)
            gl_ref[:, at] = grad.astype(BF16)
            gb_ref[:, at] += jnp.sum(grad.reshape(TILE // 8, 8, 256), axis=0)


def layer(live_count, mixed, matrix, offset, cotangent):
    live, h = mixed.shape
    nodes, n = cotangent.shape
    tiles = live // TILE

    def used(i, s):
        return (jnp.minimum(i, tiles - 1), 0)

    return pl.pallas_call(
        functools.partial(layer_kernel, tiles=tiles),
        grid_spec=pltpu.PrefetchScalarGridSpec(
            num_scalar_prefetch=1,
            grid=(tiles + 1,),
            in_specs=[
                pl.BlockSpec((TILE, h), used),
                pl.BlockSpec((h, n), lambda i, s: (0, 0)),
                pl.BlockSpec((1, n), lambda i, s: (0, 0)),
                pl.BlockSpec((TILE, n), used),
            ],
            out_specs=[
                pl.BlockSpec((TILE, n), lambda i, s: (i, 0)),
                pl.BlockSpec((TILE, n), used),
                pl.BlockSpec((8, n), lambda i, s: (0, 0)),
            ],
        ),
        out_shape=[
            jax.ShapeDtypeStruct((nodes, n), F32),
            jax.ShapeDtypeStruct((live, n), BF16),
            jax.ShapeDtypeStruct((8, n), F32),
        ],
        compiler_params=params(),
        cost_estimate=cost(2 * live * h * n, live * n * 20),
        name="layer",
    )(live_count, mixed, matrix, offset, cotangent)


def grad_weight_kernel(half_ref, m_ref, g_ref, o_ref):
    o_ref[...] = dot(m_ref[...], g_ref[...], 0, 0).astype(o_ref.dtype)


def grad_weight_half(half, mixed, grad_low, dtype):
    live, h = mixed.shape
    n = grad_low.shape[1] // 2
    return pl.pallas_call(
        grad_weight_kernel,
        grid_spec=pltpu.PrefetchScalarGridSpec(
            num_scalar_prefetch=1,
            grid=(h // TILE,),
            in_specs=[
                pl.BlockSpec((live, TILE), lambda i, s: (0, i)),
                pl.BlockSpec((live, n), lambda i, s: (0, s[0])),
            ],
            out_specs=pl.BlockSpec((TILE, n), lambda i, s: (i, 0)),
        ),
        out_shape=jax.ShapeDtypeStruct((h, n), dtype),
        compiler_params=params(),
        cost_estimate=cost(2 * live * h * n, live * h * 4),
        name="grad_weight",
    )(half, mixed, grad_low)


def grad_mixed_kernel(g_ref, w_ref, inv_ref, o_ref):
    o_ref[...] = (dot(g_ref[...], w_ref[...], 1, 1) * inv_ref[...]).astype(BF16)


def grad_mixed(grad_low, matrix, inverse):
    live, n = grad_low.shape
    h = matrix.shape[0]
    return pl.pallas_call(
        grad_mixed_kernel,
        grid=(live // TILE,),
        in_specs=[
            pl.BlockSpec((TILE, n), lambda i: (i, 0)),
            pl.BlockSpec((h, n), lambda i: (0, 0)),
            pl.BlockSpec((TILE, 1), lambda i: (i, 0)),
        ],
        out_specs=pl.BlockSpec((TILE, h), lambda i: (i, 0)),
        out_shape=jax.ShapeDtypeStruct((live, h), BF16),
        compiler_params=params(),
        cost_estimate=cost(2 * live * h * n, live * h * 4),
        name="grad_mixed",
    )(grad_low, matrix, inverse)


def scatter_bound_kernel(c_ref, g_ref, *outs):
    i = pl.program_id(0)
    part = dot(c_ref[...], g_ref[...], 1, 0).astype(BF16)
    for k, out in enumerate(outs):

        @pl.when(i == k)
        def _():
            out[...] = part


def scatter_bound(adjacency, grads):
    live, h = grads.shape
    blocks = (adjacency.shape[0] - live) // BOUND
    return pl.pallas_call(
        scatter_bound_kernel,
        grid=(blocks,),
        in_specs=[
            pl.BlockSpec((BOUND, live), lambda i: (i + live // BOUND, 0)),
            pl.BlockSpec((live, h), lambda i: (0, 0)),
        ],
        out_specs=[pl.BlockSpec((BOUND, h), lambda i: (0, 0))] * blocks,
        out_shape=[jax.ShapeDtypeStruct((BOUND, h), BF16)] * blocks,
        compiler_params=params(),
        cost_estimate=cost(2 * blocks * BOUND * live * h, live * h * 4),
        name="scatter_bound",
    )(adjacency, grads)


def scatter_own_kernel(c_ref, g_ref, o_ref, *, tiles):
    i = pl.program_id(0)

    @pl.when(i < tiles)
    def _():
        o_ref[...] = dot(c_ref[...], g_ref[...], 1, 0)

    @pl.when(i == tiles)
    def _():
        o_ref[...] = jnp.zeros_like(o_ref)


def scatter_own(adjacency, grads, nodes):
    live, h = grads.shape
    tiles = live // TILE
    return pl.pallas_call(
        functools.partial(scatter_own_kernel, tiles=tiles),
        grid=(tiles + 1,),
        in_specs=[
            pl.BlockSpec((TILE, live), lambda i: (jnp.minimum(i, tiles - 1), 0)),
            pl.BlockSpec((live, h), lambda i: (0, 0)),
        ],
        out_specs=pl.BlockSpec((TILE, h), lambda i: (i, 0)),
        out_shape=jax.ShapeDtypeStruct((nodes, h), F32),
        compiler_params=params(),
        cost_estimate=cost(2 * live * live * h, live * h * 6),
        name="scatter_own",
    )(adjacency, grads)


def add_returned_kernel(g_ref, *refs):
    total = g_ref[...]
    for ref in refs[:-1]:
        total = total + ref[...].astype(F32)
    refs[-1][...] = total


def add_returned(grads, returned):
    h = grads.shape[1]
    rows = pl.BlockSpec((64, h), lambda i: (i, 0))
    return pl.pallas_call(
        add_returned_kernel,
        grid=(BOUND // 64,),
        in_specs=[rows] * (1 + len(returned)),
        out_specs=rows,
        out_shape=jax.ShapeDtypeStruct(grads.shape, F32),
        input_output_aliases={0: 0},
        compiler_params=params(),
        cost_estimate=cost(0, BOUND * h * 14),
        name="add_returned",
    )(grads, *returned)


def body(features, weight, bias, neighbours, degrees, cluster_sizes, cotangent):
    axes = ("blk", "wa")
    n_blk, n_wa = lax.axis_size("blk"), lax.axis_size("wa")
    devices = n_blk * n_wa
    blk, wa = lax.axis_index("blk"), lax.axis_index("wa")
    core = blk % 2
    n_hi = n_blk // 4
    nodes, h = features.shape
    live = min(nodes, -(-(-(-CMAX // n_wa)) // TILE) * TILE)

    def permute(value, target):
        pairs = [(b * n_wa + w, target(b, w)) for b in range(n_blk) for w in range(n_wa)]
        return lax.ppermute(value, axes, [(s, b * n_wa + w) for s, (b, w) in pairs])

    def swap_wa(value):
        return permute(value, lambda b, w: (b, 1 - w))

    def swap_core(value):
        return permute(value, lambda b, w: (b ^ 1, w))

    def swap_outer(value):
        return permute(value, lambda b, w: ((b + (1 if b % 2 else -1)) % n_blk, w))

    def swap_lo(value):
        return permute(value, lambda b, w: (b ^ 2, w))

    def rotate_hi(value, k):
        return permute(value, lambda b, w: ((b + 4 * k) % n_blk, w))

    matrix = lax.all_gather(weight, axes, axis=0, tiled=True)
    leading = features[:BOUND]
    partner = swap_wa(leading)
    outer_same = swap_outer(leading)
    inner_same = swap_core(leading)
    inner_other = swap_core(partner)
    outer_other = swap_wa(outer_same)
    blocks = (partner, inner_same, inner_other, outer_same, outer_other)

    offset = bias
    stage, span = [("wa", n_wa)], 1
    for kind in range(1 + (n_blk - 1).bit_length()):
        if kind == 0:
            other, bit = swap_wa(offset), wa % 2
        else:
            step = 1 << (kind - 1)
            other = permute(offset, lambda b, w: (b ^ step, w))
            bit = (blk // step) % 2
        offset = jnp.where(bit == 0, jnp.concatenate([offset, other]), jnp.concatenate([other, offset]))
    offset = offset.astype(F32)[None, :]

    live_count = (cluster_sizes[0] - wa + n_wa - 1) // n_wa
    table = neighbours[:, :live]
    beyond = table - nodes
    segment, within = beyond // (n_wa * BOUND), beyond % (n_wa * BOUND)
    same = within // BOUND == wa
    row = within % BOUND
    side = jnp.where(same, 0, BOUND) + row
    inner = (segment == 2) == (core == 0)
    away = jnp.where(inner, live + BOUND, live + BOUND + n_wa * BOUND) + side
    home = jnp.where(same, row, live + row)
    index = jnp.where(table < nodes, table, jnp.where(segment == 0, home, away))
    valid = jnp.arange(FANOUT, dtype=jnp.int32)[:, None] < degrees[None, :live]
    index = jnp.where(valid, index, -1)
    inverse = (1.0 / (degrees[:live].astype(F32) + 1.0))[:, None]

    adjacency = counts(index, (live + (1 + 2 * n_wa) * BOUND) // TILE)
    part = gather_own(adjacency, features, live)
    mixed = gather_bound(adjacency, part, inverse, blocks)
    output, grad_low, bias_part = layer(live_count[None], mixed, matrix, offset, cotangent)

    mine = core[None].astype(jnp.int32)
    sent = swap_core(grad_weight_half(1 - mine, mixed, grad_low, BF16))
    kept = grad_weight_half(mine, mixed, grad_low, F32)
    grads = grad_mixed(grad_low, matrix, inverse)
    own_bound, inner_same_g, inner_other_g, outer_same_g, outer_other_g = scatter_bound(adjacency, grads)
    grad_features = scatter_own(adjacency, grads, nodes)

    def pick(value, axis, at):
        return lax.dynamic_index_in_dim(value, at, axis, keepdims=False)

    hi, lo = blk // 4, (blk // 2) % 2
    total = (kept + sent.astype(F32)).reshape(n_hi, 2, 2, n_wa, h // devices, h // 2)
    first, second = total[..., : h // 4], total[..., h // 4 :]
    first = pick(first, 3, wa) + swap_wa(pick(first, 3, 1 - wa).astype(BF16)).astype(F32)
    second = pick(second, 1, lo) + swap_lo(pick(second, 1, 1 - lo).astype(BF16)).astype(F32)
    first = pick(first, 1, lo) + swap_lo(pick(first, 1, 1 - lo).astype(BF16)).astype(F32)
    second = pick(second, 2, wa) + swap_wa(pick(second, 2, 1 - wa).astype(BF16)).astype(F32)
    rows = jnp.concatenate([first, second], axis=-1)
    summed = pick(rows, 0, hi)
    for k in range(1, n_hi):
        away = pick(rows, 0, (hi + k) % n_hi).astype(BF16)
        summed = summed + rotate_hi(away, k).astype(F32)
    mine_rows = pick(summed, 0, core)
    other_rows = swap_core(pick(summed, 0, 1 - core))
    grad_weight = jnp.where(
        core == 0,
        jnp.concatenate([mine_rows, other_rows], axis=1),
        jnp.concatenate([other_rows, mine_rows], axis=1),
    )

    bias_sum = jnp.sum(bias_part, axis=0)
    bias_sum = bias_sum + swap_wa(bias_sum)
    step = 1
    while step < n_blk:
        bias_sum = bias_sum + permute(bias_sum, lambda b, w: (b ^ step, w))
        step *= 2
    grad_bias = lax.dynamic_slice_in_dim(bias_sum, (blk * n_wa + wa) * (h // devices), h // devices)

    outer_back = (outer_same_g.astype(F32) + swap_wa(outer_other_g).astype(F32)).astype(BF16)
    own_back = (own_bound.astype(F32) + swap_core(inner_other_g).astype(F32)).astype(BF16)
    returned = (swap_core(inner_same_g), swap_wa(own_back), swap_outer(outer_back))
    grad_features = add_returned(grad_features, returned)
    return (output, grad_features, grad_weight, grad_bias)


def solution(mesh):
    return jax.shard_map(
        body,
        mesh=mesh,
        in_specs=(
            P(("blk", "wa"), None),
            P(("blk", "wa"), None),
            P(("blk", "wa")),
            P(None, ("blk", "wa")),
            P(("blk", "wa")),
            P("blk"),
            P(("blk", "wa"), None),
        ),
        out_specs=(
            P(("blk", "wa"), None),
            P(("blk", "wa"), None),
            P(("blk", "wa"), None),
            P(("blk", "wa")),
        ),
        check_vma=False,
    )
```

```python
import functools
import math

import jax
import jax.numpy as jnp
from jax import lax
from jax.experimental import pallas as pl
from jax.experimental.pallas import tpu as pltpu
from jax.sharding import PartitionSpec as P

FANOUT = 16
BOUND = 256
CMAX = 3016
TILE = 256
F32 = jnp.float32
BF16 = jnp.bfloat16
VMEM = 60 * 1024 * 1024
GELU_A = math.sqrt(2 / math.pi)
GELU_B = 0.044715


ANY = pl.BlockSpec(memory_space=pl.ANY)
SMEM = pl.BlockSpec(memory_space=pltpu.SMEM)
WHOLE = pl.BlockSpec(memory_space=pltpu.VMEM)
SPARE = 16
TOKEN = jax.ShapeDtypeStruct((8, 128), F32)


def params():
    return pltpu.CompilerParams(vmem_limit_bytes=VMEM)


def tie_kernel(*refs):
    pass


def tie(values, after):
    n = len(values)
    return pl.pallas_call(
        tie_kernel,
        in_specs=[ANY] * (n + len(after)),
        out_specs=[ANY] * n,
        out_shape=[jax.ShapeDtypeStruct(v.shape, v.dtype) for v in values],
        input_output_aliases={k: k for k in range(n)},
        name="tie",
    )(*values, *after)


def resident(shape):
    return pl.BlockSpec(shape, lambda *_: (0,) * len(shape), pipeline_mode=pl.Buffered(1))


def cost(flops, nbytes):
    return pl.CostEstimate(flops=int(flops) // 16, bytes_accessed=int(nbytes) // 16, transcendentals=0)


def dot(a, b, ca, cb):
    return lax.dot_general(a, b, (((ca,), (cb,)), ((), ())), preferred_element_type=F32)


def small(value):
    return value.astype(F32).astype(BF16)


def counts_kernel(index_ref, out_ref):
    base = pl.program_id(0) * TILE
    rows = small(lax.broadcasted_iota(jnp.int32, (TILE, 128), 0))
    lanes = lax.broadcasted_iota(jnp.int32, (FANOUT, 128), 1)
    zero, one, two = (jnp.array(v, BF16) for v in (0, 1, 2))
    for c in range(0, out_ref.shape[1], 128):
        entry = small(jnp.clip(index_ref[:, c : c + 128] - base, -1, TILE))
        own = small(jnp.clip(lanes + (c - base), -1, TILE))
        total = jnp.where(own[0:1, :] == rows, two, zero)
        for s in range(FANOUT):
            total = total + jnp.where(entry[s : s + 1, :] == rows, one, zero)
        out_ref[:, c : c + 128] = total


def counts(index, tiles):
    n = index.shape[1]
    return pl.pallas_call(
        counts_kernel,
        grid=(tiles,),
        in_specs=[pl.BlockSpec((FANOUT, n), lambda i: (0, 0))],
        out_specs=pl.BlockSpec((TILE, n), lambda i: (i, 0)),
        out_shape=jax.ShapeDtypeStruct((tiles * TILE, n), BF16),
        compiler_params=params(),
        cost_estimate=cost(0, tiles * TILE * n * 16),
        name="counts",
    )(index)


def gather_own_kernel(c_ref, t_ref, o_ref):
    o_ref[...] = dot(c_ref[...], t_ref[...], 0, 0)


def gather_own(adjacency, features, live):
    h = features.shape[1]
    return pl.pallas_call(
        gather_own_kernel,
        grid=(live // TILE,),
        in_specs=[pl.BlockSpec((live, TILE), lambda i: (0, i)), resident((live, h))],
        out_specs=pl.BlockSpec((TILE, h), lambda i: (i, 0)),
        out_shape=jax.ShapeDtypeStruct((live, h), F32),
        compiler_params=params(),
        cost_estimate=cost(2 * live * live * h, live * h * 6),
        name="gather_own",
    )(adjacency, features)


def gather_bound_kernel(c_ref, part_ref, inv_ref, *refs):
    o_ref = refs[-1]
    total = part_ref[...]
    for k, ref in enumerate(refs[:-1]):
        total = total + dot(c_ref[k * BOUND : (k + 1) * BOUND, :], ref[...], 0, 0)
    o_ref[...] = (total * inv_ref[...]).astype(BF16)


def gather_bound(adjacency, part, inverse, blocks):
    live, h = part.shape
    rest = adjacency.shape[0] - live
    return pl.pallas_call(
        gather_bound_kernel,
        grid=(live // TILE,),
        in_specs=[
            pl.BlockSpec((pl.Element(rest), pl.Element(TILE)), lambda i: (live, i * TILE)),
            pl.BlockSpec((TILE, h), lambda i: (i, 0)),
            pl.BlockSpec((TILE, 1), lambda i: (i, 0)),
        ]
        + [resident((BOUND, h))] * len(blocks),
        out_specs=pl.BlockSpec((TILE, h), lambda i: (i, 0)),
        out_shape=jax.ShapeDtypeStruct((live, h), BF16),
        compiler_params=params(),
        cost_estimate=cost(2 * live * rest * h, live * h * 6),
        name="gather_bound",
    )(adjacency, part, inverse, *blocks)


def layer_kernel(at_ref, m_ref, w, ct_ref, inv_ref, o_ref, agl_ref, own_ref, gb_ref, sent_ref, b, m_all, gl_all, gb, *, tiles):
    i = pl.program_id(0)
    h = m_ref.shape[1]
    n = h // 2
    mine = pl.ds(pl.multiple_of(at_ref[1] * n, n), n)
    other = pl.ds(pl.multiple_of((1 - at_ref[1]) * n, n), n)

    @pl.when(i == 0)
    def _():
        b[...] = w[:, h:].astype(F32).T[:8, :]
        gb[...] = jnp.zeros_like(gb)

    @pl.when(i < tiles)
    def _():
        base = pl.multiple_of(i * TILE, TILE)
        rows = pl.ds(base, TILE)
        mixed = m_ref[...]
        m_all[rows, :] = mixed
        live = base + lax.broadcasted_iota(jnp.int32, (TILE, 256), 0) < at_ref[0]
        inverse = inv_ref[...]
        for j in range(0, h, 256):
            at = slice(j, j + 256)
            v = dot(mixed, w[:, at], 1, 0) + b[0:1, at]
            square = v * v
            t = jnp.tanh(v * (GELU_A + (GELU_A * GELU_B) * square))
            half = 0.5 + 0.5 * t
            active = v * half
            o_ref[:, at] = jnp.where(live, active, 0.0)
            slope = half + (active - active * half) * (2 * GELU_A + (6 * GELU_A * GELU_B) * square)
            grad = jnp.where(live, ct_ref[:, at].astype(F32) * slope, 0.0)
            gl_all[rows, at] = grad.astype(BF16)
            agl_ref[:, at] = (grad * inverse).astype(BF16)
            gb[:, at] += jnp.sum(grad.reshape(TILE // 8, 8, 256), axis=0)
        own_ref[...] = gl_all[rows, mine]

    @pl.when(i == tiles)
    def _():
        o_ref[...] = jnp.zeros_like(o_ref)

    @pl.when((i > tiles) & (i <= tiles + h // TILE))
    def _():
        at = pl.ds(pl.multiple_of((i - tiles - 1) * TILE, TILE), TILE)
        sent_ref[...] = dot(m_all[:, at], gl_all[:, other], 0, 0).astype(BF16)

    @pl.when(i > tiles + h // TILE)
    def _():
        gb_ref[...] = jnp.broadcast_to(jnp.sum(gb[:, mine], axis=0, keepdims=True), gb_ref.shape)
        sent_ref[:SPARE, :] = jnp.broadcast_to(jnp.sum(gb[:, other], axis=0, keepdims=True), (SPARE, n)).astype(BF16)


def layer(at, mixed, weight, cotangent, inverse):
    live, h = mixed.shape
    nodes, n = cotangent.shape[0], h // 2
    tiles, blocks = live // TILE, h // TILE

    def row(i, s):
        return (jnp.minimum(i, tiles - 1), 0)

    return pl.pallas_call(
        functools.partial(layer_kernel, tiles=tiles),
        grid_spec=pltpu.PrefetchScalarGridSpec(
            num_scalar_prefetch=1,
            grid=(tiles + 1 + blocks + 1,),
            in_specs=[
                pl.BlockSpec((TILE, h), row),
                resident(weight.shape),
                pl.BlockSpec((TILE, h), row),
                pl.BlockSpec((TILE, 1), row),
            ],
            out_specs=[
                pl.BlockSpec((TILE, h), lambda i, s: (jnp.minimum(i, tiles), 0)),
                pl.BlockSpec((TILE, h), row),
                pl.BlockSpec((TILE, n), row),
                resident((8, n)),
                pl.BlockSpec((TILE, n), lambda i, s: (jnp.maximum(i - tiles - 1, 0), 0)),
            ],
            scratch_shapes=[
                pltpu.VMEM((8, h), F32),
                pltpu.VMEM((live, h), BF16),
                pltpu.VMEM((live, h), BF16),
                pltpu.VMEM((8, h), F32),
            ],
        ),
        out_shape=[
            jax.ShapeDtypeStruct((nodes, h), F32),
            jax.ShapeDtypeStruct((live, h), BF16),
            jax.ShapeDtypeStruct((live, n), BF16),
            jax.ShapeDtypeStruct((8, n), F32),
            jax.ShapeDtypeStruct((h + SPARE, n), BF16),
        ],
        compiler_params=params(),
        cost_estimate=cost(3 * live * h * h, live * h * 12),
        name="layer",
    )(at, mixed, weight, cotangent, inverse)


def halves(at_ref, value, rows):
    parts = [value[k * rows : (k + 1) * rows] for k in range(4)]
    even, odd = jnp.concatenate([parts[0], parts[2]]), jnp.concatenate([parts[1], parts[3]])
    first = at_ref[4] == 0
    return jnp.where(first, even, odd), jnp.where(first, odd, even)


def spare_rows(row, n):
    rows = lax.broadcasted_iota(jnp.int32, (SPARE, n), 0)
    return jnp.where(rows == 0, row[:, :n], jnp.where(rows == 1, row[:, n:], 0.0)).astype(BF16)


def from_spare(rows):
    return jnp.concatenate([rows[0:1, :], rows[1:2, :]], axis=1).astype(F32)


def grad_weight_kernel(at_ref, m_ref, g_ref, came_ref, cb_ref, gb_ref, _, a_own, a_sent, b_own, b_sent, gb_out, *, rows):
    t = pl.program_id(0)
    last = pl.num_programs(0) - 1
    n = g_ref.shape[1] // 2
    groups = TILE // (4 * rows)

    @pl.when(t < last)
    def _():
        part = dot(m_ref[...], g_ref[...], 0, 0) + came_ref[...].astype(F32)
        for g in range(groups):
            value = part[g * 4 * rows : (g + 1) * 4 * rows]
            mine, other = halves(at_ref, value[:, :n], rows)
            at = slice(g * 2 * rows, (g + 1) * 2 * rows)
            a_own[at, :] = mine
            a_sent[at, :] = other.astype(BF16)
            here = (t * groups + g) % 2 == at_ref[2]
            at = slice(g // 2 * 4 * rows, (g // 2 + 1) * 4 * rows)

            @pl.when(here)
            def _():
                b_own[at, :] = value[:, n:]

            @pl.when(jnp.logical_not(here))
            def _():
                b_sent[at, :] = value[:, n:].astype(BF16)

    @pl.when(t == last)
    def _():
        total = gb_ref[0:1, :] + cb_ref[0:1, :].astype(F32)
        gb_out[...] = jnp.broadcast_to(total, gb_out.shape)
        a_sent[:SPARE, :] = spare_rows(total, n)


def grad_weight_share(at, mixed, low, came, bias, rows, after):
    live, h = mixed.shape
    n = low.shape[1]
    blocks = h // TILE
    single = TILE == 4 * rows
    b_rows = TILE if single else TILE // 2

    def tile(t):
        return jnp.minimum(t, blocks - 1)

    def plane(t, s):
        return (tile(t) // 2 if single else tile(t), 0)

    return pl.pallas_call(
        functools.partial(grad_weight_kernel, rows=rows),
        grid_spec=pltpu.PrefetchScalarGridSpec(
            num_scalar_prefetch=1,
            grid=(blocks + 1,),
            in_specs=[
                pl.BlockSpec((live, TILE), lambda t, s: (0, tile(t))),
                resident((live, n)),
                pl.BlockSpec((TILE, n), lambda t, s: (tile(t), 0)),
                pl.BlockSpec((SPARE, n), lambda t, s: (h // SPARE, 0)),
                resident((8, n)),
                ANY,
            ],
            out_specs=[
                pl.BlockSpec((TILE // 2, n // 2), lambda t, s: (tile(t), 0)),
                pl.BlockSpec((TILE // 2, n // 2), lambda t, s: (t, 0)),
                pl.BlockSpec((b_rows, n // 2), plane),
                pl.BlockSpec((b_rows, n // 2), plane),
                resident((8, n)),
            ],
        ),
        out_shape=[
            jax.ShapeDtypeStruct((h // 2, n // 2), F32),
            jax.ShapeDtypeStruct((h // 2 + SPARE, n // 2), BF16),
            jax.ShapeDtypeStruct((h // 2, n // 2), F32),
            jax.ShapeDtypeStruct((h // 2, n // 2), BF16),
            jax.ShapeDtypeStruct((8, n), F32),
        ],
        compiler_params=params(),
        cost_estimate=cost(2 * live * h * n, live * h * 3),
        name="grad_weight",
    )(at, mixed, low, came, came, bias, after)


def fold_kernel(at_ref, a_ref, a_came, b_ref, b_came, gb_ref, _, a_own, a_sent, b_own, b_sent, gb_out, *, rows):
    lo, two = at_ref[2], 2 * rows
    n = a_ref.shape[1]
    planes = a_ref.shape[0] // (2 * two)
    for z in range(planes):
        out = slice(z * two, (z + 1) * two)
        near = pl.ds(pl.multiple_of((2 * z + lo) * two, two), two)
        far = pl.ds(pl.multiple_of((2 * z + 1 - lo) * two, two), two)
        a_own[out, :] = a_ref[near, :] + a_came[near, :].astype(F32)
        a_sent[out, :] = (a_ref[far, :] + a_came[far, :].astype(F32)).astype(BF16)
        at = slice(z * 2 * two, (z + 1) * 2 * two)
        mine, other = halves(at_ref, b_ref[at, :] + b_came[at, :].astype(F32), rows)
        b_own[out, :] = mine
        b_sent[out, :] = other.astype(BF16)
    total = gb_ref[0:1, :] + from_spare(a_came[a_ref.shape[0] :, :])
    gb_out[...] = jnp.broadcast_to(total, gb_out.shape)
    a_sent[planes * two :, :] = spare_rows(total, n)


def fold(at, a_own, a_came, b_own, b_came, bias, rows, after):
    count, n = b_own.shape[0] // 2, b_own.shape[1]
    return pl.pallas_call(
        functools.partial(fold_kernel, rows=rows),
        in_specs=[SMEM] + [WHOLE] * 5 + [ANY],
        out_specs=[WHOLE] * 5,
        out_shape=[
            jax.ShapeDtypeStruct((count, n), F32),
            jax.ShapeDtypeStruct((count + SPARE, n), BF16),
            jax.ShapeDtypeStruct((count, n), F32),
            jax.ShapeDtypeStruct((count, n), BF16),
            jax.ShapeDtypeStruct(bias.shape, F32),
        ],
        compiler_params=params(),
        cost_estimate=cost(0, b_own.size * 9),
        name="fold",
    )(at, a_own, a_came, b_own, b_came, bias, after)


def part_kernel(at_ref, a_ref, a_came, b_ref, b_came, gb_ref, *refs, rows, planes):
    gb_out, own, *sent = refs[-1 - planes :]
    two = 2 * rows
    n = a_ref.shape[1]
    total = gb_ref[0:1, :] + from_spare(a_came[a_ref.shape[0] :, :])
    gb_out[...] = jnp.broadcast_to(total, gb_out.shape)
    for k in range(planes):
        at = pl.ds(pl.multiple_of(lax.rem(at_ref[3] + k, planes) * two, two), two)
        out = own if k == 0 else sent[k - 1]
        out[:two, :n] = (a_ref[at, :] + a_came[at, :].astype(F32)).astype(out.dtype)
        out[:two, n:] = (b_ref[at, :] + b_came[at, :].astype(F32)).astype(out.dtype)
        if k:
            out[two:, :] = jnp.broadcast_to(total, (SPARE, 2 * n)).astype(BF16)


def part_planes(at, a_own, a_came, b_own, b_came, bias, rows, planes, after):
    n = a_own.shape[1]
    return pl.pallas_call(
        functools.partial(part_kernel, rows=rows, planes=planes),
        in_specs=[SMEM] + [WHOLE] * 5 + [ANY] * len(after),
        out_specs=[WHOLE] * (1 + planes),
        out_shape=[jax.ShapeDtypeStruct(bias.shape, F32), jax.ShapeDtypeStruct((2 * rows, 2 * n), F32)]
        + [jax.ShapeDtypeStruct((2 * rows + SPARE, 2 * n), BF16)] * (planes - 1),
        compiler_params=params(),
        cost_estimate=cost(0, a_own.size * 18),
        name="part_planes",
    )(at, a_own, a_came, b_own, b_came, bias, *after)


def finish_kernel(at_ref, gb_ref, own, *refs, rows):
    came, mine_ref, other_ref = refs[:-2], refs[-2], refs[-1]
    total, bias = own[...], gb_ref[0:1, :]
    for ref in came:
        total = total + ref[: 2 * rows, :].astype(F32)
        bias = bias + ref[2 * rows : 2 * rows + 1, :].astype(F32)
    first = at_ref[1] == 0
    low, high = total[:rows], total[rows:]
    bias = jnp.broadcast_to(bias, (8, bias.shape[1]))
    mine_ref[:rows, :], other_ref[:rows, :] = jnp.where(first, low, high), jnp.where(first, high, low)
    mine_ref[rows:, :], other_ref[rows:, :] = bias, bias


def finish(at, bias, own, came, rows):
    shape = jax.ShapeDtypeStruct((rows + 8, own.shape[1]), F32)
    return pl.pallas_call(
        functools.partial(finish_kernel, rows=rows),
        in_specs=[SMEM] + [WHOLE] * (2 + len(came)),
        out_specs=[WHOLE] * 2,
        out_shape=[shape] * 2,
        compiler_params=params(),
        cost_estimate=cost(0, own.size * 8),
        name="finish",
    )(at, bias, own, *came)


def scatter_bound_kernel(c_ref, g_ref, *refs):
    outs, part, sem = refs[:-2], refs[-2], refs[-1]
    i = pl.program_id(0)
    part[i] = dot(c_ref[...], g_ref[...], 1, 0).astype(BF16)
    copies = [pltpu.make_async_copy(part.at[k], out, sem.at[k]) for k, out in enumerate(outs)]
    for k, copy in enumerate(copies):

        @pl.when(i == k)
        def _():
            copy.start()

    @pl.when(i == len(outs) - 1)
    def _():
        for copy in copies:
            copy.wait()


def scatter_bound(adjacency, grads):
    live, h = grads.shape
    blocks = (adjacency.shape[0] - live) // BOUND
    return pl.pallas_call(
        scatter_bound_kernel,
        grid=(blocks,),
        in_specs=[pl.BlockSpec((BOUND, live), lambda i: (i + live // BOUND, 0)), resident((live, h))],
        out_specs=[ANY] * blocks,
        out_shape=[jax.ShapeDtypeStruct((BOUND, h), BF16)] * blocks,
        scratch_shapes=[pltpu.VMEM((blocks, BOUND, h), BF16), pltpu.SemaphoreType.DMA((blocks,))],
        compiler_params=params(),
        cost_estimate=cost(2 * blocks * BOUND * live * h, live * h * 4),
        name="scatter_bound",
    )(adjacency, grads)


def grad_rows_kernel(c_ref, g_ref, w_hbm, *refs, low, tiles):
    o_ref, lead_ref, w, sem = refs[-4:]
    i = pl.program_id(0)
    copy = pltpu.make_async_copy(w_hbm.at[:, pl.ds(0, w.shape[1])], w, sem)

    @pl.when(i == 0)
    def _():
        copy.start()

    if low:

        @pl.when(i == 0)
        def _():
            copy.wait()

    @pl.when(low + i < tiles)
    def _():
        total = dot(c_ref[...], g_ref[...], 1, 0)
        if low == 0:

            @pl.when(i == 0)
            def _():
                lead_ref[...] = total
                copy.wait()

        @pl.when(low + i > 0)
        def _():
            o_ref[...] = dot(total.astype(BF16), w[...], 1, 1)

    if low:
        lead_ref[...] = jnp.zeros_like(lead_ref)

    @pl.when(low + i == tiles)
    def _():
        o_ref[...] = jnp.zeros_like(o_ref)


def grad_rows(adjacency, grads, weight, nodes, low, high, before, after):
    live, h = grads.shape
    tiles = live // TILE
    extra = [] if before is None else [before]
    return pl.pallas_call(
        functools.partial(grad_rows_kernel, low=low, tiles=tiles),
        grid=(high - low,),
        in_specs=[
            pl.BlockSpec((TILE, live), lambda i: (jnp.minimum(low + i, tiles - 1), 0)),
            resident((live, h)),
            ANY,
        ]
        + [ANY] * (len(extra) + len(after)),
        out_specs=[pl.BlockSpec((TILE, h), lambda i: (low + i, 0)), resident((8, 128) if low else (TILE, h))],
        out_shape=[jax.ShapeDtypeStruct((nodes, h), F32), TOKEN if low else jax.ShapeDtypeStruct((TILE, h), F32)],
        scratch_shapes=[pltpu.VMEM((h, h), BF16), pltpu.SemaphoreType.DMA],
        input_output_aliases={3: 0} if extra else {},
        compiler_params=params(),
        cost_estimate=cost((2 * live + 2 * h) * (high - low) * TILE * h, live * h * 8),
        name="grad_rows",
    )(adjacency, grads, weight, *extra, *after)


def back_kernel(a_ref, b_ref, c_ref, d_ref, _, o_ref, p_ref):
    o_ref[...] = (a_ref[...].astype(F32) + b_ref[...].astype(F32)).astype(BF16)
    p_ref[...] = (c_ref[...].astype(F32) + d_ref[...].astype(F32)).astype(BF16)


def back(a, b, c, d, after):
    block = pl.BlockSpec((64, a.shape[1]), lambda i: (i, 0))
    return pl.pallas_call(
        back_kernel,
        grid=(a.shape[0] // 64,),
        in_specs=[block] * 4 + [ANY],
        out_specs=[block] * 2,
        out_shape=[jax.ShapeDtypeStruct(a.shape, BF16)] * 2,
        compiler_params=params(),
        cost_estimate=cost(0, a.size * 12),
        name="back",
    )(a, b, c, d, after)


def grad_lead_kernel(lead_ref, *refs):
    came, (w_ref, _, o_ref, total) = refs[:3], refs[3:]

    @pl.when(pl.program_id(0) == 0)
    def _():
        value = lead_ref[...]
        for ref in came:
            value = value + ref[...].astype(F32)
        total[...] = value.astype(BF16)

    o_ref[...] = dot(total[...], w_ref[...], 1, 1)


def grad_lead(lead, came, weight, grads):
    rows, h = lead.shape
    return pl.pallas_call(
        grad_lead_kernel,
        grid=(4,),
        in_specs=[resident((rows, h))] * 4 + [pl.BlockSpec((h // 4, h), lambda i: (i, 0)), ANY],
        out_specs=pl.BlockSpec((rows, h // 4), lambda i: (0, i)),
        out_shape=jax.ShapeDtypeStruct(grads.shape, F32),
        scratch_shapes=[pltpu.VMEM((rows, h), BF16)],
        input_output_aliases={5: 0},
        compiler_params=params(),
        cost_estimate=cost(2 * rows * h * h, h * h * 2),
        name="grad_lead",
    )(lead, *came, weight, grads)


def body(features, weight, bias, neighbours, degrees, cluster_sizes, cotangent):
    axes = ("blk", "wa")
    n_blk, n_wa = lax.axis_size("blk"), lax.axis_size("wa")
    devices, n_hi = n_blk * n_wa, n_blk // 4
    blk, wa = lax.axis_index("blk"), lax.axis_index("wa")
    core, lo, hi = blk % 2, (blk // 2) % 2, blk // 4
    nodes, h = features.shape
    share, n = h // devices, h // 2
    live = min(nodes, -(-(-(-CMAX // n_wa)) // TILE) * TILE)

    def permute(value, target):
        pairs = [(b * n_wa + w, target(b, w)) for b in range(n_blk) for w in range(n_wa)]
        return lax.ppermute(value, axes, [(s, b * n_wa + w) for s, (b, w) in pairs])

    def swap_wa(value):
        return permute(value, lambda b, w: (b, 1 - w))

    def swap_core(value):
        return permute(value, lambda b, w: (b ^ 1, w))

    def swap_outer(value):
        return permute(value, lambda b, w: ((b + (1 if b % 2 else -1)) % n_blk, w))

    def swap_lo(value):
        return permute(value, lambda b, w: (b ^ 2, w))

    def rotate_hi(value, k):
        return permute(value, lambda b, w: ((b + 4 * k) % n_blk, w))

    sheet = jnp.concatenate([weight, jnp.broadcast_to(bias[:, None], (share, 128))], axis=1)
    sheet = lax.all_gather(sheet, axes, axis=0, tiled=True)

    leading = features[:BOUND]
    partner = swap_wa(leading)
    outer_same = swap_outer(leading)
    inner_same = swap_core(leading)
    live_count = (cluster_sizes[0] - wa + n_wa - 1) // n_wa
    table = neighbours[:, :live]
    beyond = table - nodes
    segment, within = beyond // (n_wa * BOUND), beyond % (n_wa * BOUND)
    same = within // BOUND == wa
    row = within % BOUND
    side = jnp.where(same, 0, BOUND) + row
    inner = (segment == 2) == (core == 0)
    away = jnp.where(inner, live + BOUND, live + BOUND + n_wa * BOUND) + side
    home = jnp.where(same, row, live + row)
    index = jnp.where(table < nodes, table, jnp.where(segment == 0, home, away))
    valid = jnp.arange(FANOUT, dtype=jnp.int32)[:, None] < degrees[None, :live]
    index = jnp.where(valid, index, -1)
    inverse = (1.0 / (degrees[:live].astype(F32) + 1.0))[:, None]
    at = jnp.stack([live_count, core, lo, hi, wa]).astype(jnp.int32)

    adjacency = counts(index, (live + (1 + 2 * n_wa) * BOUND) // TILE)
    partner, outer_same, inner_same = tie([partner, outer_same, inner_same], [adjacency])
    inner_other = swap_core(partner)
    outer_other = swap_wa(outer_same)
    blocks = (partner, inner_same, inner_other, outer_same, outer_other)
    part = gather_own(adjacency, features, live)
    mixed = gather_bound(adjacency, part, inverse, blocks)
    output, grads, own_low, bias_sum, sent = layer(at, mixed, sheet, cotangent, inverse)
    came = swap_core(sent)

    own_bound, inner_same_g, inner_other_g, outer_same_g, outer_other_g = scatter_bound(adjacency, grads)
    outer_came, own_came, inner_came = swap_wa(outer_other_g), swap_core(inner_other_g), swap_core(inner_same_g)

    a, a_sent, b, b_sent, bias_sum = grad_weight_share(at, mixed, own_low, came, bias_sum, share, own_bound)
    a_came, b_came = swap_wa(a_sent), swap_lo(b_sent)
    split, tiles = live // TILE // 2, -(-nodes // TILE)
    grad_features, lead = grad_rows(adjacency, grads, sheet, nodes, 0, split, None, [bias_sum])
    outer_back, own_back = back(outer_same_g, outer_came, own_bound, own_came, lead)
    returned = (inner_came, swap_wa(own_back), swap_outer(outer_back))
    a, a_sent, b, b_sent, bias_sum = fold(at, a, a_came, b, b_came, bias_sum, share, own_back)
    a_came, b_came = swap_lo(a_sent), swap_wa(b_sent)
    grad_features, token = grad_rows(adjacency, grads, sheet, nodes, split, tiles, grad_features, [bias_sum])
    bias_sum, own, *rest = part_planes(
        at, a, a_came, b, b_came, bias_sum, share, n_hi, [token, returned[1]]
    )
    rest = [rotate_hi(value, k + 1) for k, value in enumerate(rest)]
    grad_features = grad_lead(lead, returned, sheet, grad_features)
    mine, other = finish(at, bias_sum, own, rest, share)
    other = swap_core(other)
    pair = jnp.where(core == 0, jnp.concatenate([mine, other], axis=1), jnp.concatenate([other, mine], axis=1))
    grad_weight = pair[:share]
    grad_bias = lax.dynamic_slice_in_dim(pair[share], (blk * n_wa + wa) * share, share)
    return (output, grad_features, grad_weight, grad_bias)


def solution(mesh):
    return jax.shard_map(
        body,
        mesh=mesh,
        in_specs=(
            P(("blk", "wa"), None),
            P(("blk", "wa"), None),
            P(("blk", "wa")),
            P(None, ("blk", "wa")),
            P(("blk", "wa")),
            P("blk"),
            P(("blk", "wa"), None),
        ),
        out_specs=(
            P(("blk", "wa"), None),
            P(("blk", "wa"), None),
            P(("blk", "wa"), None),
            P(("blk", "wa")),
        ),
        check_vma=False,
    )
```

```python
import functools
import math

import jax
import jax.numpy as jnp
from jax import lax
from jax.experimental import pallas as pl
from jax.experimental.pallas import tpu as pltpu
from jax.sharding import PartitionSpec as P

FANOUT = 16
BOUND = 256
CMAX = 3016
TILE = 256
F32 = jnp.float32
BF16 = jnp.bfloat16
MIB = 1024 * 1024
GELU_A = math.sqrt(2 / math.pi)
GELU_B = 0.044715


ANY = pl.BlockSpec(memory_space=pl.ANY)
SMEM = pl.BlockSpec(memory_space=pltpu.SMEM)
WHOLE = pl.BlockSpec(memory_space=pltpu.VMEM)
SPARE = 16
TOKEN = jax.ShapeDtypeStruct((8, 128), F32)


def params(mib):
    return pltpu.CompilerParams(vmem_limit_bytes=mib * MIB)


def tie_kernel(*refs):
    pass


def tie(values, after):
    n = len(values)
    return pl.pallas_call(
        tie_kernel,
        in_specs=[ANY] * (n + len(after)),
        out_specs=[ANY] * n,
        out_shape=[jax.ShapeDtypeStruct(v.shape, v.dtype) for v in values],
        input_output_aliases={k: k for k in range(n)},
        compiler_params=params(4),
        name="tie",
    )(*values, *after)


def resident(shape):
    return pl.BlockSpec(shape, lambda *_: (0,) * len(shape), pipeline_mode=pl.Buffered(1))


def cost(flops, nbytes):
    return pl.CostEstimate(flops=int(flops) // 16, bytes_accessed=int(nbytes) // 16, transcendentals=0)


def dot(a, b, ca, cb):
    return lax.dot_general(a, b, (((ca,), (cb,)), ((), ())), preferred_element_type=F32)


def small(value):
    return value.astype(F32).astype(BF16)


def counts_kernel(index_ref, out_ref):
    base = pl.program_id(0) * TILE
    rows = small(lax.broadcasted_iota(jnp.int32, (TILE, 128), 0))
    lanes = lax.broadcasted_iota(jnp.int32, (FANOUT, 128), 1)
    zero, one, two = (jnp.array(v, BF16) for v in (0, 1, 2))
    for c in range(0, out_ref.shape[1], 128):
        entry = small(jnp.clip(index_ref[:, c : c + 128] - base, -1, TILE))
        own = small(jnp.clip(lanes + (c - base), -1, TILE))
        total = jnp.where(own[0:1, :] == rows, two, zero)
        for s in range(FANOUT):
            total = total + jnp.where(entry[s : s + 1, :] == rows, one, zero)
        out_ref[:, c : c + 128] = total


def counts(index, tiles):
    n = index.shape[1]
    return pl.pallas_call(
        counts_kernel,
        grid=(tiles,),
        in_specs=[pl.BlockSpec((FANOUT, n), lambda i: (0, 0))],
        out_specs=pl.BlockSpec((TILE, n), lambda i: (i, 0)),
        out_shape=jax.ShapeDtypeStruct((tiles * TILE, n), BF16),
        compiler_params=params(12),
        cost_estimate=cost(0, tiles * TILE * n * 16),
        name="counts",
    )(index)


def gather_kernel(c_ref, t_ref, *refs):
    o_ref = refs[-1]
    live = t_ref.shape[0]
    total = dot(c_ref[:live, :], t_ref[...], 0, 0)
    for k, ref in enumerate(refs[:-1]):
        at = live + k * BOUND
        total = total + dot(c_ref[at : at + BOUND, :], ref[...], 0, 0)
    o_ref[...] = total


def gather(adjacency, features, blocks, live):
    h = features.shape[1]
    rows = live + len(blocks) * BOUND
    return pl.pallas_call(
        gather_kernel,
        grid=(live // TILE,),
        in_specs=[pl.BlockSpec((rows, TILE), lambda i: (0, i)), resident((live, h))] + [resident((BOUND, h))] * len(blocks),
        out_specs=pl.BlockSpec((TILE, h), lambda i: (i, 0)),
        out_shape=jax.ShapeDtypeStruct((live, h), F32),
        compiler_params=params(26),
        cost_estimate=cost(2 * live * rows * h, live * h * 6),
        name="gather",
    )(adjacency, features, *blocks)


def fetch(pieces, planes, target, sem, at_ref):
    core, lo, hi, wa = (at_ref[j] for j in range(1, 5))
    rows = pieces[0].shape[0] // planes
    copies = []
    for n, piece in enumerate(pieces):
        for k in range(planes):
            chip = lax.rem(hi - k + planes, planes) * 2 + (1 - lo if n // 2 % 2 else lo)
            owner = (chip * 2 + (1 - core if n // 4 else core)) * 2 + (1 - wa if n % 2 else wa)
            copies.append(
                pltpu.make_async_copy(
                    piece.at[pl.ds(k * rows, rows), :],
                    target.at[pl.ds(pl.multiple_of(owner * rows, rows), rows), :],
                    sem.at[n, k],
                )
            )
    return copies


def layer_kernel(at_ref, part_ref, c_ref, last_ref, inv_ref, ct_ref, *refs, tiles, planes):
    pieces, refs = refs[:8], refs[8:]
    o_ref, agl_ref, own_ref, m_ref, w_ref, gb_ref, sent_ref, w, b, m_all, gl_all, gb, sem, sem_out = refs
    i = pl.program_id(0)
    h = m_ref.shape[1]
    n = h // 2
    copies = fetch(pieces, planes, w, sem, at_ref)
    copy_out = pltpu.make_async_copy(w.at[:, pl.ds(0, h)], w_ref, sem_out)
    mine = pl.ds(pl.multiple_of(at_ref[1] * n, n), n)
    other = pl.ds(pl.multiple_of((1 - at_ref[1]) * n, n), n)

    @pl.when(i == 0)
    def _():
        for copy in copies:
            copy.start()
        gb[...] = jnp.zeros_like(gb)

    @pl.when(i < tiles)
    def _():
        total = part_ref[...] + dot(c_ref[...], last_ref[...], 0, 0)
        mixed = (total * inv_ref[...]).astype(BF16)
        m_ref[...] = mixed
        m_all[pl.ds(pl.multiple_of(i * TILE, TILE), TILE), :] = mixed

    @pl.when(i == 0)
    def _():
        for copy in copies:
            copy.wait()
        copy_out.start()
        b[...] = w[:, h:].astype(F32).T[:8, :]

    @pl.when(i < tiles)
    def _():
        base = pl.multiple_of(i * TILE, TILE)
        rows = pl.ds(base, TILE)
        mixed = m_all[rows, :]
        live = base + lax.broadcasted_iota(jnp.int32, (TILE, 256), 0) < at_ref[0]
        inverse = inv_ref[...]
        for j in range(0, h, 256):
            at = slice(j, j + 256)
            v = dot(mixed, w[:, at], 1, 0) + b[0:1, at]
            square = v * v
            t = jnp.tanh(v * (GELU_A + (GELU_A * GELU_B) * square))
            half = 0.5 + 0.5 * t
            active = v * half
            o_ref[:, at] = jnp.where(live, active, 0.0)
            slope = half + (active - active * half) * (2 * GELU_A + (6 * GELU_A * GELU_B) * square)
            grad = jnp.where(live, ct_ref[:, at].astype(F32) * slope, 0.0)
            gl_all[rows, at] = grad.astype(BF16)
            agl_ref[:, at] = (grad * inverse).astype(BF16)
            gb[:, at] += jnp.sum(grad.reshape(TILE // 8, 8, 256), axis=0)
        own_ref[...] = gl_all[rows, mine]

    @pl.when(i == tiles)
    def _():
        o_ref[...] = jnp.zeros_like(o_ref)

    @pl.when((i > tiles) & (i <= tiles + h // TILE))
    def _():
        at = pl.ds(pl.multiple_of((i - tiles - 1) * TILE, TILE), TILE)
        sent_ref[...] = dot(m_all[:, at], gl_all[:, other], 0, 0).astype(BF16)

    @pl.when(i > tiles + h // TILE)
    def _():
        copy_out.wait()
        gb_ref[...] = jnp.broadcast_to(jnp.sum(gb[:, mine], axis=0, keepdims=True), gb_ref.shape)
        sent_ref[:SPARE, :] = jnp.broadcast_to(jnp.sum(gb[:, other], axis=0, keepdims=True), (SPARE, n)).astype(BF16)


def layer(at, part, adjacency, last, inverse, cotangent, pieces, planes):
    live, h = part.shape
    nodes, n = cotangent.shape[0], h // 2
    tiles, blocks = live // TILE, h // TILE
    below = adjacency.shape[0] // BOUND - 1

    def row(i, s):
        return (jnp.minimum(i, tiles - 1), 0)

    return pl.pallas_call(
        functools.partial(layer_kernel, tiles=tiles, planes=planes),
        grid_spec=pltpu.PrefetchScalarGridSpec(
            num_scalar_prefetch=1,
            grid=(tiles + 1 + blocks + 1,),
            in_specs=[
                pl.BlockSpec((TILE, h), row),
                pl.BlockSpec((BOUND, TILE), lambda i, s: (below, jnp.minimum(i, tiles - 1))),
                resident(last.shape),
                pl.BlockSpec((TILE, 1), row),
                pl.BlockSpec((TILE, h), row),
            ]
            + [ANY] * len(pieces),
            out_specs=[
                pl.BlockSpec((TILE, h), lambda i, s: (jnp.minimum(i, tiles), 0)),
                pl.BlockSpec((TILE, h), row),
                pl.BlockSpec((TILE, n), row),
                pl.BlockSpec((TILE, h), row),
                ANY,
                resident((8, n)),
                pl.BlockSpec((TILE, n), lambda i, s: (jnp.maximum(i - tiles - 1, 0), 0)),
            ],
            scratch_shapes=[
                pltpu.VMEM((h, pieces[0].shape[1]), BF16),
                pltpu.VMEM((8, h), F32),
                pltpu.VMEM((live, h), BF16),
                pltpu.VMEM((live, h), BF16),
                pltpu.VMEM((8, h), F32),
                pltpu.SemaphoreType.DMA((len(pieces), planes)),
                pltpu.SemaphoreType.DMA,
            ],
        ),
        out_shape=[
            jax.ShapeDtypeStruct((nodes, h), F32),
            jax.ShapeDtypeStruct((live, h), BF16),
            jax.ShapeDtypeStruct((live, n), BF16),
            jax.ShapeDtypeStruct((live, h), BF16),
            jax.ShapeDtypeStruct((h, h), BF16),
            jax.ShapeDtypeStruct((8, n), F32),
            jax.ShapeDtypeStruct((h + SPARE, n), BF16),
        ],
        compiler_params=params(46),
        cost_estimate=cost(3 * live * h * h, live * h * 12),
        name="layer",
    )(at, part, adjacency, last, inverse, cotangent, *pieces)


def halves(at_ref, value, rows):
    parts = [value[k * rows : (k + 1) * rows] for k in range(4)]
    even, odd = jnp.concatenate([parts[0], parts[2]]), jnp.concatenate([parts[1], parts[3]])
    first = at_ref[4] == 0
    return jnp.where(first, even, odd), jnp.where(first, odd, even)


def spare_rows(row, n):
    rows = lax.broadcasted_iota(jnp.int32, (SPARE, n), 0)
    return jnp.where(rows == 0, row[:, :n], jnp.where(rows == 1, row[:, n:], 0.0)).astype(BF16)


def from_spare(rows):
    return jnp.concatenate([rows[0:1, :], rows[1:2, :]], axis=1).astype(F32)


def grad_weight_kernel(at_ref, m_ref, g_ref, came_ref, cb_ref, gb_ref, _, a_own, a_sent, b_own, b_sent, gb_out, *, rows):
    t = pl.program_id(0)
    last = pl.num_programs(0) - 1
    n = g_ref.shape[1] // 2
    groups = TILE // (4 * rows)

    @pl.when(t < last)
    def _():
        part = dot(m_ref[...], g_ref[...], 0, 0) + came_ref[...].astype(F32)
        for g in range(groups):
            value = part[g * 4 * rows : (g + 1) * 4 * rows]
            mine, other = halves(at_ref, value[:, :n], rows)
            at = slice(g * 2 * rows, (g + 1) * 2 * rows)
            a_own[at, :] = mine
            a_sent[at, :] = other.astype(BF16)
            here = (t * groups + g) % 2 == at_ref[2]
            at = slice(g // 2 * 4 * rows, (g // 2 + 1) * 4 * rows)

            @pl.when(here)
            def _():
                b_own[at, :] = value[:, n:]

            @pl.when(jnp.logical_not(here))
            def _():
                b_sent[at, :] = value[:, n:].astype(BF16)

    @pl.when(t == last)
    def _():
        total = gb_ref[0:1, :] + cb_ref[0:1, :].astype(F32)
        gb_out[...] = jnp.broadcast_to(total, gb_out.shape)
        a_sent[:SPARE, :] = spare_rows(total, n)


def grad_weight_share(at, mixed, low, came, bias, rows, after):
    live, h = mixed.shape
    n = low.shape[1]
    blocks = h // TILE
    single = TILE == 4 * rows
    b_rows = TILE if single else TILE // 2

    def tile(t):
        return jnp.minimum(t, blocks - 1)

    def plane(t, s):
        return (tile(t) // 2 if single else tile(t), 0)

    return pl.pallas_call(
        functools.partial(grad_weight_kernel, rows=rows),
        grid_spec=pltpu.PrefetchScalarGridSpec(
            num_scalar_prefetch=1,
            grid=(blocks + 1,),
            in_specs=[
                pl.BlockSpec((live, TILE), lambda t, s: (0, tile(t))),
                resident((live, n)),
                pl.BlockSpec((TILE, n), lambda t, s: (tile(t), 0)),
                pl.BlockSpec((SPARE, n), lambda t, s: (h // SPARE, 0)),
                resident((8, n)),
                ANY,
            ],
            out_specs=[
                pl.BlockSpec((TILE // 2, n // 2), lambda t, s: (tile(t), 0)),
                pl.BlockSpec((TILE // 2, n // 2), lambda t, s: (t, 0)),
                pl.BlockSpec((b_rows, n // 2), plane),
                pl.BlockSpec((b_rows, n // 2), plane),
                resident((8, n)),
            ],
        ),
        out_shape=[
            jax.ShapeDtypeStruct((h // 2, n // 2), F32),
            jax.ShapeDtypeStruct((h // 2 + SPARE, n // 2), BF16),
            jax.ShapeDtypeStruct((h // 2, n // 2), F32),
            jax.ShapeDtypeStruct((h // 2, n // 2), BF16),
            jax.ShapeDtypeStruct((8, n), F32),
        ],
        compiler_params=params(18),
        cost_estimate=cost(2 * live * h * n, live * h * 3),
        name="grad_weight",
    )(at, mixed, low, came, came, bias, after)


def fold_kernel(at_ref, a_ref, a_came, b_ref, b_came, gb_ref, _, a_own, a_sent, b_own, b_sent, gb_out, *, rows):
    lo, two = at_ref[2], 2 * rows
    n = a_ref.shape[1]
    planes = a_ref.shape[0] // (2 * two)
    for z in range(planes):
        out = slice(z * two, (z + 1) * two)
        near = pl.ds(pl.multiple_of((2 * z + lo) * two, two), two)
        far = pl.ds(pl.multiple_of((2 * z + 1 - lo) * two, two), two)
        a_own[out, :] = a_ref[near, :] + a_came[near, :].astype(F32)
        a_sent[out, :] = (a_ref[far, :] + a_came[far, :].astype(F32)).astype(BF16)
        at = slice(z * 2 * two, (z + 1) * 2 * two)
        mine, other = halves(at_ref, b_ref[at, :] + b_came[at, :].astype(F32), rows)
        b_own[out, :] = mine
        b_sent[out, :] = other.astype(BF16)
    total = gb_ref[0:1, :] + from_spare(a_came[a_ref.shape[0] :, :])
    gb_out[...] = jnp.broadcast_to(total, gb_out.shape)
    a_sent[planes * two :, :] = spare_rows(total, n)


def fold(at, a_own, a_came, b_own, b_came, bias, rows, after):
    count, n = b_own.shape[0] // 2, b_own.shape[1]
    return pl.pallas_call(
        functools.partial(fold_kernel, rows=rows),
        in_specs=[SMEM] + [WHOLE] * 5 + [ANY],
        out_specs=[WHOLE] * 5,
        out_shape=[
            jax.ShapeDtypeStruct((count, n), F32),
            jax.ShapeDtypeStruct((count + SPARE, n), BF16),
            jax.ShapeDtypeStruct((count, n), F32),
            jax.ShapeDtypeStruct((count, n), BF16),
            jax.ShapeDtypeStruct(bias.shape, F32),
        ],
        compiler_params=params(22),
        cost_estimate=cost(0, b_own.size * 9),
        name="fold",
    )(at, a_own, a_came, b_own, b_came, bias, after)


def part_kernel(at_ref, a_ref, a_came, b_ref, b_came, gb_ref, *refs, rows, planes):
    gb_out, own, *sent = refs[-1 - planes :]
    two = 2 * rows
    n = a_ref.shape[1]
    total = gb_ref[0:1, :] + from_spare(a_came[a_ref.shape[0] :, :])
    gb_out[...] = jnp.broadcast_to(total, gb_out.shape)
    for k in range(planes):
        at = pl.ds(pl.multiple_of(lax.rem(at_ref[3] + k, planes) * two, two), two)
        out = own if k == 0 else sent[k - 1]
        out[:two, :n] = (a_ref[at, :] + a_came[at, :].astype(F32)).astype(out.dtype)
        out[:two, n:] = (b_ref[at, :] + b_came[at, :].astype(F32)).astype(out.dtype)
        if k:
            out[two:, :] = jnp.broadcast_to(total, (SPARE, 2 * n)).astype(BF16)


def part_planes(at, a_own, a_came, b_own, b_came, bias, rows, planes, after):
    n = a_own.shape[1]
    return pl.pallas_call(
        functools.partial(part_kernel, rows=rows, planes=planes),
        in_specs=[SMEM] + [WHOLE] * 5 + [ANY] * len(after),
        out_specs=[WHOLE] * (1 + planes),
        out_shape=[jax.ShapeDtypeStruct(bias.shape, F32), jax.ShapeDtypeStruct((2 * rows, 2 * n), F32)]
        + [jax.ShapeDtypeStruct((2 * rows + SPARE, 2 * n), BF16)] * (planes - 1),
        compiler_params=params(14),
        cost_estimate=cost(0, a_own.size * 18),
        name="part_planes",
    )(at, a_own, a_came, b_own, b_came, bias, *after)


def finish_kernel(at_ref, gb_ref, own, *refs, rows):
    came, mine_ref, other_ref = refs[:-3], refs[-2], refs[-1]
    total, bias = own[...], gb_ref[0:1, :]
    for ref in came:
        total = total + ref[: 2 * rows, :].astype(F32)
        bias = bias + ref[2 * rows : 2 * rows + 1, :].astype(F32)
    first = at_ref[1] == 0
    low, high = total[:rows], total[rows:]
    bias = jnp.broadcast_to(bias, (8, bias.shape[1]))
    mine_ref[:rows, :], other_ref[:rows, :] = jnp.where(first, low, high), jnp.where(first, high, low)
    mine_ref[rows:, :], other_ref[rows:, :] = bias, bias


def finish(at, bias, own, came, rows, after):
    shape = jax.ShapeDtypeStruct((rows + 8, own.shape[1]), F32)
    return pl.pallas_call(
        functools.partial(finish_kernel, rows=rows),
        in_specs=[SMEM] + [WHOLE] * (2 + len(came)) + [ANY],
        out_specs=[WHOLE] * 2,
        out_shape=[shape] * 2,
        compiler_params=params(10),
        cost_estimate=cost(0, own.size * 8),
        name="finish",
    )(at, bias, own, *came, after)


def scatter_bound_kernel(c_ref, g_ref, *refs, count):
    *outs, part, sem = refs[len(refs) - 2 - count :]
    i = pl.program_id(0)
    part[i] = dot(c_ref[...], g_ref[...], 1, 0).astype(BF16)
    copies = [pltpu.make_async_copy(part.at[k], out, sem.at[k]) for k, out in enumerate(outs)]
    for k, copy in enumerate(copies):

        @pl.when(i == k)
        def _():
            copy.start()

    @pl.when(i == len(outs) - 1)
    def _():
        for copy in copies:
            copy.wait()


def scatter_bound(adjacency, grads, low, high, after):
    live, h = grads.shape
    blocks = high - low
    return pl.pallas_call(
        functools.partial(scatter_bound_kernel, count=blocks),
        grid=(blocks,),
        in_specs=[pl.BlockSpec((BOUND, live), lambda i: (i + low + live // BOUND, 0)), resident((live, h))]
        + [ANY] * len(after),
        out_specs=[ANY] * blocks,
        out_shape=[jax.ShapeDtypeStruct((BOUND, h), BF16)] * blocks,
        scratch_shapes=[pltpu.VMEM((blocks, BOUND, h), BF16), pltpu.SemaphoreType.DMA((blocks,))],
        compiler_params=params(22),
        cost_estimate=cost(2 * blocks * BOUND * live * h, live * h * 4),
        name="scatter_bound",
    )(adjacency, grads, *after)


def grad_rows_kernel(c_ref, g_ref, w_hbm, *refs, low, tiles):
    o_ref, lead_ref, w, sem = refs[-4:]
    i = pl.program_id(0)
    copy = pltpu.make_async_copy(w_hbm.at[:, pl.ds(0, w.shape[1])], w, sem)

    @pl.when(i == 0)
    def _():
        copy.start()

    if low:

        @pl.when(i == 0)
        def _():
            copy.wait()

    @pl.when(low + i < tiles)
    def _():
        total = dot(c_ref[...], g_ref[...], 1, 0)
        if low == 0:

            @pl.when(i == 0)
            def _():
                lead_ref[...] = total
                copy.wait()

        @pl.when(low + i > 0)
        def _():
            o_ref[...] = dot(total.astype(BF16), w[...], 1, 1)

    if low:
        lead_ref[...] = jnp.zeros_like(lead_ref)

    @pl.when(low + i == tiles)
    def _():
        o_ref[...] = jnp.zeros_like(o_ref)


def grad_rows(adjacency, grads, weight, nodes, low, high, before, after):
    live, h = grads.shape
    tiles = live // TILE
    extra = [] if before is None else [before]
    return pl.pallas_call(
        functools.partial(grad_rows_kernel, low=low, tiles=tiles),
        grid=(high - low,),
        in_specs=[
            pl.BlockSpec((TILE, live), lambda i: (jnp.minimum(low + i, tiles - 1), 0)),
            resident((live, h)),
            ANY,
        ]
        + [ANY] * (len(extra) + len(after)),
        out_specs=[pl.BlockSpec((TILE, h), lambda i: (low + i, 0)), resident((8, 128) if low else (TILE, h))],
        out_shape=[jax.ShapeDtypeStruct((nodes, h), F32), TOKEN if low else jax.ShapeDtypeStruct((TILE, h), F32)],
        scratch_shapes=[pltpu.VMEM((h, h), BF16), pltpu.SemaphoreType.DMA],
        input_output_aliases={3: 0} if extra else {},
        compiler_params=params(30),
        cost_estimate=cost((2 * live + 2 * h) * (high - low) * TILE * h, live * h * 8),
        name="grad_rows",
    )(adjacency, grads, weight, *extra, *after)


def back_kernel(a_ref, b_ref, c_ref, d_ref, _, o_ref, p_ref):
    o_ref[...] = (a_ref[...].astype(F32) + b_ref[...].astype(F32)).astype(BF16)
    p_ref[...] = (c_ref[...].astype(F32) + d_ref[...].astype(F32)).astype(BF16)


def back(a, b, c, d, after):
    block = pl.BlockSpec((64, a.shape[1]), lambda i: (i, 0))
    return pl.pallas_call(
        back_kernel,
        grid=(a.shape[0] // 64,),
        in_specs=[block] * 4 + [ANY],
        out_specs=[block] * 2,
        out_shape=[jax.ShapeDtypeStruct(a.shape, BF16)] * 2,
        compiler_params=params(10),
        cost_estimate=cost(0, a.size * 12),
        name="back",
    )(a, b, c, d, after)


def grad_lead_kernel(lead_ref, *refs):
    came, (w_ref, _, o_ref, token_ref, total) = refs[:3], refs[3:]

    @pl.when(pl.program_id(0) == 0)
    def _():
        value = lead_ref[...]
        for ref in came:
            value = value + ref[...].astype(F32)
        total[...] = value.astype(BF16)
        token_ref[...] = jnp.zeros_like(token_ref)

    o_ref[...] = dot(total[...], w_ref[...], 1, 1)


def grad_lead(lead, came, weight, grads):
    rows, h = lead.shape
    return pl.pallas_call(
        grad_lead_kernel,
        grid=(4,),
        in_specs=[resident((rows, h))] * 4 + [pl.BlockSpec((h // 4, h), lambda i: (i, 0)), ANY],
        out_specs=[pl.BlockSpec((rows, h // 4), lambda i: (0, i)), resident((8, 128))],
        out_shape=[jax.ShapeDtypeStruct(grads.shape, F32), TOKEN],
        scratch_shapes=[pltpu.VMEM((rows, h), BF16)],
        input_output_aliases={5: 0},
        compiler_params=params(20),
        cost_estimate=cost(2 * rows * h * h, h * h * 2),
        name="grad_lead",
    )(lead, *came, weight, grads)


def body(features, weight, bias, neighbours, degrees, cluster_sizes, cotangent):
    axes = ("blk", "wa")
    n_blk, n_wa = lax.axis_size("blk"), lax.axis_size("wa")
    devices, n_hi = n_blk * n_wa, n_blk // 4
    blk, wa = lax.axis_index("blk"), lax.axis_index("wa")
    core, lo, hi = blk % 2, (blk // 2) % 2, blk // 4
    nodes, h = features.shape
    share, n = h // devices, h // 2
    live = min(nodes, -(-(-(-CMAX // n_wa)) // TILE) * TILE)

    def permute(value, target):
        pairs = [(b * n_wa + w, target(b, w)) for b in range(n_blk) for w in range(n_wa)]
        return lax.ppermute(value, axes, [(s, b * n_wa + w) for s, (b, w) in pairs])

    def swap_wa(value):
        return permute(value, lambda b, w: (b, 1 - w))

    def swap_core(value):
        return permute(value, lambda b, w: (b ^ 1, w))

    def swap_outer(value):
        return permute(value, lambda b, w: ((b + (1 if b % 2 else -1)) % n_blk, w))

    def swap_lo(value):
        return permute(value, lambda b, w: (b ^ 2, w))

    def rotate_hi(value, k):
        return permute(value, lambda b, w: ((b + 4 * k) % n_blk, w))

    leading = features[:BOUND]
    partner = swap_wa(leading)
    outer_same = swap_outer(leading)

    sheet = jnp.concatenate([weight, jnp.broadcast_to(bias[:, None], (share, 128))], axis=1)
    planes = [rotate_hi(sheet, k) for k in range(1, n_hi)]

    live_count = (cluster_sizes[0] - wa + n_wa - 1) // n_wa
    table = neighbours[:, :live]
    beyond = table - nodes
    segment, within = beyond // (n_wa * BOUND), beyond % (n_wa * BOUND)
    same = within // BOUND == wa
    row = within % BOUND
    side = jnp.where(same, 0, BOUND) + row
    inner = (segment == 2) == (core == 0)
    away = jnp.where(inner, live + BOUND, live + BOUND + n_wa * BOUND) + side
    home = jnp.where(same, row, live + row)
    index = jnp.where(table < nodes, table, jnp.where(segment == 0, home, away))
    valid = jnp.arange(FANOUT, dtype=jnp.int32)[:, None] < degrees[None, :live]
    index = jnp.where(valid, index, -1)
    inverse = (1.0 / (degrees[:live].astype(F32) + 1.0))[:, None]
    at = jnp.stack([live_count, core, lo, hi, wa]).astype(jnp.int32)

    adjacency = counts(index, (live + (1 + 2 * n_wa) * BOUND) // TILE)
    partner, *planes = tie([partner, *planes], [adjacency])
    sheet = jnp.concatenate([sheet, *planes])
    half_sheet, row_sheet = swap_wa(sheet), swap_lo(sheet)
    inner_same, inner_other = swap_core(leading), swap_core(partner)
    part = gather(adjacency, features, (partner, inner_same, inner_other, outer_same), live)
    half_sheet, row_sheet, outer_same = tie([half_sheet, row_sheet, outer_same], [part])
    outer_other = swap_wa(outer_same)
    both_sheet, outer_other = tie([swap_lo(half_sheet), outer_other], [])
    pieces = [sheet, half_sheet, row_sheet, both_sheet]
    pieces = pieces + [swap_core(value) for value in pieces]
    output, grads, own_low, mixed, matrix, bias_sum, sent = layer(
        at, part, adjacency, outer_other, inverse, cotangent, pieces, n_hi
    )
    came = swap_core(sent)

    (outer_other_g,) = scatter_bound(adjacency, grads, 4, 5, [])
    outer_came = swap_wa(outer_other_g)

    a, a_sent, b, b_sent, bias_sum = grad_weight_share(at, mixed, own_low, came, bias_sum, share, outer_other_g)
    a_came, b_came = swap_wa(a_sent), swap_lo(b_sent)
    own_bound, inner_same_g, inner_other_g, outer_same_g = scatter_bound(adjacency, grads, 0, 4, [bias_sum])
    own_came, inner_came = swap_core(inner_other_g), swap_core(inner_same_g)
    split, tiles = live // TILE // 2, -(-nodes // TILE)
    grad_features, lead = grad_rows(adjacency, grads, matrix, nodes, 0, split, None, [own_bound])
    outer_back, own_back = back(outer_same_g, outer_came, own_bound, own_came, lead)
    returned = (inner_came, swap_wa(own_back), swap_outer(outer_back))
    a, a_sent, b, b_sent, bias_sum = fold(at, a, a_came, b, b_came, bias_sum, share, own_back)
    a_came, b_came = swap_lo(a_sent), swap_wa(b_sent)
    grad_features, token = grad_rows(adjacency, grads, matrix, nodes, split, tiles, grad_features, [bias_sum])
    bias_sum, own, *rest = part_planes(
        at, a, a_came, b, b_came, bias_sum, share, n_hi, [token, returned[1]]
    )
    rest = [rotate_hi(value, k + 1) for k, value in enumerate(rest)]
    grad_features, token = grad_lead(lead, returned, matrix, grad_features)
    mine, other = finish(at, bias_sum, own, rest, share, token)
    other = swap_core(other)
    pair = jnp.where(core == 0, jnp.concatenate([mine, other], axis=1), jnp.concatenate([other, mine], axis=1))
    grad_weight = pair[:share]
    grad_bias = lax.dynamic_slice_in_dim(pair[share], (blk * n_wa + wa) * share, share)
    return (output, grad_features, grad_weight, grad_bias)


def solution(mesh):
    return jax.shard_map(
        body,
        mesh=mesh,
        in_specs=(
            P(("blk", "wa"), None),
            P(("blk", "wa"), None),
            P(("blk", "wa")),
            P(None, ("blk", "wa")),
            P(("blk", "wa")),
            P("blk"),
            P(("blk", "wa"), None),
        ),
        out_specs=(
            P(("blk", "wa"), None),
            P(("blk", "wa"), None),
            P(("blk", "wa"), None),
            P(("blk", "wa")),
        ),
        check_vma=False,
    )
```

```python
import functools
import math

import jax
import jax.numpy as jnp
from jax import lax
from jax.experimental import pallas as pl
from jax.experimental.pallas import tpu as pltpu
from jax.sharding import PartitionSpec as P

FANOUT = 16
BOUND = 256
CMAX = 3016
TILE = 256
F32 = jnp.float32
BF16 = jnp.bfloat16
MIB = 1024 * 1024
GELU_A = math.sqrt(2 / math.pi)
GELU_B = 0.044715


ANY = pl.BlockSpec(memory_space=pl.ANY)
SMEM = pl.BlockSpec(memory_space=pltpu.SMEM)
WHOLE = pl.BlockSpec(memory_space=pltpu.VMEM)
SPARE = 16
TOKEN = jax.ShapeDtypeStruct((8, 128), F32)


def params(mib):
    return pltpu.CompilerParams(vmem_limit_bytes=mib * MIB)


def far(value):
    return pltpu.with_memory_space_constraint(value, pltpu.HBM)


def tie_kernel(*refs):
    pass


def tie(values, after):
    n = len(values)
    return pl.pallas_call(
        tie_kernel,
        in_specs=[ANY] * (n + len(after)),
        out_specs=[ANY] * n,
        out_shape=[jax.ShapeDtypeStruct(v.shape, v.dtype) for v in values],
        input_output_aliases={k: k for k in range(n)},
        compiler_params=params(4),
        name="tie",
    )(*values, *after)


def resident(shape):
    return pl.BlockSpec(shape, lambda *_: (0,) * len(shape), pipeline_mode=pl.Buffered(1))


def cost(flops, nbytes):
    return pl.CostEstimate(flops=int(flops) // 16, bytes_accessed=int(nbytes) // 16, transcendentals=0)


def dot(a, b, ca, cb):
    return lax.dot_general(a, b, (((ca,), (cb,)), ((), ())), preferred_element_type=F32)


def small(value):
    return value.astype(F32).astype(BF16)


def counts_kernel(index_ref, out_ref):
    base = pl.program_id(0) * TILE
    rows = small(lax.broadcasted_iota(jnp.int32, (TILE, 128), 0))
    lanes = lax.broadcasted_iota(jnp.int32, (FANOUT, 128), 1)
    zero, one, two = (jnp.array(v, BF16) for v in (0, 1, 2))
    for c in range(0, out_ref.shape[1], 128):
        entry = small(jnp.clip(index_ref[:, c : c + 128] - base, -1, TILE))
        own = small(jnp.clip(lanes + (c - base), -1, TILE))
        total = jnp.where(own[0:1, :] == rows, two, zero)
        for s in range(FANOUT):
            total = total + jnp.where(entry[s : s + 1, :] == rows, one, zero)
        out_ref[:, c : c + 128] = total


def counts(index, tiles):
    n = index.shape[1]
    return pl.pallas_call(
        counts_kernel,
        grid=(tiles,),
        in_specs=[pl.BlockSpec((FANOUT, n), lambda i: (0, 0))],
        out_specs=pl.BlockSpec((TILE, n), lambda i: (i, 0)),
        out_shape=jax.ShapeDtypeStruct((tiles * TILE, n), BF16),
        compiler_params=params(12),
        cost_estimate=cost(0, tiles * TILE * n * 16),
        name="counts",
    )(index)


def gather_kernel(c_ref, t_ref, *refs, count):
    o_ref = refs[-1]
    live = t_ref.shape[0]
    total = dot(c_ref[:live, :], t_ref[...], 0, 0)
    for k, ref in enumerate(refs[:count]):
        at = live + k * BOUND
        total = total + dot(c_ref[at : at + BOUND, :], ref[...], 0, 0)
    o_ref[...] = total


def gather(adjacency, features, blocks, live, after):
    h = features.shape[1]
    rows = live + len(blocks) * BOUND
    return pl.pallas_call(
        functools.partial(gather_kernel, count=len(blocks)),
        grid=(live // TILE,),
        in_specs=[pl.BlockSpec((rows, TILE), lambda i: (0, i)), resident((live, h))]
        + [resident((BOUND, h))] * len(blocks)
        + [ANY] * len(after),
        out_specs=pl.BlockSpec((TILE, h), lambda i: (i, 0)),
        out_shape=jax.ShapeDtypeStruct((live, h), F32),
        compiler_params=params(26),
        cost_estimate=cost(2 * live * rows * h, live * h * 6),
        name="gather",
    )(far(adjacency), far(features), *blocks, *after)


def fetch(pieces, planes, target, sem, at_ref):
    core, lo, hi, wa = (at_ref[j] for j in range(1, 5))
    rows = pieces[0].shape[0] // planes
    copies = []
    for n, piece in enumerate(pieces):
        for k in range(planes):
            chip = lax.rem(hi - k + planes, planes) * 2 + (1 - lo if n // 2 % 2 else lo)
            owner = (chip * 2 + (1 - core if n // 4 else core)) * 2 + (1 - wa if n % 2 else wa)
            copies.append(
                pltpu.make_async_copy(
                    piece.at[pl.ds(k * rows, rows), pl.ds(0, target.shape[1])],
                    target.at[pl.ds(pl.multiple_of(owner * rows, rows), rows), :],
                    sem.at[n, k],
                )
            )
    return copies


def layer_kernel(at_ref, part_ref, c_ref, cl_ref, last_ref, inv_ref, ct_ref, *refs, tiles, planes):
    pieces, refs = refs[:8], refs[8:]
    o_ref, agl_ref, gb_ref, kept_ref, sent_ref, far_ref, w, b, m_all, gl_all, gb, sem = refs
    i = pl.program_id(0)
    h = part_ref.shape[1]
    n = h // 2
    copies = fetch(pieces, planes, w, sem, at_ref)
    mine = pl.ds(pl.multiple_of(at_ref[1] * n, n), n)
    other = pl.ds(pl.multiple_of((1 - at_ref[1]) * n, n), n)

    @pl.when(i == 0)
    def _():
        for copy in copies:
            copy.start()
        gb[...] = jnp.zeros_like(gb)

    @pl.when(i < tiles)
    def _():
        total = part_ref[...] + dot(c_ref[...], last_ref[...], 0, 0)
        m_all[pl.ds(pl.multiple_of(i * TILE, TILE), TILE), :] = (total * inv_ref[...]).astype(BF16)

    @pl.when(i == 0)
    def _():
        for copy in copies:
            copy.wait()
        b[...] = w[:, h:].astype(F32).T[:8, :]

    @pl.when(i < tiles)
    def _():
        base = pl.multiple_of(i * TILE, TILE)
        rows = pl.ds(base, TILE)
        mixed = m_all[rows, :]
        live = base + lax.broadcasted_iota(jnp.int32, (TILE, 256), 0) < at_ref[0]
        inverse = inv_ref[...]
        for j in range(0, h, 256):
            at = slice(j, j + 256)
            v = dot(mixed, w[:, at], 1, 0) + b[0:1, at]
            square = v * v
            half = jnp.where(live, 0.5 + 0.5 * jnp.tanh(v * (GELU_A + (GELU_A * GELU_B) * square)), 0.0)
            o_ref[:, at] = v * half
            slope = half + (half - half * half) * (v * (2 * GELU_A + (6 * GELU_A * GELU_B) * square))
            grad = ct_ref[:, at].astype(F32) * slope
            gl_all[rows, at] = grad.astype(BF16)
            agl_ref[rows, at] = (grad * inverse).astype(BF16)
            gb[:, at] += jnp.sum(grad.reshape(TILE // 8, 8, 256), axis=0)

    @pl.when(i == tiles)
    def _():
        o_ref[...] = jnp.zeros_like(o_ref)
        far_ref[...] = dot(cl_ref[...], agl_ref[...], 1, 0).astype(BF16)

    @pl.when((i > tiles) & (i <= tiles + h // TILE))
    def _():
        at = pl.ds(pl.multiple_of((i - tiles - 1) * TILE, TILE), TILE)
        kept_ref[...] = dot(m_all[:, at], gl_all[:, mine], 0, 0).astype(BF16)
        sent_ref[...] = dot(m_all[:, at], gl_all[:, other], 0, 0).astype(BF16)

    @pl.when(i > tiles + h // TILE)
    def _():
        gb_ref[...] = jnp.broadcast_to(jnp.sum(gb[:, mine], axis=0, keepdims=True), gb_ref.shape)
        sent_ref[:SPARE, :] = jnp.broadcast_to(jnp.sum(gb[:, other], axis=0, keepdims=True), (SPARE, n)).astype(BF16)


def layer(at, part, adjacency, last, inverse, cotangent, pieces, planes):
    live, h = part.shape
    nodes, n = cotangent.shape[0], h // 2
    tiles, blocks = live // TILE, h // TILE
    below = adjacency.shape[0] // BOUND - 1

    def row(i, s):
        return (jnp.minimum(i, tiles - 1), 0)

    return pl.pallas_call(
        functools.partial(layer_kernel, tiles=tiles, planes=planes),
        grid_spec=pltpu.PrefetchScalarGridSpec(
            num_scalar_prefetch=1,
            grid=(tiles + 1 + blocks + 1,),
            in_specs=[
                pl.BlockSpec((TILE, h), row),
                pl.BlockSpec((BOUND, TILE), lambda i, s: (below, jnp.minimum(i, tiles - 1))),
                pl.BlockSpec((BOUND, live), lambda i, s: (below, 0), pipeline_mode=pl.Buffered(1)),
                resident(last.shape),
                pl.BlockSpec((TILE, 1), row),
                pl.BlockSpec((TILE, h), row),
            ]
            + [ANY] * len(pieces),
            out_specs=[
                pl.BlockSpec((TILE, h), lambda i, s: (jnp.minimum(i, tiles), 0)),
                WHOLE,
                resident((8, n)),
                pl.BlockSpec((TILE, n), lambda i, s: (jnp.clip(i - tiles - 1, 0, blocks - 1), 0)),
                pl.BlockSpec((TILE, n), lambda i, s: (jnp.maximum(i - tiles - 1, 0), 0)),
                resident((BOUND, h)),
            ],
            scratch_shapes=[
                pltpu.VMEM((h, pieces[0].shape[1]), BF16),
                pltpu.VMEM((8, h), F32),
                pltpu.VMEM((live, h), BF16),
                pltpu.VMEM((live, h), BF16),
                pltpu.VMEM((8, h), F32),
                pltpu.SemaphoreType.DMA((len(pieces), planes)),
            ],
        ),
        out_shape=[
            jax.ShapeDtypeStruct((nodes, h), F32),
            pltpu.VMEM((live, h), BF16),
            jax.ShapeDtypeStruct((8, n), F32),
            jax.ShapeDtypeStruct((h, n), BF16),
            pltpu.HBM((h + SPARE, n), BF16),
            pltpu.HBM((BOUND, h), BF16),
        ],
        compiler_params=params(46),
        cost_estimate=cost(3 * live * h * h, live * h * 12),
        name="layer",
    )(at, far(part), far(adjacency), far(adjacency), last, inverse, far(cotangent), *pieces)


def halves(at_ref, value, rows):
    parts = [value[k * rows : (k + 1) * rows] for k in range(4)]
    even, odd = jnp.concatenate([parts[0], parts[2]]), jnp.concatenate([parts[1], parts[3]])
    first = at_ref[4] == 0
    return jnp.where(first, even, odd), jnp.where(first, odd, even)


def spare_rows(row, n):
    rows = lax.broadcasted_iota(jnp.int32, (SPARE, n), 0)
    return jnp.where(rows == 0, row[:, :n], jnp.where(rows == 1, row[:, n:], 0.0)).astype(BF16)


def from_spare(rows):
    return jnp.concatenate([rows[0:1, :], rows[1:2, :]], axis=1).astype(F32)


def share_kernel(at_ref, kept_ref, came_ref, cb_ref, gb_ref, _, a_own, a_sent, b_own, b_sent, gb_out, *, rows):
    t = pl.program_id(0)
    last = pl.num_programs(0) - 1
    n = kept_ref.shape[1] // 2
    groups = TILE // (4 * rows)

    @pl.when(t < last)
    def _():
        part = kept_ref[...].astype(F32) + came_ref[...].astype(F32)
        for g in range(groups):
            value = part[g * 4 * rows : (g + 1) * 4 * rows].astype(BF16)
            mine, other = halves(at_ref, value[:, :n], rows)
            at = slice(g * 2 * rows, (g + 1) * 2 * rows)
            a_own[at, :] = mine
            a_sent[at, :] = other
            here = (t * groups + g) % 2 == at_ref[2]
            at = slice(g // 2 * 4 * rows, (g // 2 + 1) * 4 * rows)

            @pl.when(here)
            def _():
                b_own[at, :] = value[:, n:]

            @pl.when(jnp.logical_not(here))
            def _():
                b_sent[at, :] = value[:, n:]

    @pl.when(t == last)
    def _():
        total = gb_ref[0:1, :] + cb_ref[0:1, :].astype(F32)
        gb_out[...] = jnp.broadcast_to(total, gb_out.shape)
        a_sent[:SPARE, :] = spare_rows(total, n)


def share_rows(at, kept, came, bias, rows, after):
    h, n = kept.shape
    blocks = h // TILE
    single = TILE == 4 * rows
    b_rows = TILE if single else TILE // 2

    def tile(t):
        return jnp.minimum(t, blocks - 1)

    def plane(t, s):
        return (tile(t) // 2 if single else tile(t), 0)

    return pl.pallas_call(
        functools.partial(share_kernel, rows=rows),
        grid_spec=pltpu.PrefetchScalarGridSpec(
            num_scalar_prefetch=1,
            grid=(blocks + 1,),
            in_specs=[
                pl.BlockSpec((TILE, n), lambda t, s: (tile(t), 0)),
                pl.BlockSpec((TILE, n), lambda t, s: (tile(t), 0)),
                pl.BlockSpec((SPARE, n), lambda t, s: (h // SPARE, 0)),
                resident((8, n)),
                ANY,
            ],
            out_specs=[
                pl.BlockSpec((TILE // 2, n // 2), lambda t, s: (tile(t), 0)),
                pl.BlockSpec((TILE // 2, n // 2), lambda t, s: (t, 0)),
                pl.BlockSpec((b_rows, n // 2), plane),
                pl.BlockSpec((b_rows, n // 2), plane),
                resident((8, n)),
            ],
        ),
        out_shape=[
            pltpu.HBM((h // 2, n // 2), BF16),
            pltpu.HBM((h // 2 + SPARE, n // 2), BF16),
            pltpu.HBM((h // 2, n // 2), BF16),
            pltpu.HBM((h // 2, n // 2), BF16),
            jax.ShapeDtypeStruct((8, n), F32),
        ],
        compiler_params=params(10),
        cost_estimate=cost(0, h * n * 8),
        name="share",
    )(at, kept, came, came, bias, after)


def fold_kernel(at_ref, a_ref, a_came, b_ref, b_came, gb_ref, _, a_own, a_sent, b_own, b_sent, gb_out, *, rows):
    lo, two = at_ref[2], 2 * rows
    n = a_ref.shape[1]
    planes = a_ref.shape[0] // (2 * two)
    for z in range(planes):
        out = slice(z * two, (z + 1) * two)
        near = pl.ds(pl.multiple_of((2 * z + lo) * two, two), two)
        far = pl.ds(pl.multiple_of((2 * z + 1 - lo) * two, two), two)
        a_own[out, :] = a_ref[near, :].astype(F32) + a_came[near, :].astype(F32)
        a_sent[out, :] = (a_ref[far, :].astype(F32) + a_came[far, :].astype(F32)).astype(BF16)
        at = slice(z * 2 * two, (z + 1) * 2 * two)
        mine, other = halves(at_ref, b_ref[at, :].astype(F32) + b_came[at, :].astype(F32), rows)
        b_own[out, :] = mine
        b_sent[out, :] = other.astype(BF16)
    total = gb_ref[0:1, :] + from_spare(a_came[a_ref.shape[0] :, :])
    gb_out[...] = jnp.broadcast_to(total, gb_out.shape)
    a_sent[planes * two :, :] = spare_rows(total, n)


def fold(at, a_own, a_came, b_own, b_came, bias, rows, after):
    count, n = b_own.shape[0] // 2, b_own.shape[1]
    return pl.pallas_call(
        functools.partial(fold_kernel, rows=rows),
        in_specs=[SMEM] + [WHOLE] * 5 + [ANY],
        out_specs=[WHOLE] * 5,
        out_shape=[
            jax.ShapeDtypeStruct((count, n), F32),
            jax.ShapeDtypeStruct((count + SPARE, n), BF16),
            jax.ShapeDtypeStruct((count, n), F32),
            jax.ShapeDtypeStruct((count, n), BF16),
            jax.ShapeDtypeStruct(bias.shape, F32),
        ],
        compiler_params=params(22),
        cost_estimate=cost(0, b_own.size * 9),
        name="fold",
    )(at, far(a_own), far(a_came), far(b_own), far(b_came), bias, after)


def part_kernel(at_ref, a_ref, a_came, b_ref, b_came, gb_ref, *refs, rows, planes):
    gb_out, own, *sent = refs[-1 - planes :]
    two = 2 * rows
    n = a_ref.shape[1]
    total = gb_ref[0:1, :] + from_spare(a_came[a_ref.shape[0] :, :])
    gb_out[...] = jnp.broadcast_to(total, gb_out.shape)
    for k in range(planes):
        at = pl.ds(pl.multiple_of(lax.rem(at_ref[3] + k, planes) * two, two), two)
        out = own if k == 0 else sent[k - 1]
        out[:two, :n] = (a_ref[at, :] + a_came[at, :].astype(F32)).astype(out.dtype)
        out[:two, n:] = (b_ref[at, :] + b_came[at, :].astype(F32)).astype(out.dtype)
        if k:
            out[two:, :] = jnp.broadcast_to(total, (SPARE, 2 * n)).astype(BF16)


def part_planes(at, a_own, a_came, b_own, b_came, bias, rows, planes, after):
    n = a_own.shape[1]
    return pl.pallas_call(
        functools.partial(part_kernel, rows=rows, planes=planes),
        in_specs=[SMEM] + [WHOLE] * 5 + [ANY] * len(after),
        out_specs=[WHOLE] * (1 + planes),
        out_shape=[jax.ShapeDtypeStruct(bias.shape, F32), jax.ShapeDtypeStruct((2 * rows, 2 * n), F32)]
        + [jax.ShapeDtypeStruct((2 * rows + SPARE, 2 * n), BF16)] * (planes - 1),
        compiler_params=params(14),
        cost_estimate=cost(0, a_own.size * 18),
        name="part_planes",
    )(at, a_own, a_came, b_own, b_came, bias, *after)


def finish_kernel(at_ref, gb_ref, own, *refs, rows):
    came, mine_ref, other_ref = refs[:-3], refs[-2], refs[-1]
    total, bias = own[...], gb_ref[0:1, :]
    for ref in came:
        total = total + ref[: 2 * rows, :].astype(F32)
        bias = bias + ref[2 * rows : 2 * rows + 1, :].astype(F32)
    first = at_ref[1] == 0
    low, high = total[:rows], total[rows:]
    bias = jnp.broadcast_to(bias, (8, bias.shape[1]))
    mine_ref[:rows, :], other_ref[:rows, :] = jnp.where(first, low, high), jnp.where(first, high, low)
    mine_ref[rows:, :], other_ref[rows:, :] = bias, bias


def finish(at, bias, own, came, rows, after):
    shape = jax.ShapeDtypeStruct((rows + 8, own.shape[1]), F32)
    return pl.pallas_call(
        functools.partial(finish_kernel, rows=rows),
        in_specs=[SMEM] + [WHOLE] * (2 + len(came)) + [ANY],
        out_specs=[WHOLE] * 2,
        out_shape=[shape] * 2,
        compiler_params=params(10),
        cost_estimate=cost(0, own.size * 8),
        name="finish",
    )(at, bias, own, *came, after)


def scatter_bound_kernel(c_ref, g_ref, *refs, count):
    *outs, part, sem = refs[len(refs) - 2 - count :]
    i = pl.program_id(0)
    part[i] = dot(c_ref[...], g_ref[...], 1, 0).astype(BF16)
    copies = [pltpu.make_async_copy(part.at[k], out, sem.at[k]) for k, out in enumerate(outs)]
    for k, copy in enumerate(copies):

        @pl.when(i == k)
        def _():
            copy.start()

    @pl.when(i == len(outs) - 1)
    def _():
        for copy in copies:
            copy.wait()


def scatter_bound(adjacency, grads):
    live, h = grads.shape
    blocks = (adjacency.shape[0] - live) // BOUND - 1
    return pl.pallas_call(
        functools.partial(scatter_bound_kernel, count=blocks),
        grid=(blocks,),
        in_specs=[pl.BlockSpec((BOUND, live), lambda i: (i + live // BOUND, 0)), resident((live, h))],
        out_specs=[ANY] * blocks,
        out_shape=[pltpu.HBM((BOUND, h), BF16)] * blocks,
        scratch_shapes=[pltpu.VMEM((blocks, BOUND, h), BF16), pltpu.SemaphoreType.DMA((blocks,))],
        compiler_params=params(22),
        cost_estimate=cost(2 * blocks * BOUND * live * h, live * h * 4),
        name="scatter_bound",
    )(adjacency, grads)


def grad_rows_kernel(at_ref, c_ref, g_ref, *refs, low, tiles, planes):
    w, sem, sem_out = refs[-3:]
    i = pl.program_id(0)
    if low:
        o_ref, lead_ref = refs[-5:-3]
        copies = [pltpu.make_async_copy(refs[0], w, sem_out)]
    else:
        o_ref, lead_ref, w_ref = refs[-6:-3]
        copies = fetch(refs[:8], planes, w, sem, at_ref)
        copy_out = pltpu.make_async_copy(w, w_ref, sem_out)

    @pl.when(i == 0)
    def _():
        for copy in copies:
            copy.start()

    @pl.when(low + i < tiles)
    def _():
        total = dot(c_ref[...], g_ref[...], 1, 0)

        @pl.when(i == 0)
        def _():
            lead_ref[...] = total if low == 0 else jnp.zeros_like(lead_ref)
            for copy in copies:
                copy.wait()
            if low == 0:
                copy_out.start()

        @pl.when(low + i > 0)
        def _():
            o_ref[...] = dot(total.astype(BF16), w[...], 1, 1)

    @pl.when(low + i == tiles)
    def _():
        o_ref[...] = jnp.zeros_like(o_ref)

    if low == 0:

        @pl.when(i == pl.num_programs(0) - 1)
        def _():
            copy_out.wait()


def grad_rows(at, adjacency, grads, weight, nodes, low, high, planes, before, after):
    live, h = grads.shape
    tiles = live // TILE
    extra = [] if before is None else [before]
    outs = [jax.ShapeDtypeStruct((nodes, h), F32), TOKEN if low else jax.ShapeDtypeStruct((TILE, h), F32)]
    out_specs = [pl.BlockSpec((TILE, h), lambda i, s: (low + i, 0)), resident((8, 128) if low else (TILE, h))]
    if low == 0:
        outs += [jax.ShapeDtypeStruct((h, h), BF16)]
        out_specs += [ANY]
    return pl.pallas_call(
        functools.partial(grad_rows_kernel, low=low, tiles=tiles, planes=planes),
        grid_spec=pltpu.PrefetchScalarGridSpec(
            num_scalar_prefetch=1,
            grid=(high - low,),
            in_specs=[
                pl.BlockSpec((TILE, live), lambda i, s: (jnp.minimum(low + i, tiles - 1), 0)),
                resident((live, h)),
            ]
            + [ANY] * (len(weight) + len(extra) + len(after)),
            out_specs=out_specs,
            scratch_shapes=[
                pltpu.VMEM((h, h), BF16),
                pltpu.SemaphoreType.DMA((len(weight), planes)),
                pltpu.SemaphoreType.DMA,
            ],
        ),
        out_shape=outs,
        input_output_aliases={3 + len(weight): 0} if extra else {},
        compiler_params=params(30),
        cost_estimate=cost((2 * live + 2 * h) * (high - low) * TILE * h, live * h * 8),
        name="grad_rows",
    )(at, adjacency, grads, *weight, *extra, *after)


def back_kernel(a_ref, b_ref, c_ref, d_ref, _, o_ref, p_ref):
    o_ref[...] = (a_ref[...].astype(F32) + b_ref[...].astype(F32)).astype(BF16)
    p_ref[...] = (c_ref[...].astype(F32) + d_ref[...].astype(F32)).astype(BF16)


def back(a, b, c, d, after):
    block = pl.BlockSpec((64, a.shape[1]), lambda i: (i, 0))
    return pl.pallas_call(
        back_kernel,
        grid=(a.shape[0] // 64,),
        in_specs=[block] * 4 + [ANY],
        out_specs=[block] * 2,
        out_shape=[jax.ShapeDtypeStruct(a.shape, BF16)] * 2,
        compiler_params=params(10),
        cost_estimate=cost(0, a.size * 12),
        name="back",
    )(far(a), far(b), far(c), far(d), after)


def grad_lead_kernel(lead_ref, *refs):
    came, (w_ref, _, o_ref, token_ref, total) = refs[:3], refs[3:]

    @pl.when(pl.program_id(0) == 0)
    def _():
        value = lead_ref[...]
        for ref in came:
            value = value + ref[...].astype(F32)
        total[...] = value.astype(BF16)
        token_ref[...] = jnp.zeros_like(token_ref)

    o_ref[...] = dot(total[...], w_ref[...], 1, 1)


def grad_lead(lead, came, weight, grads):
    rows, h = lead.shape
    return pl.pallas_call(
        grad_lead_kernel,
        grid=(4,),
        in_specs=[resident((rows, h))] * 4 + [pl.BlockSpec((h // 4, h), lambda i: (i, 0)), ANY],
        out_specs=[pl.BlockSpec((rows, h // 4), lambda i: (0, i)), resident((8, 128))],
        out_shape=[jax.ShapeDtypeStruct(grads.shape, F32), TOKEN],
        scratch_shapes=[pltpu.VMEM((rows, h), BF16)],
        input_output_aliases={5: 0},
        compiler_params=params(20),
        cost_estimate=cost(2 * rows * h * h, h * h * 2),
        name="grad_lead",
    )(lead, *came, weight, grads)


def body(features, weight, bias, neighbours, degrees, cluster_sizes, cotangent):
    axes = ("blk", "wa")
    n_blk, n_wa = lax.axis_size("blk"), lax.axis_size("wa")
    devices, n_hi = n_blk * n_wa, n_blk // 4
    blk, wa = lax.axis_index("blk"), lax.axis_index("wa")
    core, lo, hi = blk % 2, (blk // 2) % 2, blk // 4
    nodes, h = features.shape
    share, n = h // devices, h // 2
    live = min(nodes, -(-(-(-CMAX // n_wa)) // TILE) * TILE)

    def permute(value, target):
        pairs = [(b * n_wa + w, target(b, w)) for b in range(n_blk) for w in range(n_wa)]
        return lax.ppermute(value, axes, [(s, b * n_wa + w) for s, (b, w) in pairs])

    def swap_wa(value):
        return permute(value, lambda b, w: (b, 1 - w))

    def swap_core(value):
        return permute(value, lambda b, w: (b ^ 1, w))

    def swap_outer(value):
        return permute(value, lambda b, w: ((b + (1 if b % 2 else -1)) % n_blk, w))

    def swap_lo(value):
        return permute(value, lambda b, w: (b ^ 2, w))

    def rotate_hi(value, k):
        return permute(value, lambda b, w: ((b + 4 * k) % n_blk, w))

    leading = features[:BOUND]
    partner = swap_wa(leading)
    outer_same = swap_outer(leading)

    sheet = jnp.concatenate([weight, jnp.broadcast_to(bias[:, None], (share, 128))], axis=1)
    planes = [rotate_hi(sheet, k) for k in range(1, n_hi)]

    live_count = (cluster_sizes[0] - wa + n_wa - 1) // n_wa
    table = neighbours[:, :live]
    beyond = table - nodes
    segment, within = beyond // (n_wa * BOUND), beyond % (n_wa * BOUND)
    same = within // BOUND == wa
    row = within % BOUND
    side = jnp.where(same, 0, BOUND) + row
    inner = (segment == 2) == (core == 0)
    away = jnp.where(inner, live + BOUND, live + BOUND + n_wa * BOUND) + side
    home = jnp.where(same, row, live + row)
    index = jnp.where(table < nodes, table, jnp.where(segment == 0, home, away))
    valid = jnp.arange(FANOUT, dtype=jnp.int32)[:, None] < degrees[None, :live]
    index = jnp.where(valid, index, -1)
    inverse = (1.0 / (degrees[:live].astype(F32) + 1.0))[:, None]
    at = jnp.stack([live_count, core, lo, hi, wa]).astype(jnp.int32)

    adjacency = counts(index, (live + (1 + 2 * n_wa) * BOUND) // TILE)
    partner, *planes = tie([partner, *planes], [adjacency])
    sheet = jnp.concatenate([sheet, *planes])
    half_sheet, row_sheet = swap_wa(sheet), swap_lo(sheet)
    inner_same, inner_other = swap_core(leading), swap_core(partner)
    part = gather(adjacency, features, (partner, inner_same, inner_other, outer_same), live, [inverse, at])
    half_sheet, row_sheet, outer_same = tie([half_sheet, row_sheet, outer_same], [part])
    outer_other = swap_wa(outer_same)
    both_sheet, outer_other = tie([swap_lo(half_sheet), outer_other], [])
    pieces = [sheet, half_sheet, row_sheet, both_sheet]
    pieces = pieces + [swap_core(value) for value in pieces]
    output, grads, bias_sum, kept, sent, outer_other_g = layer(
        at, part, adjacency, outer_other, inverse, cotangent, pieces, n_hi
    )
    came = swap_core(sent)

    outer_came = swap_wa(outer_other_g)
    own_bound, inner_same_g, inner_other_g, outer_same_g = scatter_bound(adjacency, grads)
    own_came, inner_came = swap_core(inner_other_g), swap_core(inner_same_g)

    a, a_sent, b, b_sent, bias_sum = share_rows(at, kept, came, bias_sum, share, own_bound)
    a_came, b_came = swap_wa(a_sent), swap_lo(b_sent)
    split, tiles = live // TILE // 2, -(-nodes // TILE)
    grad_features, lead, matrix = grad_rows(at, adjacency, grads, pieces, nodes, 0, split, n_hi, None, [bias_sum, outer_came])
    outer_back, own_back = back(outer_same_g, outer_came, own_bound, own_came, lead)
    outer_back = swap_outer(outer_back)
    a, a_sent, b, b_sent, bias_sum = fold(at, a, a_came, b, b_came, bias_sum, share, own_back)
    a_came, b_came = swap_lo(a_sent), swap_wa(b_sent)
    grad_features, token = grad_rows(
        at, adjacency, grads, [matrix], nodes, split, tiles, n_hi, grad_features, [bias_sum]
    )
    bias_sum, own, *rest = part_planes(
        at, a, a_came, b, b_came, bias_sum, share, n_hi, [token]
    )
    (own_back,) = tie([own_back], [own])
    returned = (inner_came, outer_back, swap_wa(own_back))
    rest = [rotate_hi(value, k + 1) for k, value in enumerate(rest)]
    grad_features, token = grad_lead(lead, returned, matrix, grad_features)
    mine, other = finish(at, bias_sum, own, rest, share, token)
    other = swap_core(other)
    pair = jnp.where(core == 0, jnp.concatenate([mine, other], axis=1), jnp.concatenate([other, mine], axis=1))
    grad_weight = pair[:share]
    grad_bias = lax.dynamic_slice_in_dim(pair[share], (blk * n_wa + wa) * share, share)
    return (output, grad_features, grad_weight, grad_bias)


def solution(mesh):
    return jax.shard_map(
        body,
        mesh=mesh,
        in_specs=(
            P(("blk", "wa"), None),
            P(("blk", "wa"), None),
            P(("blk", "wa")),
            P(None, ("blk", "wa")),
            P(("blk", "wa")),
            P("blk"),
            P(("blk", "wa"), None),
        ),
        out_specs=(
            P(("blk", "wa"), None),
            P(("blk", "wa"), None),
            P(("blk", "wa"), None),
            P(("blk", "wa")),
        ),
        check_vma=False,
    )
```

```python
import functools
import math

import jax
import jax.numpy as jnp
from jax import lax
from jax.experimental import pallas as pl
from jax.experimental.pallas import tpu as pltpu
from jax.sharding import PartitionSpec as P

FANOUT = 16
BOUND = 256
CMAX = 3016
TILE = 256
F32 = jnp.float32
BF16 = jnp.bfloat16
MIB = 1024 * 1024
GELU_A = math.sqrt(2 / math.pi)
GELU_B = 0.044715


ANY = pl.BlockSpec(memory_space=pl.ANY)
SMEM = pl.BlockSpec(memory_space=pltpu.SMEM)
WHOLE = pl.BlockSpec(memory_space=pltpu.VMEM)
SPARE = 16
FIRST = 4
TOKEN = jax.ShapeDtypeStruct((8, 128), F32)


def params(mib):
    return pltpu.CompilerParams(vmem_limit_bytes=mib * MIB)


def held(value):
    return pltpu.with_memory_space_constraint(value, pltpu.VMEM)


def far(value):
    return pltpu.with_memory_space_constraint(value, pltpu.HBM)


def tie_kernel(*refs):
    pass


def tie(values, after):
    n = len(values)
    return pl.pallas_call(
        tie_kernel,
        in_specs=[ANY] * (n + len(after)),
        out_specs=[ANY] * n,
        out_shape=[jax.ShapeDtypeStruct(v.shape, v.dtype) for v in values],
        input_output_aliases={k: k for k in range(n)},
        compiler_params=params(4),
        name="tie",
    )(*values, *after)


def resident(shape):
    return pl.BlockSpec(shape, lambda *_: (0,) * len(shape), pipeline_mode=pl.Buffered(1))


def cost(flops, nbytes):
    return pl.CostEstimate(flops=int(flops) // 16, bytes_accessed=int(nbytes) // 16, transcendentals=0)


def dot(a, b, ca, cb):
    return lax.dot_general(a, b, (((ca,), (cb,)), ((), ())), preferred_element_type=F32)


def small(value):
    return value.astype(F32).astype(BF16)


def counts_kernel(index_ref, *refs):
    out_ref = refs[-1]
    base = pl.program_id(0) * TILE
    rows = small(lax.broadcasted_iota(jnp.int32, (TILE, 128), 0))
    lanes = lax.broadcasted_iota(jnp.int32, (FANOUT, 128), 1)
    zero, one, two = (jnp.array(v, BF16) for v in (0, 1, 2))
    for c in range(0, out_ref.shape[1], 128):
        entry = small(jnp.clip(index_ref[:, c : c + 128] - base, -1, TILE))
        own = small(jnp.clip(lanes + (c - base), -1, TILE))
        total = jnp.where(own[0:1, :] == rows, two, zero)
        for s in range(FANOUT):
            total = total + jnp.where(entry[s : s + 1, :] == rows, one, zero)
        out_ref[:, c : c + 128] = total


def counts(index, tiles, after):
    n = index.shape[1]
    return pl.pallas_call(
        counts_kernel,
        grid=(tiles,),
        in_specs=[pl.BlockSpec((FANOUT, n), lambda i: (0, 0))] + [ANY] * len(after),
        out_specs=pl.BlockSpec((TILE, n), lambda i: (i, 0)),
        out_shape=pltpu.HBM((tiles * TILE, n), BF16),
        compiler_params=params(12),
        cost_estimate=cost(0, tiles * TILE * n * 16),
        name="counts",
    )(index, *after)


def gather_kernel(c_ref, t_ref, *refs, count):
    o_ref = refs[-1]
    live = t_ref.shape[0]
    total = dot(c_ref[:live, :], t_ref[...], 0, 0)
    for k, ref in enumerate(refs[:count]):
        at = live + k * BOUND
        total = total + dot(c_ref[at : at + BOUND, :], ref[...], 0, 0)
    o_ref[...] = total


def gather(adjacency, features, blocks, live, after):
    h = features.shape[1]
    rows = live + len(blocks) * BOUND
    return pl.pallas_call(
        functools.partial(gather_kernel, count=len(blocks)),
        grid=(live // TILE,),
        in_specs=[pl.BlockSpec((rows, TILE), lambda i: (0, i)), resident((live, h))]
        + [resident((BOUND, h))] * len(blocks)
        + [ANY] * len(after),
        out_specs=pl.BlockSpec((TILE, h), lambda i: (i, 0)),
        out_shape=pltpu.HBM((live, h), F32),
        compiler_params=params(26),
        cost_estimate=cost(2 * live * rows * h, live * h * 6),
        name="gather",
    )(far(adjacency), far(features), *blocks, *after)


def fetch(pieces, planes, target, sem, at_ref):
    core, lo, hi, wa = (at_ref[j] for j in range(1, 5))
    rows = pieces[0].shape[0] // planes
    copies = []
    for n, piece in enumerate(pieces):
        for k in range(planes):
            chip = lax.rem(hi - k + planes, planes) * 2 + (1 - lo if n // 2 % 2 else lo)
            owner = (chip * 2 + (1 - core if n // 4 else core)) * 2 + (1 - wa if n % 2 else wa)
            copies.append(
                pltpu.make_async_copy(
                    piece.at[pl.ds(k * rows, rows), pl.ds(0, target.shape[1])],
                    target.at[pl.ds(pl.multiple_of(owner * rows, rows), rows), :],
                    sem.at[n, k],
                )
            )
    return copies


def layer_kernel(at_ref, part_ref, c_ref, cl_ref, last_ref, inv_ref, ct_ref, *refs, tiles, planes):
    pieces, refs = refs[:8], refs[8:]
    o_ref, agl_ref, m_all, gl_all, gb, far_ref, w, b, sem = refs
    i = pl.program_id(0)
    h = part_ref.shape[1]
    copies = fetch(pieces, planes, w, sem, at_ref)

    @pl.when(i == 0)
    def _():
        for copy in copies:
            copy.start()
        gb[...] = jnp.zeros_like(gb)

    @pl.when(i < tiles)
    def _():
        total = part_ref[...] + dot(c_ref[...], last_ref[...], 0, 0)
        m_all[pl.ds(pl.multiple_of(i * TILE, TILE), TILE), :] = (total * inv_ref[...]).astype(BF16)

    @pl.when(i == 0)
    def _():
        for copy in copies:
            copy.wait()
        b[...] = w[:, h:].astype(F32).T[:8, :]

    @pl.when(i < tiles)
    def _():
        base = pl.multiple_of(i * TILE, TILE)
        rows = pl.ds(base, TILE)
        mixed = m_all[rows, :]
        live = base + lax.broadcasted_iota(jnp.int32, (TILE, 256), 0) < at_ref[0]
        inverse = inv_ref[...]
        for j in range(0, h, 256):
            at = slice(j, j + 256)
            v = dot(mixed, w[:, at], 1, 0) + b[0:1, at]
            square = v * v
            half = jnp.where(live, 0.5 + 0.5 * jnp.tanh(v * (GELU_A + (GELU_A * GELU_B) * square)), 0.0)
            o_ref[:, at] = v * half
            slope = half + (half - half * half) * (v * (2 * GELU_A + (6 * GELU_A * GELU_B) * square))
            grad = ct_ref[:, at].astype(F32) * slope
            gl_all[rows, at] = grad.astype(BF16)
            agl_ref[rows, at] = (grad * inverse).astype(BF16)
            gb[:, at] += jnp.sum(grad.reshape(TILE // 8, 8, 256), axis=0)

    @pl.when(i == tiles)
    def _():
        o_ref[...] = jnp.zeros_like(o_ref)
        far_ref[...] = dot(cl_ref[...], agl_ref[...], 1, 0).astype(BF16)


def weight_kernel(at_ref, m_all, gl_all, gb, *refs, mine):
    out_ref, gb_ref = refs[-2:]
    i = pl.program_id(0)
    blocks = m_all.shape[1] // TILE
    n = out_ref.shape[1]
    core = at_ref[1] if mine else 1 - at_ref[1]
    columns = pl.ds(pl.multiple_of(core * n, n), n)

    @pl.when(i < blocks)
    def _():
        at = pl.ds(pl.multiple_of(i * TILE, TILE), TILE)
        out_ref[...] = dot(m_all[:, at], gl_all[:, columns], 0, 0).astype(BF16)

    @pl.when(i == blocks)
    def _():
        total = jnp.sum(gb[:, columns], axis=0, keepdims=True)
        gb_ref[...] = jnp.broadcast_to(total, gb_ref.shape)
        if not mine:
            out_ref[:SPARE, :] = jnp.broadcast_to(total, (SPARE, n)).astype(BF16)


def weight_share(at, mixed, low, bias, mine, after):
    live, h = mixed.shape
    n, blocks = h // 2, h // TILE
    rows = h if mine else h + SPARE
    return pl.pallas_call(
        functools.partial(weight_kernel, mine=mine),
        grid_spec=pltpu.PrefetchScalarGridSpec(
            num_scalar_prefetch=1,
            grid=(blocks + 1,),
            in_specs=[WHOLE, WHOLE, resident((8, h))] + [ANY] * len(after),
            out_specs=[
                pl.BlockSpec((TILE, n), lambda i, s: (jnp.minimum(i, -(-rows // TILE) - 1), 0)),
                resident((8, n)),
            ],
        ),
        out_shape=[(pltpu.VMEM if mine else pltpu.HBM)((rows, n), BF16), jax.ShapeDtypeStruct((8, n), F32)],
        compiler_params=params(12),
        cost_estimate=cost(live * h * h, live * h * 4),
        name="weight_share",
    )(at, held(mixed), held(low), bias, *after)


def layer(at, part, adjacency, last, inverse, cotangent, pieces, planes):
    live, h = part.shape
    nodes = cotangent.shape[0]
    tiles = live // TILE
    below = adjacency.shape[0] // BOUND - 1

    def row(i, s):
        return (jnp.minimum(i, tiles - 1), 0)

    return pl.pallas_call(
        functools.partial(layer_kernel, tiles=tiles, planes=planes),
        grid_spec=pltpu.PrefetchScalarGridSpec(
            num_scalar_prefetch=1,
            grid=(tiles + 1,),
            in_specs=[
                pl.BlockSpec((TILE, h), row),
                pl.BlockSpec((BOUND, TILE), lambda i, s: (below, jnp.minimum(i, tiles - 1))),
                pl.BlockSpec((BOUND, live), lambda i, s: (below, 0), pipeline_mode=pl.Buffered(1)),
                resident(last.shape),
                pl.BlockSpec((TILE, 1), row),
                pl.BlockSpec((TILE, h), row),
            ]
            + [ANY] * len(pieces),
            out_specs=[
                pl.BlockSpec((TILE, h), lambda i, s: (i, 0)),
                WHOLE,
                WHOLE,
                WHOLE,
                resident((8, h)),
                resident((BOUND, h)),
            ],
            scratch_shapes=[
                pltpu.VMEM((h, pieces[0].shape[1]), BF16),
                pltpu.VMEM((8, h), F32),
                pltpu.SemaphoreType.DMA((len(pieces), planes)),
            ],
        ),
        out_shape=[
            jax.ShapeDtypeStruct((nodes, h), F32),
            pltpu.VMEM((live, h), BF16),
            pltpu.VMEM((live, h), BF16),
            pltpu.VMEM((live, h), BF16),
            jax.ShapeDtypeStruct((8, h), F32),
            pltpu.HBM((BOUND, h), BF16),
        ],
        compiler_params=params(24),
        cost_estimate=cost(3 * live * h * h, live * h * 12),
        name="layer",
    )(at, far(part), far(adjacency), far(adjacency), last, inverse, far(cotangent), *pieces)


def halves(at_ref, value, rows):
    parts = [value[k * rows : (k + 1) * rows] for k in range(4)]
    even, odd = jnp.concatenate([parts[0], parts[2]]), jnp.concatenate([parts[1], parts[3]])
    first = at_ref[4] == 0
    return jnp.where(first, even, odd), jnp.where(first, odd, even)


def spare_rows(row, n):
    count = -(-row.shape[1] // n)
    row = jnp.concatenate([row, jnp.zeros((1, count * n - row.shape[1]), F32)], axis=1) if count * n > row.shape[1] else row
    at = lax.broadcasted_iota(jnp.int32, (SPARE, n), 0)
    rows = jnp.zeros((SPARE, n), F32)
    for k in range(count):
        rows = jnp.where(at == k, row[:, k * n : (k + 1) * n], rows)
    return rows.astype(BF16)


def from_spare(rows, total):
    n = rows.shape[1]
    return jnp.concatenate([rows[k : k + 1, :] for k in range(-(-total // n))], axis=1)[:, :total].astype(F32)


def share_kernel(at_ref, kept_ref, came_ref, cb_ref, gb_ref, a_own, a_sent, b_own, b_sent, gb_out, *, rows):
    t = pl.program_id(0)
    last = pl.num_programs(0) - 1
    n = a_own.shape[1]
    groups = TILE // (4 * rows)

    @pl.when(t < last)
    def _():
        part = kept_ref[...].astype(F32) + came_ref[...].astype(F32)
        for g in range(groups):
            value = part[g * 4 * rows : (g + 1) * 4 * rows].astype(BF16)
            mine, other = halves(at_ref, value[:, :n], rows)
            at = slice(g * 2 * rows, (g + 1) * 2 * rows)
            a_own[at, :] = mine
            a_sent[at, :] = other
            here = (t * groups + g) % 2 == at_ref[2]
            at = slice(g // 2 * 4 * rows, (g // 2 + 1) * 4 * rows)

            @pl.when(here)
            def _():
                b_own[at, :] = value[:, n:]

            @pl.when(jnp.logical_not(here))
            def _():
                b_sent[at, :] = value[:, n:]

    @pl.when(t == last)
    def _():
        total = gb_ref[0:1, :] + cb_ref[0:1, :].astype(F32)
        gb_out[...] = jnp.broadcast_to(total, gb_out.shape)
        a_sent[:SPARE, :] = spare_rows(total, n)
        b_sent[:SPARE, :] = jnp.zeros((SPARE, b_sent.shape[1]), BF16)


def share_rows(at, kept, came, bias, rows):
    h, n = kept.shape
    n_a = n * FIRST // 8
    n_b = n - n_a
    blocks = h // TILE
    single = TILE == 4 * rows
    b_rows = TILE if single else TILE // 2

    def tile(t):
        return jnp.minimum(t, blocks - 1)

    def plane(t, s):
        return (tile(t) // 2 if single else tile(t), 0)

    return pl.pallas_call(
        functools.partial(share_kernel, rows=rows),
        grid_spec=pltpu.PrefetchScalarGridSpec(
            num_scalar_prefetch=1,
            grid=(blocks + 1,),
            in_specs=[
                pl.BlockSpec((TILE, n), lambda t, s: (tile(t), 0)),
                pl.BlockSpec((TILE, n), lambda t, s: (tile(t), 0)),
                pl.BlockSpec((SPARE, n), lambda t, s: (h // SPARE, 0)),
                resident((8, n)),
            ],
            out_specs=[
                pl.BlockSpec((TILE // 2, n_a), lambda t, s: (tile(t), 0)),
                pl.BlockSpec((TILE // 2, n_a), lambda t, s: (t, 0)),
                pl.BlockSpec((b_rows, n_b), plane),
                pl.BlockSpec((b_rows, n_b), lambda t, s: (t // 2 if single else t, 0)),
                resident((8, n)),
            ],
        ),
        out_shape=[
            pltpu.HBM((h // 2, n_a), BF16),
            pltpu.HBM((h // 2 + SPARE, n_a), BF16),
            pltpu.HBM((h // 2, n_b), BF16),
            pltpu.HBM((h // 2 + SPARE, n_b), BF16),
            jax.ShapeDtypeStruct((8, n), F32),
        ],
        compiler_params=params(10),
        cost_estimate=cost(0, h * n * 8),
        name="share",
    )(at, kept, came, came, bias)


def fold_kernel(at_ref, a_ref, a_came, b_ref, b_came, gb_ref, _, a_own, a_sent, b_own, b_sent, gb_out, *, rows):
    lo, two = at_ref[2], 2 * rows
    n = a_ref.shape[1]
    planes = a_ref.shape[0] // (2 * two)
    for z in range(planes):
        out = slice(z * two, (z + 1) * two)
        near = pl.ds(pl.multiple_of((2 * z + lo) * two, two), two)
        far = pl.ds(pl.multiple_of((2 * z + 1 - lo) * two, two), two)
        a_own[out, :] = a_ref[near, :].astype(F32) + a_came[near, :].astype(F32)
        a_sent[out, :] = (a_ref[far, :].astype(F32) + a_came[far, :].astype(F32)).astype(BF16)
        at = slice(z * 2 * two, (z + 1) * 2 * two)
        mine, other = halves(at_ref, b_ref[at, :].astype(F32) + b_came[at, :].astype(F32), rows)
        b_own[out, :] = mine
        b_sent[out, :] = other.astype(BF16)
    total = gb_ref[0:1, :] + from_spare(a_came[a_ref.shape[0] :, :], gb_ref.shape[1])
    gb_out[...] = jnp.broadcast_to(total, gb_out.shape)
    a_sent[planes * two :, :] = spare_rows(total, n)


def fold(at, a_own, a_came, b_own, b_came, bias, rows, after):
    count, n_a, n_b = b_own.shape[0] // 2, a_own.shape[1], b_own.shape[1]
    return pl.pallas_call(
        functools.partial(fold_kernel, rows=rows),
        in_specs=[SMEM] + [WHOLE] * 5 + [ANY],
        out_specs=[WHOLE] * 5,
        out_shape=[
            jax.ShapeDtypeStruct((count, n_a), F32),
            jax.ShapeDtypeStruct((count + SPARE, n_a), BF16),
            jax.ShapeDtypeStruct((count, n_b), F32),
            jax.ShapeDtypeStruct((count, n_b), BF16),
            jax.ShapeDtypeStruct(bias.shape, F32),
        ],
        compiler_params=params(22),
        cost_estimate=cost(0, b_own.size * 9),
        name="fold",
    )(at, far(a_own), a_came, far(b_own), b_came, bias, after)


def part_kernel(at_ref, a_ref, a_came, b_ref, b_came, gb_ref, *refs, rows, planes):
    gb_out, own, *sent = refs[-1 - planes :]
    two = 2 * rows
    n = a_ref.shape[1]
    total = gb_ref[0:1, :] + from_spare(a_came[a_ref.shape[0] :, :], gb_ref.shape[1])
    gb_out[...] = jnp.broadcast_to(total, gb_out.shape)
    for k in range(planes):
        at = pl.ds(pl.multiple_of(lax.rem(at_ref[3] + k, planes) * two, two), two)
        out = own if k == 0 else sent[k - 1]
        out[:two, :n] = (a_ref[at, :] + a_came[at, :].astype(F32)).astype(out.dtype)
        out[:two, n:] = (b_ref[at, :] + b_came[at, :].astype(F32)).astype(out.dtype)
        if k:
            out[two:, :] = jnp.broadcast_to(total, (SPARE, total.shape[1])).astype(BF16)


def part_planes(at, a_own, a_came, b_own, b_came, bias, rows, planes, after):
    n = a_own.shape[1] + b_own.shape[1]
    return pl.pallas_call(
        functools.partial(part_kernel, rows=rows, planes=planes),
        in_specs=[SMEM] + [WHOLE] * 5 + [ANY] * len(after),
        out_specs=[WHOLE] * (1 + planes),
        out_shape=[jax.ShapeDtypeStruct(bias.shape, F32), jax.ShapeDtypeStruct((2 * rows, n), F32)]
        + [jax.ShapeDtypeStruct((2 * rows + SPARE, n), BF16)] * (planes - 1),
        compiler_params=params(14),
        cost_estimate=cost(0, a_own.size * 18),
        name="part_planes",
    )(at, a_own, a_came, b_own, b_came, bias, *after)


def finish_kernel(at_ref, gb_ref, own, *refs, rows):
    came, mine_ref, other_ref = refs[:-3], refs[-2], refs[-1]
    total, bias = own[...], gb_ref[0:1, :]
    for ref in came:
        total = total + ref[: 2 * rows, :].astype(F32)
        bias = bias + ref[2 * rows : 2 * rows + 1, :].astype(F32)
    first = at_ref[1] == 0
    low, high = total[:rows], total[rows:]
    bias = jnp.broadcast_to(bias, (8, bias.shape[1]))
    mine_ref[:rows, :], other_ref[:rows, :] = jnp.where(first, low, high), jnp.where(first, high, low)
    mine_ref[rows:, :], other_ref[rows:, :] = bias, bias


def finish(at, bias, own, came, rows, after):
    shape = jax.ShapeDtypeStruct((rows + 8, own.shape[1]), F32)
    return pl.pallas_call(
        functools.partial(finish_kernel, rows=rows),
        in_specs=[SMEM] + [WHOLE] * (2 + len(came)) + [ANY],
        out_specs=[WHOLE] * 2,
        out_shape=[shape] * 2,
        compiler_params=params(10),
        cost_estimate=cost(0, own.size * 8),
        name="finish",
    )(at, bias, own, *came, after)


def scatter_bound_kernel(c_ref, g_ref, *refs, count):
    *outs, part, sem = refs[len(refs) - 2 - count :]
    i = pl.program_id(0)
    part[i] = dot(c_ref[...], g_ref[...], 1, 0).astype(BF16)
    copies = [pltpu.make_async_copy(part.at[k], out, sem.at[k]) for k, out in enumerate(outs)]
    for k, copy in enumerate(copies):

        @pl.when(i == k)
        def _():
            copy.start()

    @pl.when(i == len(outs) - 1)
    def _():
        for copy in copies:
            copy.wait()


def scatter_bound(adjacency, grads, after):
    live, h = grads.shape
    blocks = (adjacency.shape[0] - live) // BOUND - 1
    return pl.pallas_call(
        functools.partial(scatter_bound_kernel, count=blocks),
        grid=(blocks,),
        in_specs=[pl.BlockSpec((BOUND, live), lambda i: (i + live // BOUND, 0)), resident((live, h))] + [ANY] * len(after),
        out_specs=[ANY] * blocks,
        out_shape=[pltpu.HBM((BOUND, h), BF16)] * blocks,
        scratch_shapes=[pltpu.VMEM((blocks, BOUND, h), BF16), pltpu.SemaphoreType.DMA((blocks,))],
        compiler_params=params(22),
        cost_estimate=cost(2 * blocks * BOUND * live * h, live * h * 4),
        name="scatter_bound",
    )(far(adjacency), grads, *after)


def grad_rows_kernel(at_ref, c_ref, g_ref, *refs, low, tiles, planes):
    w, sem, sem_out = refs[-3:]
    i = pl.program_id(0)
    if low:
        o_ref, lead_ref = refs[-5:-3]
        copies = [pltpu.make_async_copy(refs[0], w, sem_out)]
    else:
        o_ref, lead_ref, w_ref = refs[-6:-3]
        copies = fetch(refs[:8], planes, w, sem, at_ref)
        copy_out = pltpu.make_async_copy(w, w_ref, sem_out)

    @pl.when(i == 0)
    def _():
        for copy in copies:
            copy.start()

    @pl.when(low + i < tiles)
    def _():
        total = dot(c_ref[...], g_ref[...], 1, 0)

        @pl.when(i == 0)
        def _():
            lead_ref[...] = total if low == 0 else jnp.zeros_like(lead_ref)
            for copy in copies:
                copy.wait()
            if low == 0:
                copy_out.start()

        @pl.when(low + i > 0)
        def _():
            o_ref[...] = dot(total.astype(BF16), w[...], 1, 1)

    @pl.when(low + i == tiles)
    def _():
        o_ref[...] = jnp.zeros_like(o_ref)

    if low == 0:

        @pl.when(i == pl.num_programs(0) - 1)
        def _():
            copy_out.wait()


def grad_rows(at, adjacency, grads, weight, nodes, low, high, planes, before, after):
    live, h = grads.shape
    tiles = live // TILE
    extra = [] if before is None else [before]
    outs = [jax.ShapeDtypeStruct((nodes, h), F32), TOKEN if low else jax.ShapeDtypeStruct((TILE, h), F32)]
    out_specs = [pl.BlockSpec((TILE, h), lambda i, s: (low + i, 0)), resident((8, 128) if low else (TILE, h))]
    if low == 0:
        outs += [jax.ShapeDtypeStruct((h, h), BF16)]
        out_specs += [ANY]
    return pl.pallas_call(
        functools.partial(grad_rows_kernel, low=low, tiles=tiles, planes=planes),
        grid_spec=pltpu.PrefetchScalarGridSpec(
            num_scalar_prefetch=1,
            grid=(high - low,),
            in_specs=[
                pl.BlockSpec((TILE, live), lambda i, s: (jnp.minimum(low + i, tiles - 1), 0)),
                resident((live, h)),
            ]
            + [ANY] * (len(weight) + len(extra) + len(after)),
            out_specs=out_specs,
            scratch_shapes=[
                pltpu.VMEM((h, h), BF16),
                pltpu.SemaphoreType.DMA((len(weight), planes)),
                pltpu.SemaphoreType.DMA,
            ],
        ),
        out_shape=outs,
        input_output_aliases={3 + len(weight): 0} if extra else {},
        compiler_params=params(30),
        cost_estimate=cost((2 * live + 2 * h) * (high - low) * TILE * h, live * h * 8),
        name="grad_rows",
    )(at, far(adjacency), grads, *weight, *extra, *after)


def back_kernel(a_ref, b_ref, c_ref, d_ref, _, o_ref, p_ref):
    o_ref[...] = (a_ref[...].astype(F32) + b_ref[...].astype(F32)).astype(BF16)
    p_ref[...] = (c_ref[...].astype(F32) + d_ref[...].astype(F32)).astype(BF16)


def back(a, b, c, d, after):
    block = pl.BlockSpec((64, a.shape[1]), lambda i: (i, 0))
    return pl.pallas_call(
        back_kernel,
        grid=(a.shape[0] // 64,),
        in_specs=[block] * 4 + [ANY],
        out_specs=[block] * 2,
        out_shape=[jax.ShapeDtypeStruct(a.shape, BF16)] * 2,
        compiler_params=params(10),
        cost_estimate=cost(0, a.size * 12),
        name="back",
    )(far(a), b, far(c), d, after)


def grad_lead_kernel(lead_ref, *refs):
    came, (w_ref, _, o_ref, token_ref, total) = refs[:3], refs[3:]

    @pl.when(pl.program_id(0) == 0)
    def _():
        value = lead_ref[...]
        for ref in came:
            value = value + ref[...].astype(F32)
        total[...] = value.astype(BF16)
        token_ref[...] = jnp.zeros_like(token_ref)

    o_ref[...] = dot(total[...], w_ref[...], 1, 1)


def grad_lead(lead, came, weight, grads):
    rows, h = lead.shape
    return pl.pallas_call(
        grad_lead_kernel,
        grid=(4,),
        in_specs=[resident((rows, h))] * 4 + [pl.BlockSpec((h // 4, h), lambda i: (i, 0)), ANY],
        out_specs=[pl.BlockSpec((rows, h // 4), lambda i: (0, i)), resident((8, 128))],
        out_shape=[jax.ShapeDtypeStruct(grads.shape, F32), TOKEN],
        scratch_shapes=[pltpu.VMEM((rows, h), BF16)],
        input_output_aliases={5: 0},
        compiler_params=params(20),
        cost_estimate=cost(2 * rows * h * h, h * h * 2),
        name="grad_lead",
    )(lead, *came, weight, grads)


def body(features, weight, bias, neighbours, degrees, cluster_sizes, cotangent):
    axes = ("blk", "wa")
    n_blk, n_wa = lax.axis_size("blk"), lax.axis_size("wa")
    devices, n_hi = n_blk * n_wa, n_blk // 4
    blk, wa = lax.axis_index("blk"), lax.axis_index("wa")
    core, lo, hi = blk % 2, (blk // 2) % 2, blk // 4
    nodes, h = features.shape
    share, n = h // devices, h // 2
    live = min(nodes, -(-(-(-CMAX // n_wa)) // TILE) * TILE)

    def permute(value, target):
        pairs = [(b * n_wa + w, target(b, w)) for b in range(n_blk) for w in range(n_wa)]
        return lax.ppermute(value, axes, [(s, b * n_wa + w) for s, (b, w) in pairs])

    def swap_wa(value):
        return permute(value, lambda b, w: (b, 1 - w))

    def swap_core(value):
        return permute(value, lambda b, w: (b ^ 1, w))

    def swap_outer(value):
        return permute(value, lambda b, w: ((b + (1 if b % 2 else -1)) % n_blk, w))

    def swap_lo(value):
        return permute(value, lambda b, w: (b ^ 2, w))

    def rotate_hi(value, k):
        return permute(value, lambda b, w: ((b + 4 * k) % n_blk, w))

    leading = features[:BOUND]
    partner = swap_wa(leading)
    outer_same = swap_outer(leading)

    sheet = jnp.concatenate([weight, jnp.broadcast_to(bias[:, None], (share, 128))], axis=1)
    planes = [rotate_hi(sheet, k) for k in range(1, n_hi)]

    live_count = (cluster_sizes[0] - wa + n_wa - 1) // n_wa
    table = neighbours[:, :live]
    beyond = table - nodes
    segment, within = beyond // (n_wa * BOUND), beyond % (n_wa * BOUND)
    same = within // BOUND == wa
    row = within % BOUND
    side = jnp.where(same, 0, BOUND) + row
    inner = (segment == 2) == (core == 0)
    away = jnp.where(inner, live + BOUND, live + BOUND + n_wa * BOUND) + side
    home = jnp.where(same, row, live + row)
    index = jnp.where(table < nodes, table, jnp.where(segment == 0, home, away))
    valid = jnp.arange(FANOUT, dtype=jnp.int32)[:, None] < degrees[None, :live]
    index = jnp.where(valid, index, -1)
    inverse = (1.0 / (degrees[:live].astype(F32) + 1.0))[:, None]
    at = jnp.stack([live_count, core, lo, hi, wa]).astype(jnp.int32)

    adjacency = counts(index, (live + (1 + 2 * n_wa) * BOUND) // TILE, [inverse, at])
    partner, *planes = tie([partner, *planes], [far(adjacency)])
    sheet = jnp.concatenate([sheet, *planes])
    half_sheet, row_sheet = swap_wa(sheet), swap_lo(sheet)
    inner_same, inner_other = swap_core(leading), swap_core(partner)
    part = gather(adjacency, features, (partner, inner_same, inner_other, outer_same), live, [inverse, at])
    half_sheet, row_sheet, outer_same = tie([half_sheet, row_sheet, outer_same], [far(part)])
    outer_other = swap_wa(outer_same)
    both_sheet, outer_other = tie([swap_lo(half_sheet), outer_other], [])
    pieces = [sheet, half_sheet, row_sheet, both_sheet]
    pieces = pieces + [swap_core(value) for value in pieces]
    output, grads, mixed, low, bias_sum, outer_other_g = layer(
        at, part, adjacency, outer_other, inverse, cotangent, pieces, n_hi
    )
    sent, token = weight_share(at, mixed, low, bias_sum, False, [])
    came = swap_core(sent)
    kept, bias_sum = weight_share(at, mixed, low, bias_sum, True, [token])

    a, a_sent, b, b_sent, bias_sum = share_rows(at, kept, came, bias_sum, share)
    a_came, b_came = swap_wa(a_sent), swap_lo(b_sent)

    outer_came = swap_wa(outer_other_g)
    own_bound, inner_same_g, inner_other_g, outer_same_g = scatter_bound(adjacency, grads, [bias_sum])
    own_came, inner_came = swap_core(inner_other_g), swap_core(inner_same_g)
    split, tiles = live // TILE // 2, -(-nodes // TILE)
    grad_features, lead, matrix = grad_rows(at, adjacency, grads, pieces, nodes, 0, split, n_hi, None, [far(own_bound), outer_came])
    outer_back, own_back = back(outer_same_g, outer_came, own_bound, own_came, lead)
    outer_back = swap_outer(outer_back)
    a, a_sent, b, b_sent, bias_sum = fold(at, a, a_came, b, b_came, bias_sum, share, own_back)
    a_came, b_came = swap_lo(a_sent), swap_wa(b_sent)
    grad_features, token = grad_rows(
        at, adjacency, grads, [matrix], nodes, split, tiles, n_hi, grad_features, [bias_sum]
    )
    bias_sum, own, *rest = part_planes(
        at, a, a_came, b, b_came, bias_sum, share, n_hi, [token]
    )
    (own_back,) = tie([own_back], [own])
    returned = (inner_came, outer_back, swap_wa(own_back))
    rest = [rotate_hi(value, k + 1) for k, value in enumerate(rest)]
    grad_features, token = grad_lead(lead, returned, matrix, grad_features)
    mine, other = finish(at, bias_sum, own, rest, share, token)
    other = swap_core(other)
    pair = jnp.where(core == 0, jnp.concatenate([mine, other], axis=1), jnp.concatenate([other, mine], axis=1))
    grad_weight = pair[:share]
    grad_bias = lax.dynamic_slice_in_dim(pair[share], (blk * n_wa + wa) * share, share)
    return (output, grad_features, grad_weight, grad_bias)


def solution(mesh):
    return jax.shard_map(
        body,
        mesh=mesh,
        in_specs=(
            P(("blk", "wa"), None),
            P(("blk", "wa"), None),
            P(("blk", "wa")),
            P(None, ("blk", "wa")),
            P(("blk", "wa")),
            P("blk"),
            P(("blk", "wa"), None),
        ),
        out_specs=(
            P(("blk", "wa"), None),
            P(("blk", "wa"), None),
            P(("blk", "wa"), None),
            P(("blk", "wa")),
        ),
        check_vma=False,
    )
```

```python
import functools
import math

import jax
import jax.numpy as jnp
from jax import lax
from jax.experimental import pallas as pl
from jax.experimental.pallas import tpu as pltpu
from jax.sharding import PartitionSpec as P

FANOUT = 16
BOUND = 256
CMAX = 3016
TILE = 256
WIDE = 512
F32 = jnp.float32
BF16 = jnp.bfloat16
MIB = 1024 * 1024
GELU_A = math.sqrt(2 / math.pi)
GELU_B = 0.044715


ANY = pl.BlockSpec(memory_space=pl.ANY)
SMEM = pl.BlockSpec(memory_space=pltpu.SMEM)
WHOLE = pl.BlockSpec(memory_space=pltpu.VMEM)
SPARE = 16
FIRST = 4
TOKEN = jax.ShapeDtypeStruct((8, 128), F32)


def params(mib):
    return pltpu.CompilerParams(vmem_limit_bytes=mib * MIB)


def held(value):
    return pltpu.with_memory_space_constraint(value, pltpu.VMEM)


def far(value):
    return pltpu.with_memory_space_constraint(value, pltpu.HBM)


def tie_kernel(*refs):
    pass


def tie(values, after):
    n = len(values)
    return pl.pallas_call(
        tie_kernel,
        in_specs=[ANY] * (n + len(after)),
        out_specs=[ANY] * n,
        out_shape=[jax.ShapeDtypeStruct(v.shape, v.dtype) for v in values],
        input_output_aliases={k: k for k in range(n)},
        compiler_params=params(4),
        name="tie",
    )(*values, *after)


def resident(shape):
    return pl.BlockSpec(shape, lambda *_: (0,) * len(shape), pipeline_mode=pl.Buffered(1))


def cost(flops, nbytes):
    return pl.CostEstimate(flops=int(flops) // 16, bytes_accessed=int(nbytes) // 16, transcendentals=0)


def dot(a, b, ca, cb):
    return lax.dot_general(a, b, (((ca,), (cb,)), ((), ())), preferred_element_type=F32)


def small(value):
    return value.astype(F32).astype(BF16)


def counts_kernel(index_ref, *refs):
    out_ref = refs[-1]
    base = pl.program_id(0) * TILE
    rows = small(lax.broadcasted_iota(jnp.int32, (TILE, 128), 0))
    lanes = lax.broadcasted_iota(jnp.int32, (FANOUT, 128), 1)
    zero, one, two = (jnp.array(v, BF16) for v in (0, 1, 2))
    for c in range(0, out_ref.shape[1], 128):
        entry = small(jnp.clip(index_ref[:, c : c + 128] - base, -1, TILE))
        own = small(jnp.clip(lanes + (c - base), -1, TILE))
        total = jnp.where(own[0:1, :] == rows, two, zero)
        for s in range(FANOUT):
            total = total + jnp.where(entry[s : s + 1, :] == rows, one, zero)
        out_ref[:, c : c + 128] = total


def counts(index, tiles, after):
    n = index.shape[1]
    return pl.pallas_call(
        counts_kernel,
        grid=(tiles,),
        in_specs=[pl.BlockSpec((FANOUT, n), lambda i: (0, 0))] + [ANY] * len(after),
        out_specs=pl.BlockSpec((TILE, n), lambda i: (i, 0)),
        out_shape=pltpu.HBM((tiles * TILE, n), BF16),
        compiler_params=params(12),
        cost_estimate=cost(0, tiles * TILE * n * 16),
        name="counts",
    )(index, *after)


def gather_kernel(c_ref, t_ref, *refs, count):
    o_ref = refs[-1]
    live = t_ref.shape[0]
    total = dot(c_ref[:live, :], t_ref[...], 0, 0)
    for k, ref in enumerate(refs[:count]):
        at = live + k * BOUND
        total = total + dot(c_ref[at : at + BOUND, :], ref[...], 0, 0)
    o_ref[...] = total


def gather(adjacency, features, blocks, live, after):
    h = features.shape[1]
    rows = live + len(blocks) * BOUND
    return pl.pallas_call(
        functools.partial(gather_kernel, count=len(blocks)),
        grid=(live // TILE,),
        in_specs=[pl.BlockSpec((rows, TILE), lambda i: (0, i)), resident((live, h))]
        + [resident((BOUND, h))] * len(blocks)
        + [ANY] * len(after),
        out_specs=pl.BlockSpec((TILE, h), lambda i: (i, 0)),
        out_shape=pltpu.HBM((live, h), F32),
        compiler_params=params(26),
        cost_estimate=cost(2 * live * rows * h, live * h * 6),
        name="gather",
    )(far(adjacency), far(features), *blocks, *after)


def fetch(pieces, numbers, planes, target, sem, at_ref):
    core, lo, hi, wa = (at_ref[j] for j in range(1, 5))
    rows = target.shape[0] // (8 * planes)
    copies = []
    for m, ((n, first), piece) in enumerate(zip(numbers, pieces)):
        for k in range(piece.shape[0] // rows):
            chip = lax.rem(hi - first - k + planes, planes) * 2 + (1 - lo if n // 2 % 2 else lo)
            owner = (chip * 2 + (1 - core if n // 4 else core)) * 2 + (1 - wa if n % 2 else wa)
            copies.append(
                pltpu.make_async_copy(
                    piece.at[pl.ds(k * rows, rows), :],
                    target.at[pl.ds(pl.multiple_of(owner * rows, rows), rows), :],
                    sem.at[m, k],
                )
            )
    return copies


def place_kernel(at_ref, *refs, numbers, planes):
    target, sem = refs[-2:]
    copies = fetch(refs[: len(numbers)], numbers, planes, target, sem, at_ref)
    for copy in copies:
        copy.start()
    for copy in copies:
        copy.wait()


def place(at, pieces, numbers, planes):
    h, n = 8 * pieces[0].shape[0], pieces[0].shape[1]
    return pl.pallas_call(
        functools.partial(place_kernel, numbers=numbers, planes=planes),
        in_specs=[SMEM] + [ANY] * len(pieces),
        out_specs=WHOLE,
        out_shape=pltpu.VMEM((h, n), BF16),
        scratch_shapes=[pltpu.SemaphoreType.DMA((len(pieces), planes))],
        compiler_params=params(4),
        cost_estimate=cost(0, h * n),
        name="place",
    )(at, *pieces)


def layer_kernel(at_ref, part_ref, c_ref, d_ref, cl_ref, same_ref, last_ref, inv_ref, ct_ref, *refs, tiles, numbers, planes):
    count = len(numbers)
    pieces, refs = refs[:count], refs[count + 1 :]
    o_ref, agl_ref, m_all, gl_all, gb, far_ref, w, b, sem = refs
    i = pl.program_id(0)
    h = part_ref.shape[1]
    copies = fetch(pieces, numbers, planes, w, sem, at_ref)

    @pl.when(i == 0)
    def _():
        for copy in copies:
            copy.start()
        gb[...] = jnp.zeros_like(gb)

    @pl.when(i < tiles)
    def _():
        total = part_ref[...] + dot(c_ref[...], same_ref[...], 0, 0) + dot(d_ref[...], last_ref[...], 0, 0)
        m_all[pl.ds(pl.multiple_of(i * TILE, TILE), TILE), :] = (total * inv_ref[...]).astype(BF16)

    @pl.when(i == 0)
    def _():
        for copy in copies:
            copy.wait()
        b[...] = w[:, h:].astype(F32).T[:8, :]

    @pl.when(i < tiles)
    def _():
        base = pl.multiple_of(i * TILE, TILE)
        rows = pl.ds(base, TILE)
        mixed = m_all[rows, :]
        live = base + lax.broadcasted_iota(jnp.int32, (TILE, 256), 0) < at_ref[0]
        inverse = inv_ref[...]
        for j in range(0, h, 256):
            at = slice(j, j + 256)
            v = dot(mixed, w[:, at], 1, 0) + b[0:1, at]
            square = v * v
            half = jnp.where(live, 0.5 + 0.5 * jnp.tanh(v * (GELU_A + (GELU_A * GELU_B) * square)), 0.0)
            o_ref[:, at] = v * half
            slope = half + (half - half * half) * (v * (2 * GELU_A + (6 * GELU_A * GELU_B) * square))
            grad = ct_ref[:, at].astype(F32) * slope
            gl_all[rows, at] = grad.astype(BF16)
            agl_ref[rows, at] = (grad * inverse).astype(BF16)
            gb[:, at] += jnp.sum(grad.reshape(TILE // 8, 8, 256), axis=0)

    @pl.when(i == tiles)
    def _():
        o_ref[...] = jnp.zeros_like(o_ref)
        far_ref[...] = dot(cl_ref[...], agl_ref[...], 1, 0).astype(BF16)


def weight_kernel(at_ref, m_all, gl_all, gb, *refs, mine):
    out_ref, gb_ref = refs[-2:]
    i = pl.program_id(0)
    blocks = m_all.shape[1] // WIDE
    n = out_ref.shape[1]
    core = at_ref[1] if mine else 1 - at_ref[1]
    columns = pl.ds(pl.multiple_of(core * n, n), n)

    @pl.when(i < blocks)
    def _():
        at = pl.ds(pl.multiple_of(i * WIDE, WIDE), WIDE)
        out_ref[...] = dot(m_all[:, at], gl_all[:, columns], 0, 0).astype(BF16)

    @pl.when(i == blocks)
    def _():
        total = jnp.sum(gb[:, columns], axis=0, keepdims=True)
        gb_ref[...] = jnp.broadcast_to(total, gb_ref.shape)
        if not mine:
            out_ref[:SPARE, :] = jnp.broadcast_to(total, (SPARE, n)).astype(BF16)


def weight_share(at, mixed, low, bias, mine, after):
    live, h = mixed.shape
    n, blocks = h // 2, h // WIDE
    rows = h if mine else h + SPARE
    return pl.pallas_call(
        functools.partial(weight_kernel, mine=mine),
        grid_spec=pltpu.PrefetchScalarGridSpec(
            num_scalar_prefetch=1,
            grid=(blocks + 1,),
            in_specs=[WHOLE, WHOLE, resident((8, h))] + [ANY] * len(after),
            out_specs=[
                pl.BlockSpec((WIDE, n), lambda i, s: (jnp.minimum(i, -(-rows // WIDE) - 1), 0)),
                resident((8, n)),
            ],
        ),
        out_shape=[(pltpu.VMEM if mine else pltpu.HBM)((rows, n), BF16), jax.ShapeDtypeStruct((8, n), F32)],
        compiler_params=params(12),
        cost_estimate=cost(live * h * h, live * h * 4),
        name="weight_share",
    )(at, held(mixed), held(low), bias, *after)


def layer(at, part, adjacency, same, last, inverse, cotangent, pieces, numbers, weight, planes):
    live, h = part.shape
    nodes = cotangent.shape[0]
    tiles = live // TILE
    below = adjacency.shape[0] // BOUND - 1

    def row(i, s):
        return (jnp.minimum(i, tiles - 1), 0)

    return pl.pallas_call(
        functools.partial(layer_kernel, tiles=tiles, numbers=numbers, planes=planes),
        grid_spec=pltpu.PrefetchScalarGridSpec(
            num_scalar_prefetch=1,
            grid=(tiles + 1,),
            in_specs=[
                pl.BlockSpec((TILE, h), row),
                pl.BlockSpec((BOUND, TILE), lambda i, s: (below - 1, jnp.minimum(i, tiles - 1))),
                pl.BlockSpec((BOUND, TILE), lambda i, s: (below, jnp.minimum(i, tiles - 1))),
                pl.BlockSpec((BOUND, live), lambda i, s: (below, 0), pipeline_mode=pl.Buffered(1)),
                resident(same.shape),
                resident(last.shape),
                pl.BlockSpec((TILE, 1), row),
                pl.BlockSpec((TILE, h), row),
            ]
            + [ANY] * len(pieces)
            + [WHOLE],
            out_specs=[
                pl.BlockSpec((TILE, h), lambda i, s: (i, 0)),
                WHOLE,
                WHOLE,
                WHOLE,
                resident((8, h)),
                resident((BOUND, h)),
                WHOLE,
            ],
            scratch_shapes=[
                pltpu.VMEM((8, h), F32),
                pltpu.SemaphoreType.DMA((len(pieces), planes)),
            ],
        ),
        out_shape=[
            jax.ShapeDtypeStruct((nodes, h), F32),
            pltpu.VMEM((live, h), BF16),
            pltpu.VMEM((live, h), BF16),
            pltpu.VMEM((live, h), BF16),
            jax.ShapeDtypeStruct((8, h), F32),
            pltpu.HBM((BOUND, h), BF16),
            pltpu.VMEM(weight.shape, BF16),
        ],
        input_output_aliases={9 + len(pieces): 6},
        compiler_params=params(16),
        cost_estimate=cost(3 * live * h * h, live * h * 12),
        name="layer",
    )(at, far(part), far(adjacency), far(adjacency), far(adjacency), same, last, inverse, far(cotangent), *pieces, held(weight))


def halves(at_ref, value, rows):
    parts = [value[k * rows : (k + 1) * rows] for k in range(4)]
    even, odd = jnp.concatenate([parts[0], parts[2]]), jnp.concatenate([parts[1], parts[3]])
    first = at_ref[4] == 0
    return jnp.where(first, even, odd), jnp.where(first, odd, even)


def spare_rows(row, n):
    count = -(-row.shape[1] // n)
    row = jnp.concatenate([row, jnp.zeros((1, count * n - row.shape[1]), F32)], axis=1) if count * n > row.shape[1] else row
    at = lax.broadcasted_iota(jnp.int32, (SPARE, n), 0)
    rows = jnp.zeros((SPARE, n), F32)
    for k in range(count):
        rows = jnp.where(at == k, row[:, k * n : (k + 1) * n], rows)
    return rows.astype(BF16)


def from_spare(rows, total):
    n = rows.shape[1]
    return jnp.concatenate([rows[k : k + 1, :] for k in range(-(-total // n))], axis=1)[:, :total].astype(F32)


def share_kernel(at_ref, kept_ref, came_ref, cb_ref, gb_ref, a_own, a_sent, b_own, b_sent, gb_out, *, rows):
    t = pl.program_id(0)
    last = pl.num_programs(0) - 1
    n = a_own.shape[1]
    groups = WIDE // (4 * rows)

    @pl.when(t < last)
    def _():
        part = kept_ref[...].astype(F32) + came_ref[...].astype(F32)
        for g in range(groups):
            value = part[g * 4 * rows : (g + 1) * 4 * rows].astype(BF16)
            mine, other = halves(at_ref, value[:, :n], rows)
            at = slice(g * 2 * rows, (g + 1) * 2 * rows)
            a_own[at, :] = mine
            a_sent[at, :] = other
            here = (t * groups + g) % 2 == at_ref[2]
            at = slice(g // 2 * 4 * rows, (g // 2 + 1) * 4 * rows)

            @pl.when(here)
            def _():
                b_own[at, :] = value[:, n:]

            @pl.when(jnp.logical_not(here))
            def _():
                b_sent[at, :] = value[:, n:]

    @pl.when(t == last)
    def _():
        total = gb_ref[0:1, :] + cb_ref[0:1, :].astype(F32)
        gb_out[...] = jnp.broadcast_to(total, gb_out.shape)
        a_sent[:SPARE, :] = spare_rows(total, n)
        b_sent[:SPARE, :] = jnp.zeros((SPARE, b_sent.shape[1]), BF16)


def share_rows(at, kept, came, bias, rows):
    h, n = kept.shape
    n_a = n * FIRST // 8
    n_b = n - n_a
    blocks = h // WIDE
    b_rows = WIDE // 2

    def tile(t):
        return jnp.minimum(t, blocks - 1)

    def plane(t, s):
        return (tile(t), 0)

    return pl.pallas_call(
        functools.partial(share_kernel, rows=rows),
        grid_spec=pltpu.PrefetchScalarGridSpec(
            num_scalar_prefetch=1,
            grid=(blocks + 1,),
            in_specs=[
                pl.BlockSpec((WIDE, n), lambda t, s: (tile(t), 0)),
                pl.BlockSpec((WIDE, n), lambda t, s: (tile(t), 0)),
                pl.BlockSpec((SPARE, n), lambda t, s: (h // SPARE, 0)),
                resident((8, n)),
            ],
            out_specs=[
                pl.BlockSpec((WIDE // 2, n_a), lambda t, s: (tile(t), 0)),
                pl.BlockSpec((WIDE // 2, n_a), lambda t, s: (t, 0)),
                pl.BlockSpec((b_rows, n_b), plane),
                pl.BlockSpec((b_rows, n_b), lambda t, s: (t, 0)),
                resident((8, n)),
            ],
        ),
        out_shape=[
            pltpu.HBM((h // 2, n_a), BF16),
            pltpu.HBM((h // 2 + SPARE, n_a), BF16),
            pltpu.HBM((h // 2, n_b), BF16),
            pltpu.HBM((h // 2 + SPARE, n_b), BF16),
            jax.ShapeDtypeStruct((8, n), F32),
        ],
        compiler_params=params(10),
        cost_estimate=cost(0, h * n * 8),
        name="share",
    )(at, kept, came, came, bias)


def fold_kernel(at_ref, a_ref, a_came, b_ref, b_came, gb_ref, _, a_own, a_sent, b_own, b_sent, gb_out, *, rows):
    lo, two = at_ref[2], 2 * rows
    n = a_ref.shape[1]
    planes = a_ref.shape[0] // (2 * two)
    for z in range(planes):
        out = slice(z * two, (z + 1) * two)
        near = pl.ds(pl.multiple_of((2 * z + lo) * two, two), two)
        far = pl.ds(pl.multiple_of((2 * z + 1 - lo) * two, two), two)
        a_own[out, :] = a_ref[near, :].astype(F32) + a_came[near, :].astype(F32)
        a_sent[out, :] = (a_ref[far, :].astype(F32) + a_came[far, :].astype(F32)).astype(BF16)
        at = slice(z * 2 * two, (z + 1) * 2 * two)
        mine, other = halves(at_ref, b_ref[at, :].astype(F32) + b_came[at, :].astype(F32), rows)
        b_own[out, :] = mine
        b_sent[out, :] = other.astype(BF16)
    total = gb_ref[0:1, :] + from_spare(a_came[a_ref.shape[0] :, :], gb_ref.shape[1])
    gb_out[...] = jnp.broadcast_to(total, gb_out.shape)
    a_sent[planes * two :, :] = spare_rows(total, n)


def fold(at, a_own, a_came, b_own, b_came, bias, rows, after):
    count, n_a, n_b = b_own.shape[0] // 2, a_own.shape[1], b_own.shape[1]
    return pl.pallas_call(
        functools.partial(fold_kernel, rows=rows),
        in_specs=[SMEM] + [WHOLE] * 5 + [ANY],
        out_specs=[WHOLE] * 5,
        out_shape=[
            jax.ShapeDtypeStruct((count, n_a), F32),
            jax.ShapeDtypeStruct((count + SPARE, n_a), BF16),
            jax.ShapeDtypeStruct((count, n_b), F32),
            jax.ShapeDtypeStruct((count, n_b), BF16),
            jax.ShapeDtypeStruct(bias.shape, F32),
        ],
        compiler_params=params(22),
        cost_estimate=cost(0, b_own.size * 9),
        name="fold",
    )(at, far(a_own), a_came, far(b_own), b_came, bias, after)


def part_kernel(at_ref, a_ref, a_came, b_ref, b_came, gb_ref, *refs, rows, planes):
    gb_out, own, *sent = refs[-1 - planes :]
    two = 2 * rows
    n = a_ref.shape[1]
    total = gb_ref[0:1, :] + from_spare(a_came[a_ref.shape[0] :, :], gb_ref.shape[1])
    gb_out[...] = jnp.broadcast_to(total, gb_out.shape)
    for k in range(planes):
        at = pl.ds(pl.multiple_of(lax.rem(at_ref[3] + k, planes) * two, two), two)
        out = own if k == 0 else sent[k - 1]
        out[:two, :n] = (a_ref[at, :] + a_came[at, :].astype(F32)).astype(out.dtype)
        out[:two, n:] = (b_ref[at, :] + b_came[at, :].astype(F32)).astype(out.dtype)
        if k:
            out[two:, :] = jnp.broadcast_to(total, (SPARE, total.shape[1])).astype(BF16)


def part_planes(at, a_own, a_came, b_own, b_came, bias, rows, planes, after):
    n = a_own.shape[1] + b_own.shape[1]
    return pl.pallas_call(
        functools.partial(part_kernel, rows=rows, planes=planes),
        in_specs=[SMEM] + [WHOLE] * 5 + [ANY] * len(after),
        out_specs=[WHOLE] * (1 + planes),
        out_shape=[jax.ShapeDtypeStruct(bias.shape, F32), jax.ShapeDtypeStruct((2 * rows, n), F32)]
        + [jax.ShapeDtypeStruct((2 * rows + SPARE, n), BF16)] * (planes - 1),
        compiler_params=params(14),
        cost_estimate=cost(0, a_own.size * 18),
        name="part_planes",
    )(at, a_own, a_came, b_own, b_came, bias, *after)


def finish_kernel(at_ref, gb_ref, own, *refs, rows):
    came, mine_ref, other_ref = refs[:-3], refs[-2], refs[-1]
    total, bias = own[...], gb_ref[0:1, :]
    for ref in came:
        total = total + ref[: 2 * rows, :].astype(F32)
        bias = bias + ref[2 * rows : 2 * rows + 1, :].astype(F32)
    first = at_ref[1] == 0
    low, high = total[:rows], total[rows:]
    bias = jnp.broadcast_to(bias, (8, bias.shape[1]))
    mine_ref[:rows, :], other_ref[:rows, :] = jnp.where(first, low, high), jnp.where(first, high, low)
    mine_ref[rows:, :], other_ref[rows:, :] = bias, bias


def finish(at, bias, own, came, rows, after):
    shape = jax.ShapeDtypeStruct((rows + 8, own.shape[1]), F32)
    return pl.pallas_call(
        functools.partial(finish_kernel, rows=rows),
        in_specs=[SMEM] + [WHOLE] * (2 + len(came)) + [ANY],
        out_specs=[WHOLE] * 2,
        out_shape=[shape] * 2,
        compiler_params=params(10),
        cost_estimate=cost(0, own.size * 8),
        name="finish",
    )(at, bias, own, *came, after)


def scatter_bound_kernel(c_ref, g_ref, *refs, count):
    *outs, part, sem = refs[len(refs) - 2 - count :]
    i = pl.program_id(0)
    part[i] = dot(c_ref[...], g_ref[...], 1, 0).astype(BF16)
    copies = [pltpu.make_async_copy(part.at[k], out, sem.at[k]) for k, out in enumerate(outs)]
    for k, copy in enumerate(copies):

        @pl.when(i == k)
        def _():
            copy.start()

    @pl.when(i == len(outs) - 1)
    def _():
        for copy in copies:
            copy.wait()


def scatter_bound(adjacency, grads, after):
    live, h = grads.shape
    blocks = (adjacency.shape[0] - live) // BOUND - 1
    return pl.pallas_call(
        functools.partial(scatter_bound_kernel, count=blocks),
        grid=(blocks,),
        in_specs=[pl.BlockSpec((BOUND, live), lambda i: (i + live // BOUND, 0)), resident((live, h))] + [ANY] * len(after),
        out_specs=[ANY] * blocks,
        out_shape=[pltpu.HBM((BOUND, h), BF16)] * blocks,
        scratch_shapes=[pltpu.VMEM((blocks, BOUND, h), BF16), pltpu.SemaphoreType.DMA((blocks,))],
        compiler_params=params(22),
        cost_estimate=cost(2 * blocks * BOUND * live * h, live * h * 4),
        name="scatter_bound",
    )(far(adjacency), grads, *after)


def grad_rows_kernel(c_ref, g_ref, *refs, low, tiles):
    o_ref, lead_ref, w, sem = refs[-4:]
    i = pl.program_id(0)
    copy = pltpu.make_async_copy(refs[0].at[:, pl.ds(0, w.shape[1])], w, sem)

    @pl.when(i == 0)
    def _():
        copy.start()

    @pl.when(low + i < tiles)
    def _():
        total = dot(c_ref[...], g_ref[...], 1, 0)

        @pl.when(i == 0)
        def _():
            lead_ref[...] = total if low == 0 else jnp.zeros_like(lead_ref)
            copy.wait()

        @pl.when(low + i > 0)
        def _():
            o_ref[...] = dot(total.astype(BF16), w[...], 1, 1)

    @pl.when(low + i == tiles)
    def _():
        o_ref[...] = jnp.zeros_like(o_ref)


def grad_rows(adjacency, grads, weight, nodes, low, high, before, after):
    live, h = grads.shape
    tiles = live // TILE
    extra = [] if before is None else [before]
    outs = [jax.ShapeDtypeStruct((nodes, h), F32), TOKEN if low else jax.ShapeDtypeStruct((TILE, h), F32)]
    out_specs = [pl.BlockSpec((TILE, h), lambda i: (low + i, 0)), resident((8, 128) if low else (TILE, h))]
    return pl.pallas_call(
        functools.partial(grad_rows_kernel, low=low, tiles=tiles),
        grid=(high - low,),
        in_specs=[
            pl.BlockSpec((TILE, live), lambda i: (jnp.minimum(low + i, tiles - 1), 0)),
            resident((live, h)),
            ANY,
        ]
        + [ANY] * (len(extra) + len(after)),
        out_specs=out_specs,
        scratch_shapes=[pltpu.VMEM((h, h), BF16), pltpu.SemaphoreType.DMA],
        out_shape=outs,
        input_output_aliases={3: 0} if extra else {},
        compiler_params=params(30),
        cost_estimate=cost((2 * live + 2 * h) * (high - low) * TILE * h, live * h * 8),
        name="grad_rows",
    )(far(adjacency), grads, far(weight), *extra, *after)


def back_kernel(a_ref, b_ref, c_ref, d_ref, _, o_ref, p_ref):
    o_ref[...] = (a_ref[...].astype(F32) + b_ref[...].astype(F32)).astype(BF16)
    p_ref[...] = (c_ref[...].astype(F32) + d_ref[...].astype(F32)).astype(BF16)


def back(a, b, c, d, after):
    block = pl.BlockSpec((64, a.shape[1]), lambda i: (i, 0))
    return pl.pallas_call(
        back_kernel,
        grid=(a.shape[0] // 64,),
        in_specs=[block] * 4 + [ANY],
        out_specs=[block] * 2,
        out_shape=[jax.ShapeDtypeStruct(a.shape, BF16)] * 2,
        compiler_params=params(10),
        cost_estimate=cost(0, a.size * 12),
        name="back",
    )(far(a), b, far(c), d, after)


def grad_lead_kernel(lead_ref, *refs):
    came, (w_ref, _, o_ref, token_ref, total) = refs[:3], refs[3:]

    @pl.when(pl.program_id(0) == 0)
    def _():
        value = lead_ref[...]
        for ref in came:
            value = value + ref[...].astype(F32)
        total[...] = value.astype(BF16)
        token_ref[...] = jnp.zeros_like(token_ref)

    o_ref[...] = dot(total[...], w_ref[...], 1, 1)


def grad_lead(lead, came, weight, grads):
    rows, h = lead.shape
    return pl.pallas_call(
        grad_lead_kernel,
        grid=(4,),
        in_specs=[resident((rows, h))] * 4 + [pl.BlockSpec((h // 4, h), lambda i: (i, 0)), ANY],
        out_specs=[pl.BlockSpec((rows, h // 4), lambda i: (0, i)), resident((8, 128))],
        out_shape=[jax.ShapeDtypeStruct(grads.shape, F32), TOKEN],
        scratch_shapes=[pltpu.VMEM((rows, h), BF16)],
        input_output_aliases={5: 0},
        compiler_params=params(20),
        cost_estimate=cost(2 * rows * h * h, h * h * 2),
        name="grad_lead",
    )(lead, *came, weight, grads)


def body(features, weight, bias, neighbours, degrees, cluster_sizes, cotangent):
    axes = ("blk", "wa")
    n_blk, n_wa = lax.axis_size("blk"), lax.axis_size("wa")
    devices, n_hi = n_blk * n_wa, n_blk // 4
    blk, wa = lax.axis_index("blk"), lax.axis_index("wa")
    core, lo, hi = blk % 2, (blk // 2) % 2, blk // 4
    nodes, h = features.shape
    share, n = h // devices, h // 2
    live = min(nodes, -(-(-(-CMAX // n_wa)) // TILE) * TILE)

    def permute(value, target):
        pairs = [(b * n_wa + w, target(b, w)) for b in range(n_blk) for w in range(n_wa)]
        return lax.ppermute(value, axes, [(s, b * n_wa + w) for s, (b, w) in pairs])

    def swap_wa(value):
        return permute(value, lambda b, w: (b, 1 - w))

    def swap_core(value):
        return permute(value, lambda b, w: (b ^ 1, w))

    def swap_outer(value, parity=None):
        pairs = [(b, (b + (1 if b % 2 else -1)) % n_blk) for b in range(n_blk)]
        chosen = [(b, t) for b, t in pairs if parity is None or (b if b % 2 else t) // 2 % 2 == parity]
        return lax.ppermute(value, axes, [(b * n_wa + w, t * n_wa + w) for b, t in chosen for w in range(n_wa)])

    def swap_lo(value):
        return permute(value, lambda b, w: (b ^ 2, w))

    def rotate_hi(value, k):
        return permute(value, lambda b, w: ((b + 4 * k) % n_blk, w))

    leading = features[:BOUND]
    partner = swap_wa(leading)
    row_same = swap_outer(leading, 0)

    sheet = jnp.concatenate([weight, jnp.broadcast_to(bias[:, None], (share, 128))], axis=1)
    planes = [rotate_hi(sheet, k) for k in range(1, n_hi)]

    live_count = (cluster_sizes[0] - wa + n_wa - 1) // n_wa
    table = neighbours[:, :live]
    beyond = table - nodes
    segment, within = beyond // (n_wa * BOUND), beyond % (n_wa * BOUND)
    same = within // BOUND == wa
    row = within % BOUND
    side = jnp.where(same, 0, BOUND) + row
    inner = (segment == 2) == (core == 0)
    away = jnp.where(inner, live + BOUND, live + BOUND + n_wa * BOUND) + side
    home = jnp.where(same, row, live + row)
    index = jnp.where(table < nodes, table, jnp.where(segment == 0, home, away))
    valid = jnp.arange(FANOUT, dtype=jnp.int32)[:, None] < degrees[None, :live]
    index = jnp.where(valid, index, -1)
    inverse = (1.0 / (degrees[:live].astype(F32) + 1.0))[:, None]
    at = jnp.stack([live_count, core, lo, hi, wa]).astype(jnp.int32)

    adjacency = counts(index, (live + (1 + 2 * n_wa) * BOUND) // TILE, [inverse, at])
    partner, late_leading, *planes = tie([partner, leading, *planes], [far(adjacency)])
    sheet = jnp.concatenate([sheet, *planes])
    half_sheet, row_sheet = swap_wa(sheet), swap_lo(sheet)
    inner_same, inner_other = swap_core(late_leading), swap_core(partner)
    plane_same = swap_outer(late_leading, 1)
    part = gather(adjacency, features, (partner, inner_same, inner_other), live, [])
    half_sheet, row_same, plane_same = tie([half_sheet, row_same, plane_same], [far(part)])
    outer_same = jnp.where((blk // 2 % 2 == 0) == (core == 1), row_same, plane_same)
    outer_other = swap_wa(outer_same)
    cut = n_hi * 3 // 4
    row_tail, outer_other = tie([row_sheet[cut * share :], outer_other], [])
    late = list(tie([swap_lo(half_sheet[: cut * share]), swap_wa(row_tail)], []))
    pieces = [sheet, half_sheet, row_sheet]
    pieces = pieces + [swap_core(value) for value in pieces]
    matrix = place(at, pieces, [(k, 0) for k in (0, 1, 2, 4, 5, 6)], n_hi)
    output, grads, mixed, low, bias_sum, outer_other_g, matrix = layer(
        at,
        part,
        adjacency,
        outer_same,
        outer_other,
        inverse,
        cotangent,
        late + [swap_core(value) for value in late],
        [(3, 0), (3, cut), (7, 0), (7, cut)],
        matrix,
        n_hi,
    )
    sent, token = weight_share(at, mixed, low, bias_sum, False, [])
    came = swap_core(sent)
    kept, bias_sum = weight_share(at, mixed, low, bias_sum, True, [token])

    a, a_sent, b, b_sent, bias_sum = share_rows(at, kept, came, bias_sum, share)
    a_came, b_came = swap_wa(a_sent), swap_lo(b_sent)

    outer_came = swap_wa(outer_other_g)
    own_bound, inner_same_g, inner_other_g, outer_same_g = scatter_bound(adjacency, grads, [bias_sum])
    own_came, inner_came = swap_core(inner_other_g), swap_core(inner_same_g)
    split, tiles = live // TILE // 2, -(-nodes // TILE)
    grad_features, lead = grad_rows(adjacency, grads, matrix, nodes, 0, split, None, [far(own_bound)])
    outer_back, own_back = back(outer_same_g, outer_came, own_bound, own_came, lead)
    outer_back = swap_outer(outer_back)
    a, a_sent, b, b_sent, bias_sum = fold(at, a, a_came, b, b_came, bias_sum, share, own_back)
    a_came, b_came = swap_lo(a_sent), swap_wa(b_sent)
    grad_features, token = grad_rows(
        adjacency, grads, matrix, nodes, split, tiles, grad_features, [bias_sum]
    )
    bias_sum, own, *rest = part_planes(
        at, a, a_came, b, b_came, bias_sum, share, n_hi, [token]
    )
    (own_back,) = tie([own_back], [own])
    returned = (inner_came, outer_back, swap_wa(own_back))
    rest = [rotate_hi(value, k + 1) for k, value in enumerate(rest)]
    grad_features, token = grad_lead(lead, returned, matrix, grad_features)
    mine, other = finish(at, bias_sum, own, rest, share, token)
    other = swap_core(other)
    pair = jnp.where(core == 0, jnp.concatenate([mine, other], axis=1), jnp.concatenate([other, mine], axis=1))
    grad_weight = pair[:share]
    grad_bias = lax.dynamic_slice_in_dim(pair[share], (blk * n_wa + wa) * share, share)
    return (output, grad_features, grad_weight, grad_bias)


def solution(mesh):
    return jax.shard_map(
        body,
        mesh=mesh,
        in_specs=(
            P(("blk", "wa"), None),
            P(("blk", "wa"), None),
            P(("blk", "wa")),
            P(None, ("blk", "wa")),
            P(("blk", "wa")),
            P("blk"),
            P(("blk", "wa"), None),
        ),
        out_specs=(
            P(("blk", "wa"), None),
            P(("blk", "wa"), None),
            P(("blk", "wa"), None),
            P(("blk", "wa")),
        ),
        check_vma=False,
    )
```

```python
import functools
import math

import jax
import jax.numpy as jnp
from jax import lax
from jax.experimental import pallas as pl
from jax.experimental.pallas import tpu as pltpu
from jax.sharding import PartitionSpec as P

FANOUT = 16
BOUND = 256
CMAX = 3016
TILE = 256
WIDE = 512
F32 = jnp.float32
BF16 = jnp.bfloat16
MIB = 1024 * 1024
GELU_A = math.sqrt(2 / math.pi)
GELU_B = 0.044715


ANY = pl.BlockSpec(memory_space=pl.ANY)
SMEM = pl.BlockSpec(memory_space=pltpu.SMEM)
WHOLE = pl.BlockSpec(memory_space=pltpu.VMEM)
SPARE = 16
FIRST = 4
TOKEN = jax.ShapeDtypeStruct((8, 128), F32)


def params(mib):
    return pltpu.CompilerParams(vmem_limit_bytes=mib * MIB)


def held(value):
    return pltpu.with_memory_space_constraint(value, pltpu.VMEM)


def far(value):
    return pltpu.with_memory_space_constraint(value, pltpu.HBM)


def tie_kernel(*refs):
    pass


def tie(values, after):
    n = len(values)
    return pl.pallas_call(
        tie_kernel,
        in_specs=[ANY] * (n + len(after)),
        out_specs=[ANY] * n,
        out_shape=[jax.ShapeDtypeStruct(v.shape, v.dtype) for v in values],
        input_output_aliases={k: k for k in range(n)},
        compiler_params=params(4),
        name="tie",
    )(*values, *after)


def resident(shape):
    return pl.BlockSpec(shape, lambda *_: (0,) * len(shape), pipeline_mode=pl.Buffered(1))


def cost(flops, nbytes):
    return pl.CostEstimate(flops=int(flops) // 16, bytes_accessed=int(nbytes) // 16, transcendentals=0)


def dot(a, b, ca, cb):
    return lax.dot_general(a, b, (((ca,), (cb,)), ((), ())), preferred_element_type=F32)


def small(value):
    return value.astype(F32).astype(BF16)


def counts_kernel(index_ref, *refs):
    out_ref = refs[-1]
    base = pl.program_id(0) * TILE
    rows = small(lax.broadcasted_iota(jnp.int32, (TILE, 128), 0))
    lanes = lax.broadcasted_iota(jnp.int32, (FANOUT, 128), 1)
    zero, one, two = (jnp.array(v, BF16) for v in (0, 1, 2))
    for c in range(0, out_ref.shape[1], 128):
        entry = small(jnp.clip(index_ref[:, c : c + 128] - base, -1, TILE))
        own = small(jnp.clip(lanes + (c - base), -1, TILE))
        total = jnp.where(own[0:1, :] == rows, two, zero)
        for s in range(FANOUT):
            total = total + jnp.where(entry[s : s + 1, :] == rows, one, zero)
        out_ref[:, c : c + 128] = total


def counts(index, tiles, after):
    n = index.shape[1]
    return pl.pallas_call(
        counts_kernel,
        grid=(tiles,),
        in_specs=[pl.BlockSpec((FANOUT, n), lambda i: (0, 0))] + [ANY] * len(after),
        out_specs=pl.BlockSpec((TILE, n), lambda i: (i, 0)),
        out_shape=pltpu.HBM((tiles * TILE, n), BF16),
        compiler_params=params(12),
        cost_estimate=cost(0, tiles * TILE * n * 16),
        name="counts",
    )(index, *after)


def gather_kernel(c_ref, t_ref, *refs, count):
    o_ref = refs[-1]
    live = t_ref.shape[0]
    total = dot(c_ref[:live, :], t_ref[...], 0, 0)
    for k, ref in enumerate(refs[:count]):
        at = live + k * BOUND
        total = total + dot(c_ref[at : at + BOUND, :], ref[...], 0, 0)
    o_ref[...] = total


def gather(adjacency, features, blocks, live, after):
    h = features.shape[1]
    rows = live + len(blocks) * BOUND
    return pl.pallas_call(
        functools.partial(gather_kernel, count=len(blocks)),
        grid=(live // TILE,),
        in_specs=[pl.BlockSpec((rows, TILE), lambda i: (0, i)), resident((live, h))]
        + [resident((BOUND, h))] * len(blocks)
        + [ANY] * len(after),
        out_specs=pl.BlockSpec((TILE, h), lambda i: (i, 0)),
        out_shape=pltpu.HBM((live, h), F32),
        compiler_params=params(26),
        cost_estimate=cost(2 * live * rows * h, live * h * 6),
        name="gather",
    )(far(adjacency), far(features), *blocks, *after)


def fetch(pieces, numbers, planes, target, sem, at_ref):
    core, lo, hi, wa = (at_ref[j] for j in range(1, 5))
    rows = target.shape[0] // (8 * planes)
    copies = []
    for m, ((n, first), piece) in enumerate(zip(numbers, pieces)):
        for k in range(piece.shape[0] // rows):
            chip = lax.rem(hi - first - k + planes, planes) * 2 + (1 - lo if n // 2 % 2 else lo)
            owner = (chip * 2 + (1 - core if n // 4 else core)) * 2 + (1 - wa if n % 2 else wa)
            copies.append(
                pltpu.make_async_copy(
                    piece.at[pl.ds(k * rows, rows), :],
                    target.at[pl.ds(pl.multiple_of(owner * rows, rows), rows), :],
                    sem.at[m, k],
                )
            )
    return copies


def place_kernel(at_ref, *refs, numbers, planes):
    target, sem = refs[-2:]
    copies = fetch(refs[: len(numbers)], numbers, planes, target, sem, at_ref)
    for copy in copies:
        copy.start()
    for copy in copies:
        copy.wait()


def place(at, pieces, numbers, planes):
    h, n = 8 * pieces[0].shape[0], pieces[0].shape[1]
    return pl.pallas_call(
        functools.partial(place_kernel, numbers=numbers, planes=planes),
        in_specs=[SMEM] + [ANY] * len(pieces),
        out_specs=WHOLE,
        out_shape=pltpu.VMEM((h, n), BF16),
        scratch_shapes=[pltpu.SemaphoreType.DMA((len(pieces), planes))],
        compiler_params=params(4),
        cost_estimate=cost(0, h * n),
        name="place",
    )(at, *pieces)


def layer_kernel(at_ref, part_ref, c_ref, d_ref, cl_ref, same_ref, last_ref, inv_ref, ct_ref, *refs, tiles, numbers, planes):
    count = len(numbers)
    pieces, refs = refs[:count], refs[count + 1 :]
    o_ref, agl_ref, m_all, gl_all, gb, far_low, far_high, w, b, sem = refs
    i = pl.program_id(0)
    h = part_ref.shape[1]
    copies = fetch(pieces, numbers, planes, w, sem, at_ref)

    @pl.when(i == 0)
    def _():
        for copy in copies:
            copy.start()
        gb[...] = jnp.zeros_like(gb)

    @pl.when(i < tiles)
    def _():
        total = part_ref[...] + dot(c_ref[...], same_ref[...], 0, 0) + dot(d_ref[...], last_ref[...], 0, 0)
        m_all[pl.ds(pl.multiple_of(i * TILE, TILE), TILE), :] = (total * inv_ref[...]).astype(BF16)

    @pl.when(i == 0)
    def _():
        for copy in copies:
            copy.wait()
        b[...] = w[:, h:].astype(F32).T[:8, :]

    @pl.when(i < tiles)
    def _():
        base = pl.multiple_of(i * TILE, TILE)
        rows = pl.ds(base, TILE)
        mixed = m_all[rows, :]
        live = base + lax.broadcasted_iota(jnp.int32, (TILE, 256), 0) < at_ref[0]
        inverse = inv_ref[...]
        for j in range(0, h, 256):
            at = slice(j, j + 256)
            v = dot(mixed, w[:, at], 1, 0) + b[0:1, at]
            square = v * v
            half = jnp.where(live, 0.5 + 0.5 * jnp.tanh(v * (GELU_A + (GELU_A * GELU_B) * square)), 0.0)
            o_ref[:, at] = v * half
            slope = half + (half - half * half) * (v * (2 * GELU_A + (6 * GELU_A * GELU_B) * square))
            grad = ct_ref[:, at].astype(F32) * slope
            gl_all[rows, at] = grad.astype(BF16)
            agl_ref[rows, at] = (grad * inverse).astype(BF16)
            gb[:, at] += jnp.sum(grad.reshape(TILE // 8, 8, 256), axis=0)

    @pl.when(i == tiles)
    def _():
        o_ref[...] = jnp.zeros_like(o_ref)
        away = dot(cl_ref[...], agl_ref[...], 1, 0).astype(BF16)
        far_low[...] = away[: BOUND // 2]
        far_high[...] = away[BOUND // 2 :]


def weight_kernel(at_ref, m_all, gl_all, gb, *refs, mine):
    out_ref, gb_ref = refs[-2:]
    i = pl.program_id(0)
    blocks = m_all.shape[1] // WIDE
    n = out_ref.shape[1]
    core = at_ref[1] if mine else 1 - at_ref[1]
    columns = pl.ds(pl.multiple_of(core * n, n), n)

    @pl.when(i < blocks)
    def _():
        at = pl.ds(pl.multiple_of(i * WIDE, WIDE), WIDE)
        out_ref[...] = dot(m_all[:, at], gl_all[:, columns], 0, 0).astype(BF16)

    @pl.when(i == blocks)
    def _():
        total = jnp.sum(gb[:, columns], axis=0, keepdims=True)
        gb_ref[...] = jnp.broadcast_to(total, gb_ref.shape)
        if not mine:
            out_ref[:SPARE, :] = jnp.broadcast_to(total, (SPARE, n)).astype(BF16)


def weight_share(at, mixed, low, bias, mine, after):
    live, h = mixed.shape
    n, blocks = h // 2, h // WIDE
    rows = h if mine else h + SPARE
    return pl.pallas_call(
        functools.partial(weight_kernel, mine=mine),
        grid_spec=pltpu.PrefetchScalarGridSpec(
            num_scalar_prefetch=1,
            grid=(blocks + 1,),
            in_specs=[WHOLE, WHOLE, resident((8, h))] + [ANY] * len(after),
            out_specs=[
                pl.BlockSpec((WIDE, n), lambda i, s: (jnp.minimum(i, -(-rows // WIDE) - 1), 0)),
                resident((8, n)),
            ],
        ),
        out_shape=[(pltpu.VMEM if mine else pltpu.HBM)((rows, n), BF16), jax.ShapeDtypeStruct((8, n), F32)],
        compiler_params=params(12),
        cost_estimate=cost(live * h * h, live * h * 4),
        name="weight_share",
    )(at, held(mixed), held(low), bias, *after)


def layer(at, part, adjacency, same, last, inverse, cotangent, pieces, numbers, weight, planes):
    live, h = part.shape
    nodes = cotangent.shape[0]
    tiles = live // TILE
    below = adjacency.shape[0] // BOUND - 1

    def row(i, s):
        return (jnp.minimum(i, tiles - 1), 0)

    return pl.pallas_call(
        functools.partial(layer_kernel, tiles=tiles, numbers=numbers, planes=planes),
        grid_spec=pltpu.PrefetchScalarGridSpec(
            num_scalar_prefetch=1,
            grid=(tiles + 1,),
            in_specs=[
                pl.BlockSpec((TILE, h), row),
                pl.BlockSpec((BOUND, TILE), lambda i, s: (below - 1, jnp.minimum(i, tiles - 1))),
                pl.BlockSpec((BOUND, TILE), lambda i, s: (below, jnp.minimum(i, tiles - 1))),
                pl.BlockSpec((BOUND, live), lambda i, s: (below, 0), pipeline_mode=pl.Buffered(1)),
                resident(same.shape),
                resident(last.shape),
                pl.BlockSpec((TILE, 1), row),
                pl.BlockSpec((TILE, h), row),
            ]
            + [ANY] * len(pieces)
            + [WHOLE],
            out_specs=[
                pl.BlockSpec((TILE, h), lambda i, s: (i, 0)),
                WHOLE,
                WHOLE,
                WHOLE,
                resident((8, h)),
                resident((BOUND // 2, h)),
                resident((BOUND // 2, h)),
                WHOLE,
            ],
            scratch_shapes=[
                pltpu.VMEM((8, h), F32),
                pltpu.SemaphoreType.DMA((len(pieces), planes)),
            ],
        ),
        out_shape=[
            jax.ShapeDtypeStruct((nodes, h), F32),
            pltpu.VMEM((live, h), BF16),
            pltpu.VMEM((live, h), BF16),
            pltpu.VMEM((live, h), BF16),
            jax.ShapeDtypeStruct((8, h), F32),
            pltpu.HBM((BOUND // 2, h), BF16),
            pltpu.HBM((BOUND // 2, h), BF16),
            pltpu.VMEM(weight.shape, BF16),
        ],
        input_output_aliases={9 + len(pieces): 7},
        compiler_params=params(16),
        cost_estimate=cost(3 * live * h * h, live * h * 12),
        name="layer",
    )(at, far(part), far(adjacency), far(adjacency), far(adjacency), same, last, inverse, far(cotangent), *pieces, held(weight))


def halves(at_ref, value, rows):
    parts = [value[k * rows : (k + 1) * rows] for k in range(4)]
    even, odd = jnp.concatenate([parts[0], parts[2]]), jnp.concatenate([parts[1], parts[3]])
    first = at_ref[4] == 0
    return jnp.where(first, even, odd), jnp.where(first, odd, even)


def spare_rows(row, n):
    count = -(-row.shape[1] // n)
    row = jnp.concatenate([row, jnp.zeros((1, count * n - row.shape[1]), F32)], axis=1) if count * n > row.shape[1] else row
    at = lax.broadcasted_iota(jnp.int32, (SPARE, n), 0)
    rows = jnp.zeros((SPARE, n), F32)
    for k in range(count):
        rows = jnp.where(at == k, row[:, k * n : (k + 1) * n], rows)
    return rows.astype(BF16)


def from_spare(rows, total):
    n = rows.shape[1]
    return jnp.concatenate([rows[k : k + 1, :] for k in range(-(-total // n))], axis=1)[:, :total].astype(F32)


def share_kernel(at_ref, kept_ref, came_ref, gb_ref, low_ref, high_ref, a_own, a_sent, b_own, b_sent, gb_out, *, rows):
    h = kept_ref.shape[0]
    n_a, n_b = a_own.shape[1], b_own.shape[1]
    for g in range(h // (4 * rows)):
        at = slice(g * 4 * rows, (g + 1) * 4 * rows)
        value = (kept_ref[at, :].astype(F32) + came_ref[at, :].astype(F32)).astype(BF16)
        mine, other = halves(at_ref, value[:, :n_a], rows)
        at = slice(g * 2 * rows, (g + 1) * 2 * rows)
        a_own[at, :] = mine
        a_sent[at, :] = other
        here = g % 2 == at_ref[2]
        at = slice(g // 2 * 4 * rows, (g // 2 + 1) * 4 * rows)

        @pl.when(here)
        def _():
            b_own[at, :] = value[:, n_a:]

        @pl.when(jnp.logical_not(here))
        def _():
            b_sent[at, :] = value[:, n_a:]

    total = gb_ref[0:1, :] + came_ref[h : h + 1, :].astype(F32)
    gb_out[...] = jnp.broadcast_to(total, gb_out.shape)
    a_sent[h // 2 :, :] = spare_rows(total, n_a)
    b_sent[h // 2 :, :] = jnp.zeros((SPARE, n_b), BF16)


def share_rows(at, kept, came, bias, rows, after):
    h, n = kept.shape
    n_a = n * FIRST // 8
    n_b = n - n_a
    return pl.pallas_call(
        functools.partial(share_kernel, rows=rows),
        in_specs=[SMEM] + [WHOLE] * 3 + [ANY] * 2,
        out_specs=[WHOLE] * 5,
        out_shape=[
            pltpu.VMEM((h // 2, n_a), BF16),
            pltpu.VMEM((h // 2 + SPARE, n_a), BF16),
            pltpu.VMEM((h // 2, n_b), BF16),
            pltpu.VMEM((h // 2 + SPARE, n_b), BF16),
            jax.ShapeDtypeStruct((8, n), F32),
        ],
        compiler_params=params(10),
        cost_estimate=cost(0, h * n * 8),
        name="share",
    )(at, kept, came, bias, *after)


def fold_kernel(at_ref, a_ref, a_came, b_ref, b_came, gb_ref, _, a_own, a_sent, b_own, b_sent, gb_out, *, rows):
    lo, two = at_ref[2], 2 * rows
    n = a_ref.shape[1]
    planes = a_ref.shape[0] // (2 * two)
    for z in range(planes):
        out = slice(z * two, (z + 1) * two)
        near = pl.ds(pl.multiple_of((2 * z + lo) * two, two), two)
        far = pl.ds(pl.multiple_of((2 * z + 1 - lo) * two, two), two)
        a_own[out, :] = a_ref[near, :].astype(F32) + a_came[near, :].astype(F32)
        a_sent[out, :] = (a_ref[far, :].astype(F32) + a_came[far, :].astype(F32)).astype(BF16)
        at = slice(z * 2 * two, (z + 1) * 2 * two)
        mine, other = halves(at_ref, b_ref[at, :].astype(F32) + b_came[at, :].astype(F32), rows)
        b_own[out, :] = mine
        b_sent[out, :] = other.astype(BF16)
    total = gb_ref[0:1, :] + from_spare(a_came[a_ref.shape[0] :, :], gb_ref.shape[1])
    gb_out[...] = jnp.broadcast_to(total, gb_out.shape)
    a_sent[planes * two :, :] = spare_rows(total, n)


def fold(at, a_own, a_came, b_own, b_came, bias, rows, after):
    count, n_a, n_b = b_own.shape[0] // 2, a_own.shape[1], b_own.shape[1]
    return pl.pallas_call(
        functools.partial(fold_kernel, rows=rows),
        in_specs=[SMEM] + [WHOLE] * 5 + [ANY],
        out_specs=[WHOLE] * 5,
        out_shape=[
            jax.ShapeDtypeStruct((count, n_a), F32),
            jax.ShapeDtypeStruct((count + SPARE, n_a), BF16),
            jax.ShapeDtypeStruct((count, n_b), F32),
            jax.ShapeDtypeStruct((count, n_b), BF16),
            jax.ShapeDtypeStruct(bias.shape, F32),
        ],
        compiler_params=params(22),
        cost_estimate=cost(0, b_own.size * 9),
        name="fold",
    )(at, a_own, a_came, b_own, b_came, bias, after)


def part_kernel(at_ref, a_ref, a_came, b_ref, b_came, gb_ref, *refs, rows, planes):
    gb_out, own, *sent = refs[-1 - planes :]
    two = 2 * rows
    n = a_ref.shape[1]
    total = gb_ref[0:1, :] + from_spare(a_came[a_ref.shape[0] :, :], gb_ref.shape[1])
    gb_out[...] = jnp.broadcast_to(total, gb_out.shape)
    for k in range(planes):
        at = pl.ds(pl.multiple_of(lax.rem(at_ref[3] + k, planes) * two, two), two)
        out = own if k == 0 else sent[k - 1]
        out[:two, :n] = (a_ref[at, :] + a_came[at, :].astype(F32)).astype(out.dtype)
        out[:two, n:] = (b_ref[at, :] + b_came[at, :].astype(F32)).astype(out.dtype)
        if k:
            out[two:, :] = jnp.broadcast_to(total, (SPARE, total.shape[1])).astype(BF16)


def part_planes(at, a_own, a_came, b_own, b_came, bias, rows, planes, after):
    n = a_own.shape[1] + b_own.shape[1]
    return pl.pallas_call(
        functools.partial(part_kernel, rows=rows, planes=planes),
        in_specs=[SMEM] + [WHOLE] * 5 + [ANY] * len(after),
        out_specs=[WHOLE] * (1 + planes),
        out_shape=[jax.ShapeDtypeStruct(bias.shape, F32), jax.ShapeDtypeStruct((2 * rows, n), F32)]
        + [jax.ShapeDtypeStruct((2 * rows + SPARE, n), BF16)] * (planes - 1),
        compiler_params=params(14),
        cost_estimate=cost(0, a_own.size * 18),
        name="part_planes",
    )(at, a_own, a_came, b_own, b_came, bias, *after)


def finish_kernel(at_ref, gb_ref, own, *refs, rows):
    came, mine_ref, other_ref = refs[:-3], refs[-2], refs[-1]
    total, bias = own[...], gb_ref[0:1, :]
    for ref in came:
        total = total + ref[: 2 * rows, :].astype(F32)
        bias = bias + ref[2 * rows : 2 * rows + 1, :].astype(F32)
    first = at_ref[1] == 0
    low, high = total[:rows], total[rows:]
    bias = jnp.broadcast_to(bias, (8, bias.shape[1]))
    mine_ref[:rows, :], other_ref[:rows, :] = jnp.where(first, low, high), jnp.where(first, high, low)
    mine_ref[rows:, :], other_ref[rows:, :] = bias, bias


def finish(at, bias, own, came, rows, after):
    shape = jax.ShapeDtypeStruct((rows + 8, own.shape[1]), F32)
    return pl.pallas_call(
        functools.partial(finish_kernel, rows=rows),
        in_specs=[SMEM] + [WHOLE] * (2 + len(came)) + [ANY],
        out_specs=[WHOLE] * 2,
        out_shape=[shape] * 2,
        compiler_params=params(10),
        cost_estimate=cost(0, own.size * 8),
        name="finish",
    )(at, bias, own, *came, after)


def scatter_bound_kernel(c_ref, g_ref, *refs, count):
    *outs, part, sem = refs[len(refs) - 2 - count :]
    i = pl.program_id(0)
    part[i] = dot(c_ref[...], g_ref[...], 1, 0).astype(BF16)
    copies = [pltpu.make_async_copy(part.at[k], out, sem.at[k]) for k, out in enumerate(outs)]
    for k, copy in enumerate(copies):

        @pl.when(i == k)
        def _():
            copy.start()

    @pl.when(i == len(outs) - 1)
    def _():
        for copy in copies:
            copy.wait()


def scatter_bound(adjacency, grads, after):
    live, h = grads.shape
    blocks = (adjacency.shape[0] - live) // BOUND - 1
    return pl.pallas_call(
        functools.partial(scatter_bound_kernel, count=blocks),
        grid=(blocks,),
        in_specs=[pl.BlockSpec((BOUND, live), lambda i: (i + live // BOUND, 0)), resident((live, h))] + [ANY] * len(after),
        out_specs=[ANY] * blocks,
        out_shape=[pltpu.HBM((BOUND, h), BF16)] * blocks,
        scratch_shapes=[pltpu.VMEM((blocks, BOUND, h), BF16), pltpu.SemaphoreType.DMA((blocks,))],
        compiler_params=params(22),
        cost_estimate=cost(2 * blocks * BOUND * live * h, live * h * 4),
        name="scatter_bound",
    )(far(adjacency), grads, *after)


def grad_rows_kernel(c_ref, g_ref, *refs, low, tiles):
    o_ref, lead_ref, w, sem = refs[-4:]
    i = pl.program_id(0)
    copy = pltpu.make_async_copy(refs[0].at[:, pl.ds(0, w.shape[1])], w, sem)

    @pl.when(i == 0)
    def _():
        copy.start()

    @pl.when(low + i < tiles)
    def _():
        total = dot(c_ref[...], g_ref[...], 1, 0)

        @pl.when(i == 0)
        def _():
            lead_ref[...] = total if low == 0 else jnp.zeros_like(lead_ref)
            copy.wait()

        @pl.when(low + i > 0)
        def _():
            o_ref[...] = dot(total.astype(BF16), w[...], 1, 1)

    @pl.when(low + i == tiles)
    def _():
        o_ref[...] = jnp.zeros_like(o_ref)


def grad_rows(adjacency, grads, weight, nodes, low, high, before, after):
    live, h = grads.shape
    tiles = live // TILE
    extra = [] if before is None else [before]
    outs = [jax.ShapeDtypeStruct((nodes, h), F32), TOKEN if low else jax.ShapeDtypeStruct((TILE, h), F32)]
    out_specs = [pl.BlockSpec((TILE, h), lambda i: (low + i, 0)), resident((8, 128) if low else (TILE, h))]
    return pl.pallas_call(
        functools.partial(grad_rows_kernel, low=low, tiles=tiles),
        grid=(high - low,),
        in_specs=[
            pl.BlockSpec((TILE, live), lambda i: (jnp.minimum(low + i, tiles - 1), 0)),
            resident((live, h)),
            ANY,
        ]
        + [ANY] * (len(extra) + len(after)),
        out_specs=out_specs,
        scratch_shapes=[pltpu.VMEM((h, h), BF16), pltpu.SemaphoreType.DMA],
        out_shape=outs,
        input_output_aliases={3: 0} if extra else {},
        compiler_params=params(30),
        cost_estimate=cost((2 * live + 2 * h) * (high - low) * TILE * h, live * h * 8),
        name="grad_rows",
    )(far(adjacency), grads, far(weight), *extra, *after)


def back_kernel(outer_ref, low_ref, own_ref, came_ref, high_ref, _, outer_back, own_back):
    i = pl.program_id(0)
    half = pl.num_programs(0) // 2
    early = (i < half).astype(F32)
    outer_back[...] = (outer_ref[...].astype(F32) + early * low_ref[...].astype(F32)).astype(BF16)
    own = own_ref[...].astype(F32) + came_ref[...].astype(F32)
    own_back[...] = (own + (1 - early) * high_ref[...].astype(F32)).astype(BF16)


def back(outer, low, own, came, high, after):
    rows, h = own.shape
    steps = 4
    half = steps // 2
    whole = pl.BlockSpec((rows // steps, h), lambda i: (i, 0))
    first = pl.BlockSpec((rows // steps, h), lambda i: (jnp.minimum(i, half - 1), 0))
    second = pl.BlockSpec((rows // steps, h), lambda i: (jnp.maximum(i - half, 0), 0))
    return pl.pallas_call(
        back_kernel,
        grid=(steps,),
        in_specs=[whole, first, whole, whole, second, ANY],
        out_specs=[whole] * 2,
        out_shape=[jax.ShapeDtypeStruct((rows, h), BF16)] * 2,
        compiler_params=params(10),
        cost_estimate=cost(0, own.size * 12),
        name="back",
    )(far(outer), low, far(own), came, high, after)


def grad_lead_kernel(lead_ref, *refs):
    came, (w_ref, _, o_ref, token_ref, total) = refs[:3], refs[3:]

    @pl.when(pl.program_id(0) == 0)
    def _():
        value = lead_ref[...]
        for ref in came:
            value = value + ref[...].astype(F32)
        total[...] = value.astype(BF16)
        token_ref[...] = jnp.zeros_like(token_ref)

    o_ref[...] = dot(total[...], w_ref[...], 1, 1)


def grad_lead(lead, came, weight, grads):
    rows, h = lead.shape
    return pl.pallas_call(
        grad_lead_kernel,
        grid=(4,),
        in_specs=[resident((rows, h))] * 4 + [pl.BlockSpec((h // 4, h), lambda i: (i, 0)), ANY],
        out_specs=[pl.BlockSpec((rows, h // 4), lambda i: (0, i)), resident((8, 128))],
        out_shape=[jax.ShapeDtypeStruct(grads.shape, F32), TOKEN],
        scratch_shapes=[pltpu.VMEM((rows, h), BF16)],
        input_output_aliases={5: 0},
        compiler_params=params(20),
        cost_estimate=cost(2 * rows * h * h, h * h * 2),
        name="grad_lead",
    )(lead, *came, weight, grads)


def body(features, weight, bias, neighbours, degrees, cluster_sizes, cotangent):
    axes = ("blk", "wa")
    n_blk, n_wa = lax.axis_size("blk"), lax.axis_size("wa")
    devices, n_hi = n_blk * n_wa, n_blk // 4
    blk, wa = lax.axis_index("blk"), lax.axis_index("wa")
    core, lo, hi = blk % 2, (blk // 2) % 2, blk // 4
    nodes, h = features.shape
    share, n = h // devices, h // 2
    live = min(nodes, -(-(-(-CMAX // n_wa)) // TILE) * TILE)

    def permute(value, target):
        pairs = [(b * n_wa + w, target(b, w)) for b in range(n_blk) for w in range(n_wa)]
        return lax.ppermute(value, axes, [(s, b * n_wa + w) for s, (b, w) in pairs])

    def swap_wa(value):
        return permute(value, lambda b, w: (b, 1 - w))

    def swap_core(value):
        return permute(value, lambda b, w: (b ^ 1, w))

    def swap_outer(value, parity=None):
        pairs = [(b, (b + (1 if b % 2 else -1)) % n_blk) for b in range(n_blk)]
        chosen = [(b, t) for b, t in pairs if parity is None or (b if b % 2 else t) // 2 % 2 == parity]
        return lax.ppermute(value, axes, [(b * n_wa + w, t * n_wa + w) for b, t in chosen for w in range(n_wa)])

    def swap_lo(value):
        return permute(value, lambda b, w: (b ^ 2, w))

    def rotate_hi(value, k):
        return permute(value, lambda b, w: ((b + 4 * k) % n_blk, w))

    leading = features[:BOUND]
    partner = swap_wa(leading)
    row_same = swap_outer(leading, 0)

    sheet = jnp.concatenate([weight, jnp.broadcast_to(bias[:, None], (share, 128))], axis=1)
    planes = [rotate_hi(sheet, k) for k in range(1, n_hi)]

    live_count = (cluster_sizes[0] - wa + n_wa - 1) // n_wa
    table = neighbours[:, :live]
    beyond = table - nodes
    segment, within = beyond // (n_wa * BOUND), beyond % (n_wa * BOUND)
    same = within // BOUND == wa
    row = within % BOUND
    side = jnp.where(same, 0, BOUND) + row
    inner = (segment == 2) == (core == 0)
    away = jnp.where(inner, live + BOUND, live + BOUND + n_wa * BOUND) + side
    home = jnp.where(same, row, live + row)
    index = jnp.where(table < nodes, table, jnp.where(segment == 0, home, away))
    valid = jnp.arange(FANOUT, dtype=jnp.int32)[:, None] < degrees[None, :live]
    index = jnp.where(valid, index, -1)
    inverse = (1.0 / (degrees[:live].astype(F32) + 1.0))[:, None]
    at = jnp.stack([live_count, core, lo, hi, wa]).astype(jnp.int32)

    adjacency = counts(index, (live + (1 + 2 * n_wa) * BOUND) // TILE, [inverse, at])
    partner, late_leading, *planes = tie([partner, leading, *planes], [far(adjacency)])
    sheet = jnp.concatenate([sheet, *planes])
    half_sheet, row_sheet = swap_wa(sheet), swap_lo(sheet)
    inner_same, inner_other = swap_core(late_leading), swap_core(partner)
    plane_same = swap_outer(late_leading, 1)
    part = gather(adjacency, features, (partner, inner_same, inner_other), live, [])
    half_sheet, row_same, plane_same = tie([half_sheet, row_same, plane_same], [far(part)])
    outer_same = jnp.where((blk // 2 % 2 == 0) == (core == 1), row_same, plane_same)
    outer_other = swap_wa(outer_same)
    cut = n_hi * 3 // 4
    row_tail, outer_other = tie([row_sheet[cut * share :], outer_other], [])
    late = list(tie([swap_lo(half_sheet[: cut * share]), swap_wa(row_tail)], []))
    pieces = [sheet, half_sheet, row_sheet]
    pieces = pieces + [swap_core(value) for value in pieces]
    matrix = place(at, pieces, [(k, 0) for k in (0, 1, 2, 4, 5, 6)], n_hi)
    output, grads, mixed, low, bias_sum, far_low, far_high, matrix = layer(
        at,
        part,
        adjacency,
        outer_same,
        outer_other,
        inverse,
        cotangent,
        late + [swap_core(value) for value in late],
        [(3, 0), (3, cut), (7, 0), (7, cut)],
        matrix,
        n_hi,
    )
    sent, token = weight_share(at, mixed, low, bias_sum, False, [])
    came = swap_core(sent)
    kept, bias_sum = weight_share(at, mixed, low, bias_sum, True, [token])

    far_low, far_high = swap_wa(far_low), swap_outer(far_high)
    a, a_sent, b, b_sent, bias_sum = share_rows(at, kept, came, bias_sum, share, [far_low, far_high])
    a_came, b_came = swap_wa(a_sent), swap_lo(b_sent)

    own_bound, inner_same_g, inner_other_g, outer_same_g = scatter_bound(adjacency, grads, [bias_sum])
    own_came, inner_came = swap_core(inner_other_g), swap_core(inner_same_g)
    split, tiles = live // TILE // 3, -(-nodes // TILE)
    grad_features, lead = grad_rows(adjacency, grads, matrix, nodes, 0, split, None, [far(own_bound)])
    outer_back, own_back = back(outer_same_g, far_low, own_bound, own_came, far_high, lead)
    outer_back = swap_outer(outer_back)
    a, a_sent, b, b_sent, bias_sum = fold(at, a, a_came, b, b_came, bias_sum, share, own_back)
    a_came, b_came = swap_lo(a_sent), swap_wa(b_sent)
    grad_features, token = grad_rows(
        adjacency, grads, matrix, nodes, split, tiles, grad_features, [bias_sum]
    )
    bias_sum, own, *rest = part_planes(
        at, a, a_came, b, b_came, bias_sum, share, n_hi, [token]
    )
    (own_back,) = tie([own_back], [own])
    returned = (inner_came, outer_back, swap_wa(own_back))
    rest = [rotate_hi(value, k + 1) for k, value in enumerate(rest)]
    grad_features, token = grad_lead(lead, returned, matrix, grad_features)
    mine, other = finish(at, bias_sum, own, rest, share, token)
    other = swap_core(other)
    first, second = jnp.where(core == 0, mine, other), jnp.where(core == 0, other, mine)
    grad_weight = jnp.concatenate([first[:share], second[:share]], axis=1)
    bias_row = jnp.concatenate([first[share], second[share]])
    grad_bias = lax.dynamic_slice_in_dim(bias_row, (blk * n_wa + wa) * share, share)
    return (output, grad_features, grad_weight, grad_bias)


def solution(mesh):
    return jax.shard_map(
        body,
        mesh=mesh,
        in_specs=(
            P(("blk", "wa"), None),
            P(("blk", "wa"), None),
            P(("blk", "wa")),
            P(None, ("blk", "wa")),
            P(("blk", "wa")),
            P("blk"),
            P(("blk", "wa"), None),
        ),
        out_specs=(
            P(("blk", "wa"), None),
            P(("blk", "wa"), None),
            P(("blk", "wa"), None),
            P(("blk", "wa")),
        ),
        check_vma=False,
    )
```

```python
import functools
import math

import jax
import jax.numpy as jnp
from jax import lax
from jax.experimental import pallas as pl
from jax.experimental.pallas import tpu as pltpu
from jax.sharding import PartitionSpec as P

FANOUT = 16
BOUND = 256
CMAX = 3016
TILE = 256
WIDE = 1024
F32 = jnp.float32
BF16 = jnp.bfloat16
MIB = 1024 * 1024
GELU_A = math.sqrt(2 / math.pi)
GELU_B = 0.044715


ANY = pl.BlockSpec(memory_space=pl.ANY)
SMEM = pl.BlockSpec(memory_space=pltpu.SMEM)
WHOLE = pl.BlockSpec(memory_space=pltpu.VMEM)
SPARE = 16
FIRST = 4
TOKEN = jax.ShapeDtypeStruct((8, 128), F32)


def params(mib):
    return pltpu.CompilerParams(vmem_limit_bytes=mib * MIB)


def held(value):
    return pltpu.with_memory_space_constraint(value, pltpu.VMEM)


def far(value):
    return pltpu.with_memory_space_constraint(value, pltpu.HBM)


def tie_kernel(*refs):
    pass


def tie(values, after):
    n = len(values)
    return pl.pallas_call(
        tie_kernel,
        in_specs=[ANY] * (n + len(after)),
        out_specs=[ANY] * n,
        out_shape=[jax.ShapeDtypeStruct(v.shape, v.dtype) for v in values],
        input_output_aliases={k: k for k in range(n)},
        compiler_params=params(4),
        name="tie",
    )(*values, *after)


def resident(shape):
    return pl.BlockSpec(shape, lambda *_: (0,) * len(shape), pipeline_mode=pl.Buffered(1))


def cost(flops, nbytes):
    return pl.CostEstimate(flops=int(flops) // 16, bytes_accessed=int(nbytes) // 16, transcendentals=0)


def dot(a, b, ca, cb):
    return lax.dot_general(a, b, (((ca,), (cb,)), ((), ())), preferred_element_type=F32)


def small(value):
    return value.astype(F32).astype(BF16)


def counts_kernel(index_ref, *refs):
    out_ref = refs[-1]
    base = pl.program_id(0) * TILE
    rows = small(lax.broadcasted_iota(jnp.int32, (TILE, 128), 0))
    lanes = lax.broadcasted_iota(jnp.int32, (FANOUT, 128), 1)
    zero, one, two = (jnp.array(v, BF16) for v in (0, 1, 2))
    for c in range(0, out_ref.shape[1], 128):
        entry = small(jnp.clip(index_ref[:, c : c + 128] - base, -1, TILE))
        own = small(jnp.clip(lanes + (c - base), -1, TILE))
        total = jnp.where(own[0:1, :] == rows, two, zero)
        for s in range(FANOUT):
            total = total + jnp.where(entry[s : s + 1, :] == rows, one, zero)
        out_ref[:, c : c + 128] = total


def counts(index, tiles, after):
    n = index.shape[1]
    return pl.pallas_call(
        counts_kernel,
        grid=(tiles,),
        in_specs=[pl.BlockSpec((FANOUT, n), lambda i: (0, 0))] + [ANY] * len(after),
        out_specs=pl.BlockSpec((TILE, n), lambda i: (i, 0)),
        out_shape=pltpu.HBM((tiles * TILE, n), BF16),
        compiler_params=params(12),
        cost_estimate=cost(0, tiles * TILE * n * 16),
        name="counts",
    )(index, *after)


def gather_kernel(c_ref, t_ref, *refs, count):
    o_ref = refs[-1]
    live = t_ref.shape[0]
    total = dot(c_ref[:live, :], t_ref[...], 0, 0)
    for k, ref in enumerate(refs[:count]):
        at = live + k * BOUND
        total = total + dot(c_ref[at : at + BOUND, :], ref[...], 0, 0)
    o_ref[...] = total


def gather(adjacency, features, blocks, live, after):
    h = features.shape[1]
    rows = live + len(blocks) * BOUND
    return pl.pallas_call(
        functools.partial(gather_kernel, count=len(blocks)),
        grid=(live // TILE,),
        in_specs=[pl.BlockSpec((rows, TILE), lambda i: (0, i)), resident((live, h))]
        + [resident((BOUND, h))] * len(blocks)
        + [ANY] * len(after),
        out_specs=pl.BlockSpec((TILE, h), lambda i: (i, 0)),
        out_shape=pltpu.HBM((live, h), F32),
        compiler_params=params(26),
        cost_estimate=cost(2 * live * rows * h, live * h * 6),
        name="gather",
    )(far(adjacency), far(features), *blocks, *after)


def fetch(pieces, numbers, planes, target, sem, at_ref):
    core, lo, hi, wa = (at_ref[j] for j in range(1, 5))
    rows = target.shape[0] // (8 * planes)
    copies = []
    for m, ((n, first), piece) in enumerate(zip(numbers, pieces)):
        for k in range(piece.shape[0] // rows):
            chip = lax.rem(hi - first - k + planes, planes) * 2 + (1 - lo if n // 2 % 2 else lo)
            owner = (chip * 2 + (1 - core if n // 4 else core)) * 2 + (1 - wa if n % 2 else wa)
            copies.append(
                pltpu.make_async_copy(
                    piece.at[pl.ds(k * rows, rows), :],
                    target.at[pl.ds(pl.multiple_of(owner * rows, rows), rows), :],
                    sem.at[m, k],
                )
            )
    return copies


def place_kernel(at_ref, *refs, numbers, planes):
    target, sem = refs[-2:]
    copies = fetch(refs[: len(numbers)], numbers, planes, target, sem, at_ref)
    for copy in copies:
        copy.start()
    for copy in copies:
        copy.wait()


def place(at, pieces, numbers, planes):
    h, n = 8 * pieces[0].shape[0], pieces[0].shape[1]
    return pl.pallas_call(
        functools.partial(place_kernel, numbers=numbers, planes=planes),
        in_specs=[SMEM] + [ANY] * len(pieces),
        out_specs=WHOLE,
        out_shape=pltpu.VMEM((h, n), BF16),
        scratch_shapes=[pltpu.SemaphoreType.DMA((len(pieces), planes))],
        compiler_params=params(4),
        cost_estimate=cost(0, h * n),
        name="place",
    )(at, *pieces)


def layer_kernel(at_ref, part_ref, c_ref, d_ref, cl_ref, same_ref, last_ref, inv_ref, ct_ref, *refs, tiles, numbers, planes):
    count = len(numbers)
    pieces, refs = refs[:count], refs[count + 1 :]
    o_ref, agl_ref, m_all, gl_all, gb, far_low, far_high, w, b, sem = refs
    i = pl.program_id(0)
    h = part_ref.shape[1]
    copies = fetch(pieces, numbers, planes, w, sem, at_ref)

    @pl.when(i == 0)
    def _():
        for copy in copies:
            copy.start()
        gb[...] = jnp.zeros_like(gb)

    @pl.when(i < tiles)
    def _():
        total = part_ref[...] + dot(c_ref[...], same_ref[...], 0, 0) + dot(d_ref[...], last_ref[...], 0, 0)
        m_all[pl.ds(pl.multiple_of(i * TILE, TILE), TILE), :] = (total * inv_ref[...]).astype(BF16)

    @pl.when(i == 0)
    def _():
        for copy in copies:
            copy.wait()
        b[...] = w[:, h:].astype(F32).T[:8, :]

    @pl.when(i < tiles)
    def _():
        base = pl.multiple_of(i * TILE, TILE)
        rows = pl.ds(base, TILE)
        mixed = m_all[rows, :]
        live = base + lax.broadcasted_iota(jnp.int32, (TILE, 256), 0) < at_ref[0]
        inverse = inv_ref[...]
        for j in range(0, h, 256):
            at = slice(j, j + 256)
            v = dot(mixed, w[:, at], 1, 0) + b[0:1, at]
            square = v * v
            half = jnp.where(live, 0.5 + 0.5 * jnp.tanh(v * (GELU_A + (GELU_A * GELU_B) * square)), 0.0)
            o_ref[:, at] = v * half
            slope = half + (half - half * half) * (v * (2 * GELU_A + (6 * GELU_A * GELU_B) * square))
            grad = ct_ref[:, at].astype(F32) * slope
            gl_all[rows, at] = grad.astype(BF16)
            agl_ref[rows, at] = (grad * inverse).astype(BF16)
            gb[:, at] += jnp.sum(grad.reshape(TILE // 8, 8, 256), axis=0)

    @pl.when(i == tiles)
    def _():
        o_ref[...] = jnp.zeros_like(o_ref)
        away = dot(cl_ref[...], agl_ref[...], 1, 0).astype(BF16)
        far_low[...] = away[: BOUND // 2]
        far_high[...] = away[BOUND // 2 :]


def weight_kernel(at_ref, m_all, gl_all, gb, *refs, mine):
    out_ref, gb_ref = refs[-2:]
    i = pl.program_id(0)
    blocks = m_all.shape[1] // WIDE
    n = out_ref.shape[1]
    core = at_ref[1] if mine else 1 - at_ref[1]
    columns = pl.ds(pl.multiple_of(core * n, n), n)

    @pl.when(i < blocks)
    def _():
        at = pl.ds(pl.multiple_of(i * WIDE, WIDE), WIDE)
        out_ref[...] = dot(m_all[:, at], gl_all[:, columns], 0, 0).astype(BF16)

    @pl.when(i == blocks)
    def _():
        total = jnp.sum(gb[:, columns], axis=0, keepdims=True)
        gb_ref[...] = jnp.broadcast_to(total, gb_ref.shape)
        if not mine:
            out_ref[:SPARE, :] = jnp.broadcast_to(total, (SPARE, n)).astype(BF16)


def weight_share(at, mixed, low, bias, mine, after):
    live, h = mixed.shape
    n, blocks = h // 2, h // WIDE
    rows = h if mine else h + SPARE
    return pl.pallas_call(
        functools.partial(weight_kernel, mine=mine),
        grid_spec=pltpu.PrefetchScalarGridSpec(
            num_scalar_prefetch=1,
            grid=(blocks + 1,),
            in_specs=[WHOLE, WHOLE, resident((8, h))] + [ANY] * len(after),
            out_specs=[
                pl.BlockSpec((WIDE, n), lambda i, s: (jnp.minimum(i, -(-rows // WIDE) - 1), 0)),
                resident((8, n)),
            ],
        ),
        out_shape=[(pltpu.VMEM if mine else pltpu.HBM)((rows, n), BF16), jax.ShapeDtypeStruct((8, n), F32)],
        compiler_params=params(12),
        cost_estimate=cost(live * h * h, live * h * 4),
        name="weight_share",
    )(at, held(mixed), held(low), bias, *after)


def layer(at, part, adjacency, same, last, inverse, cotangent, pieces, numbers, weight, planes):
    live, h = part.shape
    nodes = cotangent.shape[0]
    tiles = live // TILE
    below = adjacency.shape[0] // BOUND - 1

    def row(i, s):
        return (jnp.minimum(i, tiles - 1), 0)

    return pl.pallas_call(
        functools.partial(layer_kernel, tiles=tiles, numbers=numbers, planes=planes),
        grid_spec=pltpu.PrefetchScalarGridSpec(
            num_scalar_prefetch=1,
            grid=(tiles + 1,),
            in_specs=[
                pl.BlockSpec((TILE, h), row),
                pl.BlockSpec((BOUND, TILE), lambda i, s: (below - 1, jnp.minimum(i, tiles - 1))),
                pl.BlockSpec((BOUND, TILE), lambda i, s: (below, jnp.minimum(i, tiles - 1))),
                pl.BlockSpec((BOUND, live), lambda i, s: (below, 0), pipeline_mode=pl.Buffered(1)),
                resident(same.shape),
                resident(last.shape),
                pl.BlockSpec((TILE, 1), row),
                pl.BlockSpec((TILE, h), row),
            ]
            + [ANY] * len(pieces)
            + [WHOLE],
            out_specs=[
                pl.BlockSpec((TILE, h), lambda i, s: (i, 0)),
                WHOLE,
                WHOLE,
                WHOLE,
                resident((8, h)),
                resident((BOUND // 2, h)),
                resident((BOUND // 2, h)),
                WHOLE,
            ],
            scratch_shapes=[
                pltpu.VMEM((8, h), F32),
                pltpu.SemaphoreType.DMA((len(pieces), planes)),
            ],
        ),
        out_shape=[
            jax.ShapeDtypeStruct((nodes, h), F32),
            pltpu.VMEM((live, h), BF16),
            pltpu.VMEM((live, h), BF16),
            pltpu.VMEM((live, h), BF16),
            jax.ShapeDtypeStruct((8, h), F32),
            pltpu.HBM((BOUND // 2, h), BF16),
            pltpu.HBM((BOUND // 2, h), BF16),
            pltpu.VMEM(weight.shape, BF16),
        ],
        input_output_aliases={9 + len(pieces): 7},
        compiler_params=params(16),
        cost_estimate=cost(3 * live * h * h, live * h * 12),
        name="layer",
    )(at, far(part), far(adjacency), far(adjacency), far(adjacency), same, last, inverse, far(cotangent), *pieces, held(weight))


def halves(at_ref, value, rows):
    parts = [value[k * rows : (k + 1) * rows] for k in range(4)]
    even, odd = jnp.concatenate([parts[0], parts[2]]), jnp.concatenate([parts[1], parts[3]])
    first = at_ref[4] == 0
    return jnp.where(first, even, odd), jnp.where(first, odd, even)


def spare_rows(row, n):
    count = -(-row.shape[1] // n)
    row = jnp.concatenate([row, jnp.zeros((1, count * n - row.shape[1]), F32)], axis=1) if count * n > row.shape[1] else row
    at = lax.broadcasted_iota(jnp.int32, (SPARE, n), 0)
    rows = jnp.zeros((SPARE, n), F32)
    for k in range(count):
        rows = jnp.where(at == k, row[:, k * n : (k + 1) * n], rows)
    return rows.astype(BF16)


def from_spare(rows, total):
    n = rows.shape[1]
    return jnp.concatenate([rows[k : k + 1, :] for k in range(-(-total // n))], axis=1)[:, :total].astype(F32)


def share_kernel(at_ref, kept_ref, came_ref, gb_ref, low_ref, high_ref, a_own, a_sent, b_own, b_sent, gb_out, *, rows):
    h = kept_ref.shape[0]
    n_a, n_b = a_own.shape[1], b_own.shape[1]
    for g in range(h // (4 * rows)):
        at = slice(g * 4 * rows, (g + 1) * 4 * rows)
        value = (kept_ref[at, :].astype(F32) + came_ref[at, :].astype(F32)).astype(BF16)
        mine, other = halves(at_ref, value[:, :n_a], rows)
        at = slice(g * 2 * rows, (g + 1) * 2 * rows)
        a_own[at, :] = mine
        a_sent[at, :] = other
        here = g % 2 == at_ref[2]
        at = slice(g // 2 * 4 * rows, (g // 2 + 1) * 4 * rows)

        @pl.when(here)
        def _():
            b_own[at, :] = value[:, n_a:]

        @pl.when(jnp.logical_not(here))
        def _():
            b_sent[at, :] = value[:, n_a:]

    total = gb_ref[0:1, :] + came_ref[h : h + 1, :].astype(F32)
    gb_out[...] = jnp.broadcast_to(total, gb_out.shape)
    a_sent[h // 2 :, :] = spare_rows(total, n_a)
    b_sent[h // 2 :, :] = jnp.zeros((SPARE, n_b), BF16)


def share_rows(at, kept, came, bias, rows, after):
    h, n = kept.shape
    n_a = n * FIRST // 8
    n_b = n - n_a
    return pl.pallas_call(
        functools.partial(share_kernel, rows=rows),
        in_specs=[SMEM] + [WHOLE] * 3 + [ANY] * 2,
        out_specs=[WHOLE] * 5,
        out_shape=[
            pltpu.VMEM((h // 2, n_a), BF16),
            pltpu.VMEM((h // 2 + SPARE, n_a), BF16),
            pltpu.VMEM((h // 2, n_b), BF16),
            pltpu.VMEM((h // 2 + SPARE, n_b), BF16),
            jax.ShapeDtypeStruct((8, n), F32),
        ],
        compiler_params=params(10),
        cost_estimate=cost(0, h * n * 8),
        name="share",
    )(at, kept, came, bias, *after)


def fold_kernel(at_ref, a_ref, a_came, b_ref, b_came, gb_ref, _, a_own, a_sent, b_own, b_sent, gb_out, *, rows):
    lo, two = at_ref[2], 2 * rows
    n = a_ref.shape[1]
    planes = a_ref.shape[0] // (2 * two)
    for z in range(planes):
        out = slice(z * two, (z + 1) * two)
        near = pl.ds(pl.multiple_of((2 * z + lo) * two, two), two)
        far = pl.ds(pl.multiple_of((2 * z + 1 - lo) * two, two), two)
        a_own[out, :] = a_ref[near, :].astype(F32) + a_came[near, :].astype(F32)
        a_sent[out, :] = (a_ref[far, :].astype(F32) + a_came[far, :].astype(F32)).astype(BF16)
        at = slice(z * 2 * two, (z + 1) * 2 * two)
        mine, other = halves(at_ref, b_ref[at, :].astype(F32) + b_came[at, :].astype(F32), rows)
        b_own[out, :] = mine
        b_sent[out, :] = other.astype(BF16)
    total = gb_ref[0:1, :] + from_spare(a_came[a_ref.shape[0] :, :], gb_ref.shape[1])
    gb_out[...] = jnp.broadcast_to(total, gb_out.shape)
    a_sent[planes * two :, :] = spare_rows(total, n)


def fold(at, a_own, a_came, b_own, b_came, bias, rows, after):
    count, n_a, n_b = b_own.shape[0] // 2, a_own.shape[1], b_own.shape[1]
    return pl.pallas_call(
        functools.partial(fold_kernel, rows=rows),
        in_specs=[SMEM] + [WHOLE] * 5 + [ANY],
        out_specs=[WHOLE] * 5,
        out_shape=[
            jax.ShapeDtypeStruct((count, n_a), F32),
            jax.ShapeDtypeStruct((count + SPARE, n_a), BF16),
            jax.ShapeDtypeStruct((count, n_b), F32),
            jax.ShapeDtypeStruct((count, n_b), BF16),
            jax.ShapeDtypeStruct(bias.shape, F32),
        ],
        compiler_params=params(22),
        cost_estimate=cost(0, b_own.size * 9),
        name="fold",
    )(at, a_own, a_came, b_own, b_came, bias, after)


def part_kernel(at_ref, a_ref, a_came, b_ref, b_came, gb_ref, *refs, rows, planes):
    gb_out, own, *sent = refs[-1 - planes :]
    two = 2 * rows
    n = a_ref.shape[1]
    total = gb_ref[0:1, :] + from_spare(a_came[a_ref.shape[0] :, :], gb_ref.shape[1])
    gb_out[...] = jnp.broadcast_to(total, gb_out.shape)
    for k in range(planes):
        at = pl.ds(pl.multiple_of(lax.rem(at_ref[3] + k, planes) * two, two), two)
        out = own if k == 0 else sent[k - 1]
        out[:two, :n] = (a_ref[at, :] + a_came[at, :].astype(F32)).astype(out.dtype)
        out[:two, n:] = (b_ref[at, :] + b_came[at, :].astype(F32)).astype(out.dtype)
        if k:
            out[two:, :] = jnp.broadcast_to(total, (SPARE, total.shape[1])).astype(BF16)


def part_planes(at, a_own, a_came, b_own, b_came, bias, rows, planes, after):
    n = a_own.shape[1] + b_own.shape[1]
    return pl.pallas_call(
        functools.partial(part_kernel, rows=rows, planes=planes),
        in_specs=[SMEM] + [WHOLE] * 5 + [ANY] * len(after),
        out_specs=[WHOLE] * (1 + planes),
        out_shape=[jax.ShapeDtypeStruct(bias.shape, F32), jax.ShapeDtypeStruct((2 * rows, n), F32)]
        + [jax.ShapeDtypeStruct((2 * rows + SPARE, n), BF16)] * (planes - 1),
        compiler_params=params(14),
        cost_estimate=cost(0, a_own.size * 18),
        name="part_planes",
    )(at, a_own, a_came, b_own, b_came, bias, *after)


def finish_kernel(at_ref, gb_ref, own, *refs, rows):
    came, mine_ref, other_ref = refs[:-3], refs[-2], refs[-1]
    total, bias = own[...], gb_ref[0:1, :]
    for ref in came:
        total = total + ref[: 2 * rows, :].astype(F32)
        bias = bias + ref[2 * rows : 2 * rows + 1, :].astype(F32)
    first = at_ref[1] == 0
    low, high = total[:rows], total[rows:]
    bias = jnp.broadcast_to(bias, (8, bias.shape[1]))
    mine_ref[:rows, :], other_ref[:rows, :] = jnp.where(first, low, high), jnp.where(first, high, low)
    mine_ref[rows:, :], other_ref[rows:, :] = bias, bias


def finish(at, bias, own, came, rows, after):
    shape = jax.ShapeDtypeStruct((rows + 8, own.shape[1]), F32)
    return pl.pallas_call(
        functools.partial(finish_kernel, rows=rows),
        in_specs=[SMEM] + [WHOLE] * (2 + len(came)) + [ANY],
        out_specs=[WHOLE] * 2,
        out_shape=[shape] * 2,
        compiler_params=params(10),
        cost_estimate=cost(0, own.size * 8),
        name="finish",
    )(at, bias, own, *came, after)


def scatter_bound_kernel(c_ref, g_ref, *refs, count):
    *outs, part, sem = refs[len(refs) - 2 - count :]
    i = pl.program_id(0)
    part[i] = dot(c_ref[...], g_ref[...], 1, 0).astype(BF16)
    copies = [pltpu.make_async_copy(part.at[k], out, sem.at[k]) for k, out in enumerate(outs)]
    for k, copy in enumerate(copies):

        @pl.when(i == k)
        def _():
            copy.start()

    @pl.when(i == len(outs) - 1)
    def _():
        for copy in copies:
            copy.wait()


def scatter_bound(adjacency, grads, after):
    live, h = grads.shape
    blocks = (adjacency.shape[0] - live) // BOUND - 1
    return pl.pallas_call(
        functools.partial(scatter_bound_kernel, count=blocks),
        grid=(blocks,),
        in_specs=[pl.BlockSpec((BOUND, live), lambda i: (i + live // BOUND, 0)), resident((live, h))] + [ANY] * len(after),
        out_specs=[ANY] * blocks,
        out_shape=[pltpu.HBM((BOUND, h), BF16)] * blocks,
        scratch_shapes=[pltpu.VMEM((blocks, BOUND, h), BF16), pltpu.SemaphoreType.DMA((blocks,))],
        compiler_params=params(22),
        cost_estimate=cost(2 * blocks * BOUND * live * h, live * h * 4),
        name="scatter_bound",
    )(far(adjacency), grads, *after)


def grad_rows_kernel(c_ref, g_ref, *refs, low, tiles):
    o_ref, lead_ref, w, sem = refs[-4:]
    i = pl.program_id(0)
    copy = pltpu.make_async_copy(refs[0].at[:, pl.ds(0, w.shape[1])], w, sem)

    @pl.when(i == 0)
    def _():
        copy.start()

    @pl.when(low + i < tiles)
    def _():
        total = dot(c_ref[...], g_ref[...], 1, 0)

        @pl.when(i == 0)
        def _():
            lead_ref[...] = total if low == 0 else jnp.zeros_like(lead_ref)
            copy.wait()

        @pl.when(low + i > 0)
        def _():
            o_ref[...] = dot(total.astype(BF16), w[...], 1, 1)

    @pl.when(low + i == tiles)
    def _():
        o_ref[...] = jnp.zeros_like(o_ref)


def grad_rows(adjacency, grads, weight, nodes, low, high, before, after):
    live, h = grads.shape
    tiles = live // TILE
    extra = [] if before is None else [before]
    outs = [jax.ShapeDtypeStruct((nodes, h), F32), TOKEN if low else jax.ShapeDtypeStruct((TILE, h), F32)]
    out_specs = [pl.BlockSpec((TILE, h), lambda i: (low + i, 0)), resident((8, 128) if low else (TILE, h))]
    return pl.pallas_call(
        functools.partial(grad_rows_kernel, low=low, tiles=tiles),
        grid=(high - low,),
        in_specs=[
            pl.BlockSpec((TILE, live), lambda i: (jnp.minimum(low + i, tiles - 1), 0)),
            resident((live, h)),
            ANY,
        ]
        + [ANY] * (len(extra) + len(after)),
        out_specs=out_specs,
        scratch_shapes=[pltpu.VMEM((h, h), BF16), pltpu.SemaphoreType.DMA],
        out_shape=outs,
        input_output_aliases={3: 0} if extra else {},
        compiler_params=params(30),
        cost_estimate=cost((2 * live + 2 * h) * (high - low) * TILE * h, live * h * 8),
        name="grad_rows",
    )(far(adjacency), grads, far(weight), *extra, *after)


def back_kernel(outer_ref, low_ref, own_ref, came_ref, high_ref, _, outer_back, own_back):
    i = pl.program_id(0)
    half = pl.num_programs(0) // 2
    early = (i < half).astype(F32)
    outer_back[...] = (outer_ref[...].astype(F32) + early * low_ref[...].astype(F32)).astype(BF16)
    own = own_ref[...].astype(F32) + came_ref[...].astype(F32)
    own_back[...] = (own + (1 - early) * high_ref[...].astype(F32)).astype(BF16)


def back(outer, low, own, came, high, after):
    rows, h = own.shape
    steps = 2
    half = steps // 2
    whole = pl.BlockSpec((rows // steps, h), lambda i: (i, 0))
    first = pl.BlockSpec((rows // steps, h), lambda i: (jnp.minimum(i, half - 1), 0))
    second = pl.BlockSpec((rows // steps, h), lambda i: (jnp.maximum(i - half, 0), 0))
    return pl.pallas_call(
        back_kernel,
        grid=(steps,),
        in_specs=[whole, first, whole, whole, second, ANY],
        out_specs=[whole] * 2,
        out_shape=[jax.ShapeDtypeStruct((rows, h), BF16)] * 2,
        compiler_params=params(10),
        cost_estimate=cost(0, own.size * 12),
        name="back",
    )(far(outer), low, far(own), came, high, after)


def grad_lead_kernel(lead_ref, *refs):
    came, (w_ref, _, o_ref, token_ref, total) = refs[:3], refs[3:]

    @pl.when(pl.program_id(0) == 0)
    def _():
        value = lead_ref[...]
        for ref in came:
            value = value + ref[...].astype(F32)
        total[...] = value.astype(BF16)
        token_ref[...] = jnp.zeros_like(token_ref)

    o_ref[...] = dot(total[...], w_ref[...], 1, 1)


def grad_lead(lead, came, weight, grads):
    rows, h = lead.shape
    return pl.pallas_call(
        grad_lead_kernel,
        grid=(4,),
        in_specs=[resident((rows, h))] * 4 + [pl.BlockSpec((h // 4, h), lambda i: (i, 0)), ANY],
        out_specs=[pl.BlockSpec((rows, h // 4), lambda i: (0, i)), resident((8, 128))],
        out_shape=[jax.ShapeDtypeStruct(grads.shape, F32), TOKEN],
        scratch_shapes=[pltpu.VMEM((rows, h), BF16)],
        input_output_aliases={5: 0},
        compiler_params=params(20),
        cost_estimate=cost(2 * rows * h * h, h * h * 2),
        name="grad_lead",
    )(lead, *came, weight, grads)


def body(features, weight, bias, neighbours, degrees, cluster_sizes, cotangent):
    axes = ("blk", "wa")
    n_blk, n_wa = lax.axis_size("blk"), lax.axis_size("wa")
    devices, n_hi = n_blk * n_wa, n_blk // 4
    blk, wa = lax.axis_index("blk"), lax.axis_index("wa")
    core, lo, hi = blk % 2, (blk // 2) % 2, blk // 4
    nodes, h = features.shape
    share, n = h // devices, h // 2
    live = min(nodes, -(-(-(-CMAX // n_wa)) // TILE) * TILE)

    def permute(value, target):
        pairs = [(b * n_wa + w, target(b, w)) for b in range(n_blk) for w in range(n_wa)]
        return lax.ppermute(value, axes, [(s, b * n_wa + w) for s, (b, w) in pairs])

    def swap_wa(value):
        return permute(value, lambda b, w: (b, 1 - w))

    def swap_core(value):
        return permute(value, lambda b, w: (b ^ 1, w))

    def swap_outer(value, parity=None):
        pairs = [(b, (b + (1 if b % 2 else -1)) % n_blk) for b in range(n_blk)]
        chosen = [(b, t) for b, t in pairs if parity is None or (b if b % 2 else t) // 2 % 2 == parity]
        return lax.ppermute(value, axes, [(b * n_wa + w, t * n_wa + w) for b, t in chosen for w in range(n_wa)])

    def swap_lo(value):
        return permute(value, lambda b, w: (b ^ 2, w))

    def rotate_hi(value, k):
        return permute(value, lambda b, w: ((b + 4 * k) % n_blk, w))

    leading = features[:BOUND]
    partner = swap_wa(leading)
    row_same = swap_outer(leading, 0)

    sheet = jnp.concatenate([weight, jnp.broadcast_to(bias[:, None], (share, 128))], axis=1)
    planes = [rotate_hi(sheet, k) for k in range(1, n_hi)]

    live_count = (cluster_sizes[0] - wa + n_wa - 1) // n_wa
    table = neighbours[:, :live]
    beyond = table - nodes
    segment, within = beyond // (n_wa * BOUND), beyond % (n_wa * BOUND)
    same = within // BOUND == wa
    row = within % BOUND
    side = jnp.where(same, 0, BOUND) + row
    inner = (segment == 2) == (core == 0)
    away = jnp.where(inner, live + BOUND, live + BOUND + n_wa * BOUND) + side
    home = jnp.where(same, row, live + row)
    index = jnp.where(table < nodes, table, jnp.where(segment == 0, home, away))
    valid = jnp.arange(FANOUT, dtype=jnp.int32)[:, None] < degrees[None, :live]
    index = jnp.where(valid, index, -1)
    inverse = (1.0 / (degrees[:live].astype(F32) + 1.0))[:, None]
    at = jnp.stack([live_count, core, lo, hi, wa]).astype(jnp.int32)

    adjacency = counts(index, (live + (1 + 2 * n_wa) * BOUND) // TILE, [inverse, at])
    partner, late_leading, *planes = tie([partner, leading, *planes], [far(adjacency)])
    sheet = jnp.concatenate([sheet, *planes])
    half_sheet, row_sheet = swap_wa(sheet), swap_lo(sheet)
    inner_same, inner_other = swap_core(late_leading), swap_core(partner)
    plane_same = swap_outer(late_leading, 1)
    part = gather(adjacency, features, (partner, inner_same, inner_other), live, [])
    half_sheet, row_same, plane_same = tie([half_sheet, row_same, plane_same], [far(part)])
    outer_same = jnp.where((blk // 2 % 2 == 0) == (core == 1), row_same, plane_same)
    outer_other = swap_wa(outer_same)
    cut = n_hi * 3 // 4
    row_tail, outer_other = tie([row_sheet[cut * share :], outer_other], [])
    late = list(tie([swap_lo(half_sheet[: cut * share]), swap_wa(row_tail)], []))
    pieces = [sheet, half_sheet, row_sheet]
    pieces = pieces + [swap_core(value) for value in pieces]
    matrix = place(at, pieces, [(k, 0) for k in (0, 1, 2, 4, 5, 6)], n_hi)
    output, grads, mixed, low, bias_sum, far_low, far_high, matrix = layer(
        at,
        part,
        adjacency,
        outer_same,
        outer_other,
        inverse,
        cotangent,
        late + [swap_core(value) for value in late],
        [(3, 0), (3, cut), (7, 0), (7, cut)],
        matrix,
        n_hi,
    )
    sent, token = weight_share(at, mixed, low, bias_sum, False, [])
    came = swap_core(sent)
    kept, bias_sum = weight_share(at, mixed, low, bias_sum, True, [token])

    far_low, far_high = swap_wa(far_low), swap_outer(far_high)
    a, a_sent, b, b_sent, bias_sum = share_rows(at, kept, came, bias_sum, share, [far_low, far_high])
    a_came, b_came = swap_wa(a_sent), swap_lo(b_sent)

    own_bound, inner_same_g, inner_other_g, outer_same_g = scatter_bound(adjacency, grads, [bias_sum])
    own_came, inner_came = swap_core(inner_other_g), swap_core(inner_same_g)
    split, tiles = live // TILE // 3, -(-nodes // TILE)
    grad_features, lead = grad_rows(adjacency, grads, matrix, nodes, 0, split, None, [far(own_bound)])
    outer_back, own_back = back(outer_same_g, far_low, own_bound, own_came, far_high, lead)
    outer_back = swap_outer(outer_back)
    a, a_sent, b, b_sent, bias_sum = fold(at, a, a_came, b, b_came, bias_sum, share, own_back)
    a_came, b_came = swap_lo(a_sent), swap_wa(b_sent)
    late = live // TILE * 5 // 6
    grad_features, token = grad_rows(
        adjacency, grads, matrix, nodes, split, late, grad_features, [bias_sum]
    )
    bias_sum, own, *rest = part_planes(
        at, a, a_came, b, b_came, bias_sum, share, n_hi, [token]
    )
    (own_back,) = tie([own_back], [own])
    returned = (inner_came, outer_back, swap_wa(own_back))
    rest = [rotate_hi(value, k + 1) for k, value in enumerate(rest)]
    grad_features, _ = grad_rows(adjacency, grads, matrix, nodes, late, tiles, grad_features, [bias_sum])
    grad_features, token = grad_lead(lead, returned, matrix, grad_features)
    mine, other = finish(at, bias_sum, own, rest, share, token)
    other = swap_core(other)
    first, second = jnp.where(core == 0, mine, other), jnp.where(core == 0, other, mine)
    grad_weight = jnp.concatenate([first[:share], second[:share]], axis=1)
    bias_row = jnp.concatenate([first[share], second[share]])
    grad_bias = lax.dynamic_slice_in_dim(bias_row, (blk * n_wa + wa) * share, share)
    return (output, grad_features, grad_weight, grad_bias)


def solution(mesh):
    return jax.shard_map(
        body,
        mesh=mesh,
        in_specs=(
            P(("blk", "wa"), None),
            P(("blk", "wa"), None),
            P(("blk", "wa")),
            P(None, ("blk", "wa")),
            P(("blk", "wa")),
            P("blk"),
            P(("blk", "wa"), None),
        ),
        out_specs=(
            P(("blk", "wa"), None),
            P(("blk", "wa"), None),
            P(("blk", "wa"), None),
            P(("blk", "wa")),
        ),
        check_vma=False,
    )
```

```python
import functools
import math

import jax
import jax.numpy as jnp
from jax import lax
from jax.experimental import pallas as pl
from jax.experimental.pallas import tpu as pltpu
from jax.sharding import PartitionSpec as P

FANOUT = 16
BOUND = 256
CMAX = 3016
TILE = 256
WIDE = 1024
F32 = jnp.float32
BF16 = jnp.bfloat16
MIB = 1024 * 1024
GELU_A = math.sqrt(2 / math.pi)
GELU_B = 0.044715


ANY = pl.BlockSpec(memory_space=pl.ANY)
SMEM = pl.BlockSpec(memory_space=pltpu.SMEM)
WHOLE = pl.BlockSpec(memory_space=pltpu.VMEM)
SPARE = 16
FIRST = 4
TOKEN = jax.ShapeDtypeStruct((8, 128), F32)


def params(mib):
    return pltpu.CompilerParams(vmem_limit_bytes=mib * MIB)


def held(value):
    return pltpu.with_memory_space_constraint(value, pltpu.VMEM)


def far(value):
    return pltpu.with_memory_space_constraint(value, pltpu.HBM)


def tie_kernel(*refs):
    pass


def tie(values, after):
    n = len(values)
    return pl.pallas_call(
        tie_kernel,
        in_specs=[ANY] * (n + len(after)),
        out_specs=[ANY] * n,
        out_shape=[jax.ShapeDtypeStruct(v.shape, v.dtype) for v in values],
        input_output_aliases={k: k for k in range(n)},
        compiler_params=params(4),
        name="tie",
    )(*values, *after)


def resident(shape):
    return pl.BlockSpec(shape, lambda *_: (0,) * len(shape), pipeline_mode=pl.Buffered(1))


def cost(flops, nbytes):
    return pl.CostEstimate(flops=int(flops) // 16, bytes_accessed=int(nbytes) // 16, transcendentals=0)


def dot(a, b, ca, cb):
    return lax.dot_general(a, b, (((ca,), (cb,)), ((), ())), preferred_element_type=F32)


def small(value):
    return value.astype(F32).astype(BF16)


def counts_kernel(index_ref, *refs):
    out_ref = refs[-1]
    base = pl.program_id(0) * TILE
    rows = small(lax.broadcasted_iota(jnp.int32, (TILE, 128), 0))
    lanes = lax.broadcasted_iota(jnp.int32, (FANOUT, 128), 1)
    zero, one, two = (jnp.array(v, BF16) for v in (0, 1, 2))
    for c in range(0, out_ref.shape[1], 128):
        entry = small(jnp.clip(index_ref[:, c : c + 128] - base, -1, TILE))
        own = small(jnp.clip(lanes + (c - base), -1, TILE))
        total = jnp.where(own[0:1, :] == rows, two, zero)
        for s in range(FANOUT):
            total = total + jnp.where(entry[s : s + 1, :] == rows, one, zero)
        out_ref[:, c : c + 128] = total


def counts(index, tiles, after):
    n = index.shape[1]
    return pl.pallas_call(
        counts_kernel,
        grid=(tiles,),
        in_specs=[pl.BlockSpec((FANOUT, n), lambda i: (0, 0))] + [ANY] * len(after),
        out_specs=pl.BlockSpec((TILE, n), lambda i: (i, 0)),
        out_shape=pltpu.HBM((tiles * TILE, n), BF16),
        compiler_params=params(12),
        cost_estimate=cost(0, tiles * TILE * n * 16),
        name="counts",
    )(index, *after)


def gather_kernel(c_ref, t_ref, *refs, count):
    o_ref = refs[-1]
    live = t_ref.shape[0]
    total = dot(c_ref[:live, :], t_ref[...], 0, 0)
    for k, ref in enumerate(refs[:count]):
        at = live + k * BOUND
        total = total + dot(c_ref[at : at + BOUND, :], ref[...], 0, 0)
    o_ref[...] = total


def gather(adjacency, features, blocks, live, after):
    h = features.shape[1]
    rows = live + len(blocks) * BOUND
    return pl.pallas_call(
        functools.partial(gather_kernel, count=len(blocks)),
        grid=(live // TILE,),
        in_specs=[pl.BlockSpec((rows, TILE), lambda i: (0, i)), resident((live, h))]
        + [resident((BOUND, h))] * len(blocks)
        + [ANY] * len(after),
        out_specs=pl.BlockSpec((TILE, h), lambda i: (i, 0)),
        out_shape=pltpu.HBM((live, h), F32),
        compiler_params=params(26),
        cost_estimate=cost(2 * live * rows * h, live * h * 6),
        name="gather",
    )(far(adjacency), far(features), *blocks, *after)


def fetch(pieces, numbers, planes, target, sem, at_ref):
    core, lo, hi, wa = (at_ref[j] for j in range(1, 5))
    rows = target.shape[0] // (8 * planes)
    copies = []
    for m, ((n, first), piece) in enumerate(zip(numbers, pieces)):
        for k in range(piece.shape[0] // rows):
            chip = lax.rem(hi - first - k + planes, planes) * 2 + (1 - lo if n // 2 % 2 else lo)
            owner = (chip * 2 + (1 - core if n // 4 else core)) * 2 + (1 - wa if n % 2 else wa)
            copies.append(
                pltpu.make_async_copy(
                    piece.at[pl.ds(k * rows, rows), :],
                    target.at[pl.ds(pl.multiple_of(owner * rows, rows), rows), :],
                    sem.at[m, k],
                )
            )
    return copies


def place_kernel(at_ref, *refs, numbers, planes):
    target, sem = refs[-2:]
    copies = fetch(refs[: len(numbers)], numbers, planes, target, sem, at_ref)
    for copy in copies:
        copy.start()
    for copy in copies:
        copy.wait()


def place(at, pieces, numbers, planes):
    h, n = 8 * pieces[0].shape[0], pieces[0].shape[1]
    return pl.pallas_call(
        functools.partial(place_kernel, numbers=numbers, planes=planes),
        in_specs=[SMEM] + [ANY] * len(pieces),
        out_specs=WHOLE,
        out_shape=pltpu.VMEM((h, n), BF16),
        scratch_shapes=[pltpu.SemaphoreType.DMA((len(pieces), planes))],
        compiler_params=params(4),
        cost_estimate=cost(0, h * n),
        name="place",
    )(at, *pieces)


def layer_kernel(at_ref, part_ref, c_ref, d_ref, cl_ref, same_ref, last_ref, inv_ref, ct_ref, *refs, tiles, numbers, planes):
    count = len(numbers)
    pieces, refs = refs[:count], refs[count + 1 :]
    o_ref, agl_ref, m_all, gl_all, gb, far_low, far_high, w, b, sem = refs
    i = pl.program_id(0)
    h = part_ref.shape[1]
    copies = fetch(pieces, numbers, planes, w, sem, at_ref)

    @pl.when(i == 0)
    def _():
        for copy in copies:
            copy.start()
        gb[...] = jnp.zeros_like(gb)

    @pl.when(i < tiles)
    def _():
        total = part_ref[...] + dot(c_ref[...], same_ref[...], 0, 0) + dot(d_ref[...], last_ref[...], 0, 0)
        m_all[pl.ds(pl.multiple_of(i * TILE, TILE), TILE), :] = (total * inv_ref[...]).astype(BF16)

    @pl.when(i == 0)
    def _():
        for copy in copies:
            copy.wait()
        b[...] = w[:, h:].astype(F32).T[:8, :]

    @pl.when(i < tiles)
    def _():
        base = pl.multiple_of(i * TILE, TILE)
        rows = pl.ds(base, TILE)
        mixed = m_all[rows, :]
        live = base + lax.broadcasted_iota(jnp.int32, (TILE, 256), 0) < at_ref[0]
        inverse = inv_ref[...]
        for j in range(0, h, 256):
            at = slice(j, j + 256)
            v = dot(mixed, w[:, at], 1, 0) + b[0:1, at]
            square = v * v
            half = jnp.where(live, 0.5 + 0.5 * jnp.tanh(v * (GELU_A + (GELU_A * GELU_B) * square)), 0.0)
            o_ref[:, at] = v * half
            slope = half + (half - half * half) * (v * (2 * GELU_A + (6 * GELU_A * GELU_B) * square))
            grad = ct_ref[:, at].astype(F32) * slope
            gl_all[rows, at] = grad.astype(BF16)
            agl_ref[rows, at] = (grad * inverse).astype(BF16)
            gb[:, at] += jnp.sum(grad.reshape(TILE // 8, 8, 256), axis=0)

    @pl.when(i == tiles)
    def _():
        o_ref[...] = jnp.zeros_like(o_ref)
        away = dot(cl_ref[...], agl_ref[...], 1, 0).astype(BF16)
        far_low[...] = away[: BOUND // 2]
        far_high[...] = away[BOUND // 2 :]


def weight_kernel(at_ref, m_all, gl_all, gb, *refs, mine):
    out_ref, gb_ref = refs[-2:]
    i = pl.program_id(0)
    blocks = m_all.shape[1] // WIDE
    n = out_ref.shape[1]
    core = at_ref[1] if mine else 1 - at_ref[1]
    columns = pl.ds(pl.multiple_of(core * n, n), n)

    @pl.when(i < blocks)
    def _():
        at = pl.ds(pl.multiple_of(i * WIDE, WIDE), WIDE)
        out_ref[...] = dot(m_all[:, at], gl_all[:, columns], 0, 0).astype(BF16)

    @pl.when(i == blocks)
    def _():
        total = jnp.sum(gb[:, columns], axis=0, keepdims=True)
        gb_ref[...] = jnp.broadcast_to(total, gb_ref.shape)
        if not mine:
            out_ref[:SPARE, :] = jnp.broadcast_to(total, (SPARE, n)).astype(BF16)


def weight_share(at, mixed, low, bias, mine, after):
    live, h = mixed.shape
    n, blocks = h // 2, h // WIDE
    rows = h if mine else h + SPARE
    return pl.pallas_call(
        functools.partial(weight_kernel, mine=mine),
        grid_spec=pltpu.PrefetchScalarGridSpec(
            num_scalar_prefetch=1,
            grid=(blocks + 1,),
            in_specs=[WHOLE, WHOLE, resident((8, h))] + [ANY] * len(after),
            out_specs=[
                pl.BlockSpec((WIDE, n), lambda i, s: (jnp.minimum(i, -(-rows // WIDE) - 1), 0)),
                resident((8, n)),
            ],
        ),
        out_shape=[(pltpu.VMEM if mine else pltpu.HBM)((rows, n), BF16), jax.ShapeDtypeStruct((8, n), F32)],
        compiler_params=params(12),
        cost_estimate=cost(live * h * h, live * h * 4),
        name="weight_share",
    )(at, held(mixed), held(low), bias, *after)


def layer(at, part, adjacency, same, last, inverse, cotangent, pieces, numbers, weight, planes):
    live, h = part.shape
    nodes = cotangent.shape[0]
    tiles = live // TILE
    below = adjacency.shape[0] // BOUND - 1

    def row(i, s):
        return (jnp.minimum(i, tiles - 1), 0)

    return pl.pallas_call(
        functools.partial(layer_kernel, tiles=tiles, numbers=numbers, planes=planes),
        grid_spec=pltpu.PrefetchScalarGridSpec(
            num_scalar_prefetch=1,
            grid=(tiles + 1,),
            in_specs=[
                pl.BlockSpec((TILE, h), row),
                pl.BlockSpec((BOUND, TILE), lambda i, s: (below - 1, jnp.minimum(i, tiles - 1))),
                pl.BlockSpec((BOUND, TILE), lambda i, s: (below, jnp.minimum(i, tiles - 1))),
                pl.BlockSpec((BOUND, live), lambda i, s: (below, 0), pipeline_mode=pl.Buffered(1)),
                resident(same.shape),
                resident(last.shape),
                pl.BlockSpec((TILE, 1), row),
                pl.BlockSpec((TILE, h), row),
            ]
            + [ANY] * len(pieces)
            + [WHOLE],
            out_specs=[
                pl.BlockSpec((TILE, h), lambda i, s: (i, 0)),
                WHOLE,
                WHOLE,
                WHOLE,
                resident((8, h)),
                resident((BOUND // 2, h)),
                resident((BOUND // 2, h)),
                WHOLE,
            ],
            scratch_shapes=[
                pltpu.VMEM((8, h), F32),
                pltpu.SemaphoreType.DMA((len(pieces), planes)),
            ],
        ),
        out_shape=[
            jax.ShapeDtypeStruct((nodes, h), F32),
            pltpu.VMEM((live, h), BF16),
            pltpu.VMEM((live, h), BF16),
            pltpu.VMEM((live, h), BF16),
            jax.ShapeDtypeStruct((8, h), F32),
            pltpu.HBM((BOUND // 2, h), BF16),
            pltpu.HBM((BOUND // 2, h), BF16),
            pltpu.VMEM(weight.shape, BF16),
        ],
        input_output_aliases={9 + len(pieces): 7},
        compiler_params=params(16),
        cost_estimate=cost(3 * live * h * h, live * h * 12),
        name="layer",
    )(at, far(part), far(adjacency), far(adjacency), far(adjacency), same, last, inverse, far(cotangent), *pieces, held(weight))


def halves(at_ref, value, rows):
    parts = [value[k * rows : (k + 1) * rows] for k in range(4)]
    even, odd = jnp.concatenate([parts[0], parts[2]]), jnp.concatenate([parts[1], parts[3]])
    first = at_ref[4] == 0
    return jnp.where(first, even, odd), jnp.where(first, odd, even)


def spare_rows(row, n):
    count = -(-row.shape[1] // n)
    row = jnp.concatenate([row, jnp.zeros((1, count * n - row.shape[1]), F32)], axis=1) if count * n > row.shape[1] else row
    at = lax.broadcasted_iota(jnp.int32, (SPARE, n), 0)
    rows = jnp.zeros((SPARE, n), F32)
    for k in range(count):
        rows = jnp.where(at == k, row[:, k * n : (k + 1) * n], rows)
    return rows.astype(BF16)


def from_spare(rows, total):
    n = rows.shape[1]
    return jnp.concatenate([rows[k : k + 1, :] for k in range(-(-total // n))], axis=1)[:, :total].astype(F32)


def share_kernel(at_ref, kept_ref, came_ref, gb_ref, low_ref, high_ref, a_own, a_sent, b_own, b_sent, gb_out, *, rows):
    h = kept_ref.shape[0]
    n_a, n_b = a_own.shape[1], b_own.shape[1]
    for g in range(h // (4 * rows)):
        at = slice(g * 4 * rows, (g + 1) * 4 * rows)
        value = (kept_ref[at, :].astype(F32) + came_ref[at, :].astype(F32)).astype(BF16)
        mine, other = halves(at_ref, value[:, :n_a], rows)
        at = slice(g * 2 * rows, (g + 1) * 2 * rows)
        a_own[at, :] = mine
        a_sent[at, :] = other
        here = g % 2 == at_ref[2]
        at = slice(g // 2 * 4 * rows, (g // 2 + 1) * 4 * rows)

        @pl.when(here)
        def _():
            b_own[at, :] = value[:, n_a:]

        @pl.when(jnp.logical_not(here))
        def _():
            b_sent[at, :] = value[:, n_a:]

    total = gb_ref[0:1, :] + came_ref[h : h + 1, :].astype(F32)
    gb_out[...] = jnp.broadcast_to(total, gb_out.shape)
    a_sent[h // 2 :, :] = spare_rows(total, n_a)
    b_sent[h // 2 :, :] = jnp.zeros((SPARE, n_b), BF16)


def share_rows(at, kept, came, bias, rows, after):
    h, n = kept.shape
    n_a = n * FIRST // 8
    n_b = n - n_a
    return pl.pallas_call(
        functools.partial(share_kernel, rows=rows),
        in_specs=[SMEM] + [WHOLE] * 3 + [ANY] * 2,
        out_specs=[WHOLE] * 5,
        out_shape=[
            pltpu.VMEM((h // 2, n_a), BF16),
            pltpu.VMEM((h // 2 + SPARE, n_a), BF16),
            pltpu.VMEM((h // 2, n_b), BF16),
            pltpu.VMEM((h // 2 + SPARE, n_b), BF16),
            jax.ShapeDtypeStruct((8, n), F32),
        ],
        compiler_params=params(10),
        cost_estimate=cost(0, h * n * 8),
        name="share",
    )(at, kept, came, bias, *after)


def fold_kernel(at_ref, a_ref, a_came, b_ref, b_came, gb_ref, _, a_own, a_sent, b_own, b_sent, gb_out, *, rows):
    lo, two = at_ref[2], 2 * rows
    n = a_ref.shape[1]
    planes = a_ref.shape[0] // (2 * two)
    for z in range(planes):
        out = slice(z * two, (z + 1) * two)
        near = pl.ds(pl.multiple_of((2 * z + lo) * two, two), two)
        far = pl.ds(pl.multiple_of((2 * z + 1 - lo) * two, two), two)
        a_own[out, :] = a_ref[near, :].astype(F32) + a_came[near, :].astype(F32)
        a_sent[out, :] = (a_ref[far, :].astype(F32) + a_came[far, :].astype(F32)).astype(BF16)
        at = slice(z * 2 * two, (z + 1) * 2 * two)
        mine, other = halves(at_ref, b_ref[at, :].astype(F32) + b_came[at, :].astype(F32), rows)
        b_own[out, :] = mine
        b_sent[out, :] = other.astype(BF16)
    total = gb_ref[0:1, :] + from_spare(a_came[a_ref.shape[0] :, :], gb_ref.shape[1])
    gb_out[...] = jnp.broadcast_to(total, gb_out.shape)
    a_sent[planes * two :, :] = spare_rows(total, n)


def fold(at, a_own, a_came, b_own, b_came, bias, rows, after):
    count, n_a, n_b = b_own.shape[0] // 2, a_own.shape[1], b_own.shape[1]
    return pl.pallas_call(
        functools.partial(fold_kernel, rows=rows),
        in_specs=[SMEM] + [WHOLE] * 5 + [ANY],
        out_specs=[WHOLE] * 5,
        out_shape=[
            jax.ShapeDtypeStruct((count, n_a), F32),
            jax.ShapeDtypeStruct((count + SPARE, n_a), BF16),
            jax.ShapeDtypeStruct((count, n_b), F32),
            jax.ShapeDtypeStruct((count, n_b), BF16),
            jax.ShapeDtypeStruct(bias.shape, F32),
        ],
        compiler_params=params(22),
        cost_estimate=cost(0, b_own.size * 9),
        name="fold",
    )(at, a_own, a_came, b_own, b_came, bias, after)


def part_kernel(at_ref, a_ref, a_came, b_ref, b_came, gb_ref, *refs, rows, planes):
    gb_out, own, *sent = refs[-1 - planes :]
    two = 2 * rows
    n = a_ref.shape[1]
    total = gb_ref[0:1, :] + from_spare(a_came[a_ref.shape[0] :, :], gb_ref.shape[1])
    gb_out[...] = jnp.broadcast_to(total, gb_out.shape)
    for k in range(planes):
        at = pl.ds(pl.multiple_of(lax.rem(at_ref[3] + k, planes) * two, two), two)
        out = own if k == 0 else sent[k - 1]
        out[:two, :n] = (a_ref[at, :] + a_came[at, :].astype(F32)).astype(out.dtype)
        out[:two, n:] = (b_ref[at, :] + b_came[at, :].astype(F32)).astype(out.dtype)
        if k:
            out[two:, :] = jnp.broadcast_to(total, (SPARE, total.shape[1])).astype(BF16)


def part_planes(at, a_own, a_came, b_own, b_came, bias, rows, planes, after):
    n = a_own.shape[1] + b_own.shape[1]
    return pl.pallas_call(
        functools.partial(part_kernel, rows=rows, planes=planes),
        in_specs=[SMEM] + [WHOLE] * 5 + [ANY] * len(after),
        out_specs=[WHOLE] * (1 + planes),
        out_shape=[jax.ShapeDtypeStruct(bias.shape, F32), jax.ShapeDtypeStruct((2 * rows, n), F32)]
        + [jax.ShapeDtypeStruct((2 * rows + SPARE, n), BF16)] * (planes - 1),
        compiler_params=params(14),
        cost_estimate=cost(0, a_own.size * 18),
        name="part_planes",
    )(at, a_own, a_came, b_own, b_came, bias, *after)


def finish_kernel(at_ref, gb_ref, own, *refs, rows):
    came, mine_ref, other_ref = refs[:-3], refs[-2], refs[-1]
    total, bias = own[...], gb_ref[0:1, :]
    for ref in came:
        total = total + ref[: 2 * rows, :].astype(F32)
        bias = bias + ref[2 * rows : 2 * rows + 1, :].astype(F32)
    first = at_ref[1] == 0
    low, high = total[:rows], total[rows:]
    bias = jnp.broadcast_to(bias, (8, bias.shape[1]))
    mine_ref[:rows, :], other_ref[:rows, :] = jnp.where(first, low, high), jnp.where(first, high, low)
    mine_ref[rows:, :], other_ref[rows:, :] = bias, bias


def finish(at, bias, own, came, rows, after):
    shape = jax.ShapeDtypeStruct((rows + 8, own.shape[1]), F32)
    return pl.pallas_call(
        functools.partial(finish_kernel, rows=rows),
        in_specs=[SMEM] + [WHOLE] * (2 + len(came)) + [ANY],
        out_specs=[WHOLE] * 2,
        out_shape=[shape] * 2,
        compiler_params=params(10),
        cost_estimate=cost(0, own.size * 8),
        name="finish",
    )(at, bias, own, *came, after)


def scatter_bound_kernel(c_ref, g_ref, *refs, count):
    *outs, part, sem = refs[len(refs) - 2 - count :]
    i = pl.program_id(0)
    part[i] = dot(c_ref[...], g_ref[...], 1, 0).astype(BF16)
    copies = [pltpu.make_async_copy(part.at[k], out, sem.at[k]) for k, out in enumerate(outs)]
    for k, copy in enumerate(copies):

        @pl.when(i == k)
        def _():
            copy.start()

    @pl.when(i == len(outs) - 1)
    def _():
        for copy in copies:
            copy.wait()


def scatter_bound(adjacency, grads, after):
    live, h = grads.shape
    blocks = (adjacency.shape[0] - live) // BOUND - 1
    return pl.pallas_call(
        functools.partial(scatter_bound_kernel, count=blocks),
        grid=(blocks,),
        in_specs=[pl.BlockSpec((BOUND, live), lambda i: (i + live // BOUND, 0)), resident((live, h))] + [ANY] * len(after),
        out_specs=[ANY] * blocks,
        out_shape=[pltpu.HBM((BOUND, h), BF16)] * blocks,
        scratch_shapes=[pltpu.VMEM((blocks, BOUND, h), BF16), pltpu.SemaphoreType.DMA((blocks,))],
        compiler_params=params(22),
        cost_estimate=cost(2 * blocks * BOUND * live * h, live * h * 4),
        name="scatter_bound",
    )(far(adjacency), grads, *after)


def grad_rows_kernel(c_ref, g_ref, *refs, low, tiles):
    o_ref, lead_ref, w, sem = refs[-4:]
    i = pl.program_id(0)
    copy = pltpu.make_async_copy(refs[0].at[:, pl.ds(0, w.shape[1])], w, sem)

    @pl.when(i == 0)
    def _():
        copy.start()

    @pl.when(low + i < tiles)
    def _():
        total = dot(c_ref[...], g_ref[...], 1, 0)

        @pl.when(i == 0)
        def _():
            lead_ref[...] = total if low == 0 else jnp.zeros_like(lead_ref)
            copy.wait()

        @pl.when(low + i > 0)
        def _():
            o_ref[...] = dot(total.astype(BF16), w[...], 1, 1)

    @pl.when(low + i == tiles)
    def _():
        o_ref[...] = jnp.zeros_like(o_ref)


def grad_rows(adjacency, grads, weight, nodes, low, high, before, after):
    live, h = grads.shape
    tiles = live // TILE
    extra = [] if before is None else [before]
    outs = [jax.ShapeDtypeStruct((nodes, h), F32), TOKEN if low else jax.ShapeDtypeStruct((TILE, h), F32)]
    out_specs = [pl.BlockSpec((TILE, h), lambda i: (low + i, 0)), resident((8, 128) if low else (TILE, h))]
    return pl.pallas_call(
        functools.partial(grad_rows_kernel, low=low, tiles=tiles),
        grid=(high - low,),
        in_specs=[
            pl.BlockSpec((TILE, live), lambda i: (jnp.minimum(low + i, tiles - 1), 0)),
            resident((live, h)),
            ANY,
        ]
        + [ANY] * (len(extra) + len(after)),
        out_specs=out_specs,
        scratch_shapes=[pltpu.VMEM((h, h), BF16), pltpu.SemaphoreType.DMA],
        out_shape=outs,
        input_output_aliases={3: 0} if extra else {},
        compiler_params=params(30),
        cost_estimate=cost((2 * live + 2 * h) * (high - low) * TILE * h, live * h * 8),
        name="grad_rows",
    )(far(adjacency), grads, far(weight), *extra, *after)


def back_kernel(outer_ref, low_ref, own_ref, came_ref, high_ref, _, outer_back, own_back):
    i = pl.program_id(0)
    half = pl.num_programs(0) // 2
    early = (i < half).astype(F32)
    outer_back[...] = (outer_ref[...].astype(F32) + early * low_ref[...].astype(F32)).astype(BF16)
    own = own_ref[...].astype(F32) + came_ref[...].astype(F32)
    own_back[...] = (own + (1 - early) * high_ref[...].astype(F32)).astype(BF16)


def back(outer, low, own, came, high, after):
    rows, h = own.shape
    steps = 2
    half = steps // 2
    whole = pl.BlockSpec((rows // steps, h), lambda i: (i, 0))
    first = pl.BlockSpec((rows // steps, h), lambda i: (jnp.minimum(i, half - 1), 0))
    second = pl.BlockSpec((rows // steps, h), lambda i: (jnp.maximum(i - half, 0), 0))
    return pl.pallas_call(
        back_kernel,
        grid=(steps,),
        in_specs=[whole, first, whole, whole, second, ANY],
        out_specs=[whole] * 2,
        out_shape=[jax.ShapeDtypeStruct((rows, h), BF16)] * 2,
        compiler_params=params(10),
        cost_estimate=cost(0, own.size * 12),
        name="back",
    )(far(outer), low, far(own), came, high, after)


def grad_lead_kernel(lead_ref, *refs):
    came, (w_ref, _, o_ref, token_ref, total) = refs[:3], refs[3:]

    @pl.when(pl.program_id(0) == 0)
    def _():
        value = lead_ref[...]
        for ref in came:
            value = value + ref[...].astype(F32)
        total[...] = value.astype(BF16)
        token_ref[...] = jnp.zeros_like(token_ref)

    o_ref[...] = dot(total[...], w_ref[...], 1, 1)


def grad_lead(lead, came, weight, grads):
    rows, h = lead.shape
    return pl.pallas_call(
        grad_lead_kernel,
        grid=(1,),
        in_specs=[resident((rows, h))] * 4 + [pl.BlockSpec((h, h), lambda i: (i, 0)), ANY],
        out_specs=[pl.BlockSpec((rows, h), lambda i: (0, i)), resident((8, 128))],
        out_shape=[jax.ShapeDtypeStruct(grads.shape, F32), TOKEN],
        scratch_shapes=[pltpu.VMEM((rows, h), BF16)],
        input_output_aliases={5: 0},
        compiler_params=params(20),
        cost_estimate=cost(2 * rows * h * h, h * h * 2),
        name="grad_lead",
    )(lead, *came, weight, grads)


def body(features, weight, bias, neighbours, degrees, cluster_sizes, cotangent):
    axes = ("blk", "wa")
    n_blk, n_wa = lax.axis_size("blk"), lax.axis_size("wa")
    devices, n_hi = n_blk * n_wa, n_blk // 4
    blk, wa = lax.axis_index("blk"), lax.axis_index("wa")
    core, lo, hi = blk % 2, (blk // 2) % 2, blk // 4
    nodes, h = features.shape
    share, n = h // devices, h // 2
    live = min(nodes, -(-(-(-CMAX // n_wa)) // TILE) * TILE)

    def permute(value, target):
        pairs = [(b * n_wa + w, target(b, w)) for b in range(n_blk) for w in range(n_wa)]
        return lax.ppermute(value, axes, [(s, b * n_wa + w) for s, (b, w) in pairs])

    def swap_wa(value):
        return permute(value, lambda b, w: (b, 1 - w))

    def swap_core(value):
        return permute(value, lambda b, w: (b ^ 1, w))

    def swap_outer(value, parity=None):
        pairs = [(b, (b + (1 if b % 2 else -1)) % n_blk) for b in range(n_blk)]
        chosen = [(b, t) for b, t in pairs if parity is None or (b if b % 2 else t) // 2 % 2 == parity]
        return lax.ppermute(value, axes, [(b * n_wa + w, t * n_wa + w) for b, t in chosen for w in range(n_wa)])

    def swap_lo(value):
        return permute(value, lambda b, w: (b ^ 2, w))

    def rotate_hi(value, k):
        return permute(value, lambda b, w: ((b + 4 * k) % n_blk, w))

    leading = features[:BOUND]
    partner = swap_wa(leading)
    row_same = swap_outer(leading, 0)

    sheet = jnp.concatenate([weight, jnp.broadcast_to(bias[:, None], (share, 128))], axis=1)
    planes = [rotate_hi(sheet, k) for k in range(1, n_hi)]

    live_count = (cluster_sizes[0] - wa + n_wa - 1) // n_wa
    table = neighbours[:, :live]
    beyond = table - nodes
    segment, within = beyond // (n_wa * BOUND), beyond % (n_wa * BOUND)
    same = within // BOUND == wa
    row = within % BOUND
    side = jnp.where(same, 0, BOUND) + row
    inner = (segment == 2) == (core == 0)
    away = jnp.where(inner, live + BOUND, live + BOUND + n_wa * BOUND) + side
    home = jnp.where(same, row, live + row)
    index = jnp.where(table < nodes, table, jnp.where(segment == 0, home, away))
    valid = jnp.arange(FANOUT, dtype=jnp.int32)[:, None] < degrees[None, :live]
    index = jnp.where(valid, index, -1)
    inverse = (1.0 / (degrees[:live].astype(F32) + 1.0))[:, None]
    at = jnp.stack([live_count, core, lo, hi, wa]).astype(jnp.int32)

    adjacency = counts(index, (live + (1 + 2 * n_wa) * BOUND) // TILE, [inverse, at])
    partner, late_leading, *planes = tie([partner, leading, *planes], [far(adjacency)])
    sheet = jnp.concatenate([sheet, *planes])
    half_sheet, row_sheet = swap_wa(sheet), swap_lo(sheet)
    inner_same, inner_other = swap_core(late_leading), swap_core(partner)
    plane_same = swap_outer(late_leading, 1)
    part = gather(adjacency, features, (partner, inner_same, inner_other), live, [])
    half_sheet, row_same, plane_same = tie([half_sheet, row_same, plane_same], [far(part)])
    outer_same = jnp.where((blk // 2 % 2 == 0) == (core == 1), row_same, plane_same)
    outer_other = swap_wa(outer_same)
    cut = n_hi * 3 // 4
    row_tail, outer_other = tie([row_sheet[cut * share :], outer_other], [])
    late = list(tie([swap_lo(half_sheet[: cut * share]), swap_wa(row_tail)], []))
    pieces = [sheet, half_sheet, row_sheet]
    pieces = pieces + [swap_core(value) for value in pieces]
    matrix = place(at, pieces, [(k, 0) for k in (0, 1, 2, 4, 5, 6)], n_hi)
    output, grads, mixed, low, bias_sum, far_low, far_high, matrix = layer(
        at,
        part,
        adjacency,
        outer_same,
        outer_other,
        inverse,
        cotangent,
        late + [swap_core(value) for value in late],
        [(3, 0), (3, cut), (7, 0), (7, cut)],
        matrix,
        n_hi,
    )
    sent, token = weight_share(at, mixed, low, bias_sum, False, [])
    came = swap_core(sent)
    kept, bias_sum = weight_share(at, mixed, low, bias_sum, True, [token])

    far_low, far_high = swap_wa(far_low), swap_outer(far_high)
    a, a_sent, b, b_sent, bias_sum = share_rows(at, kept, came, bias_sum, share, [far_low, far_high])
    a_came, b_came = swap_wa(a_sent), swap_lo(b_sent)

    own_bound, inner_same_g, inner_other_g, outer_same_g = scatter_bound(adjacency, grads, [bias_sum])
    own_came, inner_came = swap_core(inner_other_g), swap_core(inner_same_g)
    split, tiles = live // TILE // 3, -(-nodes // TILE)
    grad_features, lead = grad_rows(adjacency, grads, matrix, nodes, 0, split, None, [far(own_bound)])
    outer_back, own_back = back(outer_same_g, far_low, own_bound, own_came, far_high, lead)
    outer_back = swap_outer(outer_back)
    a, a_sent, b, b_sent, bias_sum = fold(at, a, a_came, b, b_came, bias_sum, share, own_back)
    a_came, b_came = swap_lo(a_sent), swap_wa(b_sent)
    late = live // TILE * 5 // 6
    grad_features, token = grad_rows(
        adjacency, grads, matrix, nodes, split, late, grad_features, [bias_sum]
    )
    bias_sum, own, *rest = part_planes(
        at, a, a_came, b, b_came, bias_sum, share, n_hi, [token]
    )
    (own_back,) = tie([own_back], [own])
    returned = (inner_came, outer_back, swap_wa(own_back))
    rest = [rotate_hi(value, k + 1) for k, value in enumerate(rest)]
    grad_features, _ = grad_rows(adjacency, grads, matrix, nodes, late, tiles, grad_features, [bias_sum])
    grad_features, token = grad_lead(lead, returned, matrix, grad_features)
    mine, other = finish(at, bias_sum, own, rest, share, token)
    other = swap_core(other)
    first, second = jnp.where(core == 0, mine, other), jnp.where(core == 0, other, mine)
    grad_weight = jnp.concatenate([first[:share], second[:share]], axis=1)
    bias_row = jnp.concatenate([first[share], second[share]])
    grad_bias = lax.dynamic_slice_in_dim(bias_row, (blk * n_wa + wa) * share, share)
    return (output, grad_features, grad_weight, grad_bias)


def solution(mesh):
    return jax.shard_map(
        body,
        mesh=mesh,
        in_specs=(
            P(("blk", "wa"), None),
            P(("blk", "wa"), None),
            P(("blk", "wa")),
            P(None, ("blk", "wa")),
            P(("blk", "wa")),
            P("blk"),
            P(("blk", "wa"), None),
        ),
        out_specs=(
            P(("blk", "wa"), None),
            P(("blk", "wa"), None),
            P(("blk", "wa"), None),
            P(("blk", "wa")),
        ),
        check_vma=False,
    )
```

```python
import functools
import math

import jax
import jax.numpy as jnp
from jax import lax
from jax.experimental import pallas as pl
from jax.experimental.pallas import tpu as pltpu
from jax.sharding import PartitionSpec as P

FANOUT = 16
BOUND = 256
CMAX = 3016
TILE = 256
WIDE = 1024
F32 = jnp.float32
BF16 = jnp.bfloat16
MIB = 1024 * 1024
GELU_A = math.sqrt(2 / math.pi)
GELU_B = 0.044715


ANY = pl.BlockSpec(memory_space=pl.ANY)
SMEM = pl.BlockSpec(memory_space=pltpu.SMEM)
WHOLE = pl.BlockSpec(memory_space=pltpu.VMEM)
SPARE = 16
FIRST = 4
TOKEN = jax.ShapeDtypeStruct((8, 128), F32)


def params(mib):
    return pltpu.CompilerParams(vmem_limit_bytes=mib * MIB)


def held(value):
    return pltpu.with_memory_space_constraint(value, pltpu.VMEM)


def far(value):
    return pltpu.with_memory_space_constraint(value, pltpu.HBM)


def tie_kernel(*refs):
    pass


def tie(values, after):
    n = len(values)
    return pl.pallas_call(
        tie_kernel,
        in_specs=[ANY] * (n + len(after)),
        out_specs=[ANY] * n,
        out_shape=[jax.ShapeDtypeStruct(v.shape, v.dtype) for v in values],
        input_output_aliases={k: k for k in range(n)},
        compiler_params=params(4),
        name="tie",
    )(*values, *after)


def resident(shape):
    return pl.BlockSpec(shape, lambda *_: (0,) * len(shape), pipeline_mode=pl.Buffered(1))


def cost(flops, nbytes):
    return pl.CostEstimate(flops=int(flops) // 16, bytes_accessed=int(nbytes) // 16, transcendentals=0)


def dot(a, b, ca, cb):
    return lax.dot_general(a, b, (((ca,), (cb,)), ((), ())), preferred_element_type=F32)


def small(value):
    return value.astype(F32).astype(BF16)


def counts_kernel(index_ref, *refs):
    out_ref = refs[-1]
    base = pl.program_id(0) * TILE
    rows = small(lax.broadcasted_iota(jnp.int32, (TILE, 128), 0))
    lanes = lax.broadcasted_iota(jnp.int32, (FANOUT, 128), 1)
    zero, one, two = (jnp.array(v, BF16) for v in (0, 1, 2))
    for c in range(0, out_ref.shape[1], 128):
        entry = small(jnp.clip(index_ref[:, c : c + 128] - base, -1, TILE))
        own = small(jnp.clip(lanes + (c - base), -1, TILE))
        total = jnp.where(own[0:1, :] == rows, two, zero)
        for s in range(FANOUT):
            total = total + jnp.where(entry[s : s + 1, :] == rows, one, zero)
        out_ref[:, c : c + 128] = total


def counts(index, tiles, after):
    n = index.shape[1]
    return pl.pallas_call(
        counts_kernel,
        grid=(tiles,),
        in_specs=[pl.BlockSpec((FANOUT, n), lambda i: (0, 0))] + [ANY] * len(after),
        out_specs=pl.BlockSpec((TILE, n), lambda i: (i, 0)),
        out_shape=pltpu.HBM((tiles * TILE, n), BF16),
        compiler_params=params(12),
        cost_estimate=cost(0, tiles * TILE * n * 16),
        name="counts",
    )(index, *after)


def gather_kernel(c_ref, t_ref, *refs, count):
    o_ref = refs[-1]
    live = t_ref.shape[0]
    total = dot(c_ref[:live, :], t_ref[...], 0, 0)
    for k, ref in enumerate(refs[:count]):
        at = live + k * BOUND
        total = total + dot(c_ref[at : at + BOUND, :], ref[...], 0, 0)
    o_ref[...] = total


def gather(adjacency, features, blocks, live, after):
    h = features.shape[1]
    rows = live + len(blocks) * BOUND
    return pl.pallas_call(
        functools.partial(gather_kernel, count=len(blocks)),
        grid=(live // TILE,),
        in_specs=[pl.BlockSpec((rows, TILE), lambda i: (0, i)), resident((live, h))]
        + [resident((BOUND, h))] * len(blocks)
        + [ANY] * len(after),
        out_specs=pl.BlockSpec((TILE, h), lambda i: (i, 0)),
        out_shape=pltpu.HBM((live, h), F32),
        compiler_params=params(26),
        cost_estimate=cost(2 * live * rows * h, live * h * 6),
        name="gather",
    )(far(adjacency), far(features), *blocks, *after)


def fetch(pieces, numbers, planes, target, sem, at_ref):
    core, lo, hi, wa = (at_ref[j] for j in range(1, 5))
    rows = target.shape[0] // (8 * planes)
    copies = []
    for m, ((n, first), piece) in enumerate(zip(numbers, pieces)):
        for k in range(piece.shape[0] // rows):
            chip = lax.rem(hi - first - k + planes, planes) * 2 + (1 - lo if n // 2 % 2 else lo)
            owner = (chip * 2 + (1 - core if n // 4 else core)) * 2 + (1 - wa if n % 2 else wa)
            copies.append(
                pltpu.make_async_copy(
                    piece.at[pl.ds(k * rows, rows), :],
                    target.at[pl.ds(pl.multiple_of(owner * rows, rows), rows), :],
                    sem.at[m, k],
                )
            )
    return copies


def place_kernel(at_ref, *refs, numbers, planes):
    target, sem = refs[-2:]
    copies = fetch(refs[: len(numbers)], numbers, planes, target, sem, at_ref)
    for copy in copies:
        copy.start()
    for copy in copies:
        copy.wait()


def place(at, pieces, numbers, planes):
    h, n = 8 * pieces[0].shape[0], pieces[0].shape[1]
    return pl.pallas_call(
        functools.partial(place_kernel, numbers=numbers, planes=planes),
        in_specs=[SMEM] + [ANY] * len(pieces),
        out_specs=WHOLE,
        out_shape=pltpu.VMEM((h, n), BF16),
        scratch_shapes=[pltpu.SemaphoreType.DMA((len(pieces), planes))],
        compiler_params=params(4),
        cost_estimate=cost(0, h * n),
        name="place",
    )(at, *pieces)


def layer_kernel(at_ref, part_ref, c_ref, d_ref, cl_ref, same_ref, last_ref, inv_ref, ct_ref, *refs, tiles, numbers, planes):
    count = len(numbers)
    pieces, refs = refs[:count], refs[count + 1 :]
    o_ref, agl_ref, m_all, gl_all, gb, far_low, far_high, w, b, sem = refs
    i = pl.program_id(0)
    h = part_ref.shape[1]
    copies = fetch(pieces, numbers, planes, w, sem, at_ref)

    @pl.when(i == 0)
    def _():
        for copy in copies:
            copy.start()
        gb[...] = jnp.zeros_like(gb)

    @pl.when(i < tiles)
    def _():
        total = part_ref[...] + dot(c_ref[...], same_ref[...], 0, 0) + dot(d_ref[...], last_ref[...], 0, 0)
        m_all[pl.ds(pl.multiple_of(i * TILE, TILE), TILE), :] = (total * inv_ref[...]).astype(BF16)

    @pl.when(i == 0)
    def _():
        for copy in copies:
            copy.wait()
        b[...] = w[:, h:].astype(F32).T[:8, :]

    @pl.when(i < tiles)
    def _():
        base = pl.multiple_of(i * TILE, TILE)
        rows = pl.ds(base, TILE)
        mixed = m_all[rows, :]
        live = base + lax.broadcasted_iota(jnp.int32, (TILE, 256), 0) < at_ref[0]
        inverse = inv_ref[...]
        for j in range(0, h, 256):
            at = slice(j, j + 256)
            v = dot(mixed, w[:, at], 1, 0) + b[0:1, at]
            square = v * v
            half = jnp.where(live, 0.5 + 0.5 * jnp.tanh(v * (GELU_A + (GELU_A * GELU_B) * square)), 0.0)
            o_ref[:, at] = v * half
            slope = half + (half - half * half) * (v * (2 * GELU_A + (6 * GELU_A * GELU_B) * square))
            grad = ct_ref[:, at].astype(F32) * slope
            gl_all[rows, at] = grad.astype(BF16)
            agl_ref[rows, at] = (grad * inverse).astype(BF16)
            gb[:, at] += jnp.sum(grad.reshape(TILE // 8, 8, 256), axis=0)

    @pl.when(i == tiles)
    def _():
        o_ref[...] = jnp.zeros_like(o_ref)
        away = dot(cl_ref[...], agl_ref[...], 1, 0).astype(BF16)
        far_low[...] = away[: BOUND // 2]
        far_high[...] = away[BOUND // 2 :]


def weight_kernel(at_ref, m_all, gl_all, gb, *refs, mine):
    out_ref, gb_ref = refs[-2:]
    i = pl.program_id(0)
    blocks = m_all.shape[1] // WIDE
    n = out_ref.shape[1]
    core = at_ref[1] if mine else 1 - at_ref[1]
    columns = pl.ds(pl.multiple_of(core * n, n), n)

    @pl.when(i < blocks)
    def _():
        at = pl.ds(pl.multiple_of(i * WIDE, WIDE), WIDE)
        out_ref[...] = dot(m_all[:, at], gl_all[:, columns], 0, 0).astype(BF16)

    @pl.when(i == blocks)
    def _():
        total = jnp.sum(gb[:, columns], axis=0, keepdims=True)
        gb_ref[...] = jnp.broadcast_to(total, gb_ref.shape)
        if not mine:
            out_ref[:SPARE, :] = jnp.broadcast_to(total, (SPARE, n)).astype(BF16)


def weight_share(at, mixed, low, bias, mine, after):
    live, h = mixed.shape
    n, blocks = h // 2, h // WIDE
    rows = h if mine else h + SPARE
    return pl.pallas_call(
        functools.partial(weight_kernel, mine=mine),
        grid_spec=pltpu.PrefetchScalarGridSpec(
            num_scalar_prefetch=1,
            grid=(blocks + 1,),
            in_specs=[WHOLE, WHOLE, resident((8, h))] + [ANY] * len(after),
            out_specs=[
                pl.BlockSpec((WIDE, n), lambda i, s: (jnp.minimum(i, -(-rows // WIDE) - 1), 0)),
                resident((8, n)),
            ],
        ),
        out_shape=[pltpu.VMEM((rows, n), BF16), jax.ShapeDtypeStruct((8, n), F32)],
        compiler_params=params(12),
        cost_estimate=cost(live * h * h, live * h * 4),
        name="weight_share",
    )(at, held(mixed), held(low), bias, *after)


def layer(at, part, adjacency, same, last, inverse, cotangent, pieces, numbers, weight, planes):
    live, h = part.shape
    nodes = cotangent.shape[0]
    tiles = live // TILE
    below = adjacency.shape[0] // BOUND - 1

    def row(i, s):
        return (jnp.minimum(i, tiles - 1), 0)

    return pl.pallas_call(
        functools.partial(layer_kernel, tiles=tiles, numbers=numbers, planes=planes),
        grid_spec=pltpu.PrefetchScalarGridSpec(
            num_scalar_prefetch=1,
            grid=(tiles + 1,),
            in_specs=[
                pl.BlockSpec((TILE, h), row),
                pl.BlockSpec((BOUND, TILE), lambda i, s: (below - 1, jnp.minimum(i, tiles - 1))),
                pl.BlockSpec((BOUND, TILE), lambda i, s: (below, jnp.minimum(i, tiles - 1))),
                pl.BlockSpec((BOUND, live), lambda i, s: (below, 0), pipeline_mode=pl.Buffered(1)),
                resident(same.shape),
                resident(last.shape),
                pl.BlockSpec((TILE, 1), row),
                pl.BlockSpec((TILE, h), row),
            ]
            + [ANY] * len(pieces)
            + [WHOLE],
            out_specs=[
                pl.BlockSpec((TILE, h), lambda i, s: (i, 0)),
                WHOLE,
                WHOLE,
                WHOLE,
                resident((8, h)),
                resident((BOUND // 2, h)),
                resident((BOUND // 2, h)),
                WHOLE,
            ],
            scratch_shapes=[
                pltpu.VMEM((8, h), F32),
                pltpu.SemaphoreType.DMA((len(pieces), planes)),
            ],
        ),
        out_shape=[
            jax.ShapeDtypeStruct((nodes, h), F32),
            pltpu.VMEM((live, h), BF16),
            pltpu.VMEM((live, h), BF16),
            pltpu.VMEM((live, h), BF16),
            jax.ShapeDtypeStruct((8, h), F32),
            pltpu.HBM((BOUND // 2, h), BF16),
            pltpu.HBM((BOUND // 2, h), BF16),
            pltpu.VMEM(weight.shape, BF16),
        ],
        input_output_aliases={9 + len(pieces): 7},
        compiler_params=params(16),
        cost_estimate=cost(3 * live * h * h, live * h * 12),
        name="layer",
    )(at, far(part), far(adjacency), far(adjacency), far(adjacency), same, last, inverse, far(cotangent), *pieces, held(weight))


def halves(at_ref, value, rows):
    parts = [value[k * rows : (k + 1) * rows] for k in range(4)]
    even, odd = jnp.concatenate([parts[0], parts[2]]), jnp.concatenate([parts[1], parts[3]])
    first = at_ref[4] == 0
    return jnp.where(first, even, odd), jnp.where(first, odd, even)


def spare_rows(row, n):
    count = -(-row.shape[1] // n)
    row = jnp.concatenate([row, jnp.zeros((1, count * n - row.shape[1]), F32)], axis=1) if count * n > row.shape[1] else row
    at = lax.broadcasted_iota(jnp.int32, (SPARE, n), 0)
    rows = jnp.zeros((SPARE, n), F32)
    for k in range(count):
        rows = jnp.where(at == k, row[:, k * n : (k + 1) * n], rows)
    return rows.astype(BF16)


def from_spare(rows, total):
    n = rows.shape[1]
    return jnp.concatenate([rows[k : k + 1, :] for k in range(-(-total // n))], axis=1)[:, :total].astype(F32)


def share_kernel(at_ref, kept_ref, came_ref, gb_ref, low_ref, high_ref, a_own, a_sent, b_own, b_sent, gb_out, *, rows):
    h = kept_ref.shape[0]
    n_a, n_b = a_own.shape[1], b_own.shape[1]
    for g in range(h // (4 * rows)):
        at = slice(g * 4 * rows, (g + 1) * 4 * rows)
        value = (kept_ref[at, :].astype(F32) + came_ref[at, :].astype(F32)).astype(BF16)
        mine, other = halves(at_ref, value[:, :n_a], rows)
        at = slice(g * 2 * rows, (g + 1) * 2 * rows)
        a_own[at, :] = mine
        a_sent[at, :] = other
        here = g % 2 == at_ref[2]
        at = slice(g // 2 * 4 * rows, (g // 2 + 1) * 4 * rows)

        @pl.when(here)
        def _():
            b_own[at, :] = value[:, n_a:]

        @pl.when(jnp.logical_not(here))
        def _():
            b_sent[at, :] = value[:, n_a:]

    total = gb_ref[0:1, :] + came_ref[h : h + 1, :].astype(F32)
    gb_out[...] = jnp.broadcast_to(total, gb_out.shape)
    a_sent[h // 2 :, :] = spare_rows(total, n_a)
    b_sent[h // 2 :, :] = jnp.zeros((SPARE, n_b), BF16)


def share_rows(at, kept, came, bias, rows, after):
    h, n = kept.shape
    n_a = n * FIRST // 8
    n_b = n - n_a
    return pl.pallas_call(
        functools.partial(share_kernel, rows=rows),
        in_specs=[SMEM] + [WHOLE] * 3 + [ANY] * 2,
        out_specs=[WHOLE] * 5,
        out_shape=[
            pltpu.VMEM((h // 2, n_a), BF16),
            pltpu.VMEM((h // 2 + SPARE, n_a), BF16),
            pltpu.VMEM((h // 2, n_b), BF16),
            pltpu.VMEM((h // 2 + SPARE, n_b), BF16),
            jax.ShapeDtypeStruct((8, n), F32),
        ],
        compiler_params=params(10),
        cost_estimate=cost(0, h * n * 8),
        name="share",
    )(at, kept, came, bias, *after)


def fold_kernel(at_ref, a_ref, a_came, b_ref, b_came, gb_ref, _, a_own, a_sent, b_own, b_sent, gb_out, *, rows):
    lo, two = at_ref[2], 2 * rows
    n = a_ref.shape[1]
    planes = a_ref.shape[0] // (2 * two)
    for z in range(planes):
        out = slice(z * two, (z + 1) * two)
        near = pl.ds(pl.multiple_of((2 * z + lo) * two, two), two)
        far = pl.ds(pl.multiple_of((2 * z + 1 - lo) * two, two), two)
        a_own[out, :] = a_ref[near, :].astype(F32) + a_came[near, :].astype(F32)
        a_sent[out, :] = (a_ref[far, :].astype(F32) + a_came[far, :].astype(F32)).astype(BF16)
        at = slice(z * 2 * two, (z + 1) * 2 * two)
        mine, other = halves(at_ref, b_ref[at, :].astype(F32) + b_came[at, :].astype(F32), rows)
        b_own[out, :] = mine
        b_sent[out, :] = other.astype(BF16)
    total = gb_ref[0:1, :] + from_spare(a_came[a_ref.shape[0] :, :], gb_ref.shape[1])
    gb_out[...] = jnp.broadcast_to(total, gb_out.shape)
    a_sent[planes * two :, :] = spare_rows(total, n)


def fold(at, a_own, a_came, b_own, b_came, bias, rows, after):
    count, n_a, n_b = b_own.shape[0] // 2, a_own.shape[1], b_own.shape[1]
    return pl.pallas_call(
        functools.partial(fold_kernel, rows=rows),
        in_specs=[SMEM] + [WHOLE] * 5 + [ANY],
        out_specs=[WHOLE] * 5,
        out_shape=[
            jax.ShapeDtypeStruct((count, n_a), F32),
            jax.ShapeDtypeStruct((count + SPARE, n_a), BF16),
            jax.ShapeDtypeStruct((count, n_b), F32),
            jax.ShapeDtypeStruct((count, n_b), BF16),
            jax.ShapeDtypeStruct(bias.shape, F32),
        ],
        compiler_params=params(22),
        cost_estimate=cost(0, b_own.size * 9),
        name="fold",
    )(at, a_own, a_came, b_own, b_came, bias, after)


def part_kernel(at_ref, a_ref, a_came, b_ref, b_came, gb_ref, *refs, rows, planes):
    gb_out, own, *sent = refs[-1 - planes :]
    two = 2 * rows
    n = a_ref.shape[1]
    total = gb_ref[0:1, :] + from_spare(a_came[a_ref.shape[0] :, :], gb_ref.shape[1])
    gb_out[...] = jnp.broadcast_to(total, gb_out.shape)
    for k in range(planes):
        at = pl.ds(pl.multiple_of(lax.rem(at_ref[3] + k, planes) * two, two), two)
        out = own if k == 0 else sent[k - 1]
        out[:two, :n] = (a_ref[at, :] + a_came[at, :].astype(F32)).astype(out.dtype)
        out[:two, n:] = (b_ref[at, :] + b_came[at, :].astype(F32)).astype(out.dtype)
        if k:
            out[two:, :] = jnp.broadcast_to(total, (SPARE, total.shape[1])).astype(BF16)


def part_planes(at, a_own, a_came, b_own, b_came, bias, rows, planes, after):
    n = a_own.shape[1] + b_own.shape[1]
    return pl.pallas_call(
        functools.partial(part_kernel, rows=rows, planes=planes),
        in_specs=[SMEM] + [WHOLE] * 5 + [ANY] * len(after),
        out_specs=[WHOLE] * (1 + planes),
        out_shape=[jax.ShapeDtypeStruct(bias.shape, F32), jax.ShapeDtypeStruct((2 * rows, n), F32)]
        + [jax.ShapeDtypeStruct((2 * rows + SPARE, n), BF16)] * (planes - 1),
        compiler_params=params(14),
        cost_estimate=cost(0, a_own.size * 18),
        name="part_planes",
    )(at, a_own, a_came, b_own, b_came, bias, *after)


def finish_kernel(at_ref, gb_ref, own, *refs, rows):
    came, mine_ref, other_ref = refs[:-3], refs[-2], refs[-1]
    total, bias = own[...], gb_ref[0:1, :]
    for ref in came:
        total = total + ref[: 2 * rows, :].astype(F32)
        bias = bias + ref[2 * rows : 2 * rows + 1, :].astype(F32)
    first = at_ref[1] == 0
    low, high = total[:rows], total[rows:]
    bias = jnp.broadcast_to(bias, (8, bias.shape[1]))
    mine_ref[:rows, :], other_ref[:rows, :] = jnp.where(first, low, high), jnp.where(first, high, low)
    mine_ref[rows:, :], other_ref[rows:, :] = bias, bias


def finish(at, bias, own, came, rows, after):
    shape = jax.ShapeDtypeStruct((rows + 8, own.shape[1]), F32)
    return pl.pallas_call(
        functools.partial(finish_kernel, rows=rows),
        in_specs=[SMEM] + [WHOLE] * (2 + len(came)) + [ANY],
        out_specs=[WHOLE] * 2,
        out_shape=[shape] * 2,
        compiler_params=params(10),
        cost_estimate=cost(0, own.size * 8),
        name="finish",
    )(at, bias, own, *came, after)


def scatter_bound_kernel(c_ref, g_ref, *refs, count):
    *outs, part, sem = refs[len(refs) - 2 - count :]
    i = pl.program_id(0)
    part[i] = dot(c_ref[...], g_ref[...], 1, 0).astype(BF16)
    copies = [pltpu.make_async_copy(part.at[k], out, sem.at[k]) for k, out in enumerate(outs)]
    for k, copy in enumerate(copies):

        @pl.when(i == k)
        def _():
            copy.start()

    @pl.when(i == len(outs) - 1)
    def _():
        for copy in copies:
            copy.wait()


def scatter_bound(adjacency, grads, after):
    live, h = grads.shape
    blocks = (adjacency.shape[0] - live) // BOUND - 1
    return pl.pallas_call(
        functools.partial(scatter_bound_kernel, count=blocks),
        grid=(blocks,),
        in_specs=[pl.BlockSpec((BOUND, live), lambda i: (i + live // BOUND, 0)), resident((live, h))] + [ANY] * len(after),
        out_specs=[ANY] * blocks,
        out_shape=[pltpu.HBM((BOUND, h), BF16)] * blocks,
        scratch_shapes=[pltpu.VMEM((blocks, BOUND, h), BF16), pltpu.SemaphoreType.DMA((blocks,))],
        compiler_params=params(22),
        cost_estimate=cost(2 * blocks * BOUND * live * h, live * h * 4),
        name="scatter_bound",
    )(far(adjacency), grads, *after)


def grad_rows_kernel(c_ref, g_ref, *refs, low, tiles):
    o_ref, lead_ref, w, sem = refs[-4:]
    i = pl.program_id(0)
    copy = pltpu.make_async_copy(refs[0].at[:, pl.ds(0, w.shape[1])], w, sem)

    @pl.when(i == 0)
    def _():
        copy.start()

    @pl.when(low + i < tiles)
    def _():
        total = dot(c_ref[...], g_ref[...], 1, 0)

        @pl.when(i == 0)
        def _():
            lead_ref[...] = total if low == 0 else jnp.zeros_like(lead_ref)
            copy.wait()

        @pl.when(low + i > 0)
        def _():
            o_ref[...] = dot(total.astype(BF16), w[...], 1, 1)

    @pl.when(low + i == tiles)
    def _():
        o_ref[...] = jnp.zeros_like(o_ref)


def grad_rows(adjacency, grads, weight, nodes, low, high, before, after):
    live, h = grads.shape
    tiles = live // TILE
    extra = [] if before is None else [before]
    outs = [jax.ShapeDtypeStruct((nodes, h), F32), TOKEN if low else jax.ShapeDtypeStruct((TILE, h), F32)]
    out_specs = [pl.BlockSpec((TILE, h), lambda i: (low + i, 0)), resident((8, 128) if low else (TILE, h))]
    return pl.pallas_call(
        functools.partial(grad_rows_kernel, low=low, tiles=tiles),
        grid=(high - low,),
        in_specs=[
            pl.BlockSpec((TILE, live), lambda i: (jnp.minimum(low + i, tiles - 1), 0)),
            resident((live, h)),
            ANY,
        ]
        + [ANY] * (len(extra) + len(after)),
        out_specs=out_specs,
        scratch_shapes=[pltpu.VMEM((h, h), BF16), pltpu.SemaphoreType.DMA],
        out_shape=outs,
        input_output_aliases={3: 0} if extra else {},
        compiler_params=params(30),
        cost_estimate=cost((2 * live + 2 * h) * (high - low) * TILE * h, live * h * 8),
        name="grad_rows",
    )(far(adjacency), grads, far(weight), *extra, *after)


def back_kernel(outer_ref, low_ref, own_ref, came_ref, high_ref, _, outer_back, own_back):
    i = pl.program_id(0)
    half = pl.num_programs(0) // 2
    early = (i < half).astype(F32)
    outer_back[...] = (outer_ref[...].astype(F32) + early * low_ref[...].astype(F32)).astype(BF16)
    own = own_ref[...].astype(F32) + came_ref[...].astype(F32)
    own_back[...] = (own + (1 - early) * high_ref[...].astype(F32)).astype(BF16)


def back(outer, low, own, came, high, after):
    rows, h = own.shape
    steps = 2
    half = steps // 2
    whole = pl.BlockSpec((rows // steps, h), lambda i: (i, 0))
    first = pl.BlockSpec((rows // steps, h), lambda i: (jnp.minimum(i, half - 1), 0))
    second = pl.BlockSpec((rows // steps, h), lambda i: (jnp.maximum(i - half, 0), 0))
    return pl.pallas_call(
        back_kernel,
        grid=(steps,),
        in_specs=[whole, first, whole, whole, second, ANY],
        out_specs=[whole] * 2,
        out_shape=[jax.ShapeDtypeStruct((rows, h), BF16)] * 2,
        compiler_params=params(10),
        cost_estimate=cost(0, own.size * 12),
        name="back",
    )(far(outer), low, far(own), came, high, after)


def grad_lead_kernel(lead_ref, *refs):
    came, (w_ref, _, o_ref, token_ref, total) = refs[:3], refs[3:]

    @pl.when(pl.program_id(0) == 0)
    def _():
        value = lead_ref[...]
        for ref in came:
            value = value + ref[...].astype(F32)
        total[...] = value.astype(BF16)
        token_ref[...] = jnp.zeros_like(token_ref)

    o_ref[...] = dot(total[...], w_ref[...], 1, 1)


def grad_lead(lead, came, weight, grads):
    rows, h = lead.shape
    return pl.pallas_call(
        grad_lead_kernel,
        grid=(1,),
        in_specs=[resident((rows, h))] * 4 + [pl.BlockSpec((h, h), lambda i: (i, 0)), ANY],
        out_specs=[pl.BlockSpec((rows, h), lambda i: (0, i)), resident((8, 128))],
        out_shape=[jax.ShapeDtypeStruct(grads.shape, F32), TOKEN],
        scratch_shapes=[pltpu.VMEM((rows, h), BF16)],
        input_output_aliases={5: 0},
        compiler_params=params(20),
        cost_estimate=cost(2 * rows * h * h, h * h * 2),
        name="grad_lead",
    )(lead, *came, weight, grads)


def body(features, weight, bias, neighbours, degrees, cluster_sizes, cotangent):
    axes = ("blk", "wa")
    n_blk, n_wa = lax.axis_size("blk"), lax.axis_size("wa")
    devices, n_hi = n_blk * n_wa, n_blk // 4
    blk, wa = lax.axis_index("blk"), lax.axis_index("wa")
    core, lo, hi = blk % 2, (blk // 2) % 2, blk // 4
    nodes, h = features.shape
    share, n = h // devices, h // 2
    live = min(nodes, -(-(-(-CMAX // n_wa)) // TILE) * TILE)

    def permute(value, target):
        pairs = [(b * n_wa + w, target(b, w)) for b in range(n_blk) for w in range(n_wa)]
        return lax.ppermute(value, axes, [(s, b * n_wa + w) for s, (b, w) in pairs])

    def swap_wa(value):
        return permute(value, lambda b, w: (b, 1 - w))

    def swap_core(value):
        return permute(value, lambda b, w: (b ^ 1, w))

    def swap_outer(value, parity=None):
        pairs = [(b, (b + (1 if b % 2 else -1)) % n_blk) for b in range(n_blk)]
        chosen = [(b, t) for b, t in pairs if parity is None or (b if b % 2 else t) // 2 % 2 == parity]
        return lax.ppermute(value, axes, [(b * n_wa + w, t * n_wa + w) for b, t in chosen for w in range(n_wa)])

    def swap_lo(value):
        return permute(value, lambda b, w: (b ^ 2, w))

    def rotate_hi(value, k):
        return permute(value, lambda b, w: ((b + 4 * k) % n_blk, w))

    leading = features[:BOUND]
    partner = swap_wa(leading)
    row_same = swap_outer(leading, 0)

    sheet = jnp.concatenate([weight, jnp.broadcast_to(bias[:, None], (share, 128))], axis=1)
    planes = [rotate_hi(sheet, k) for k in range(1, n_hi)]

    live_count = (cluster_sizes[0] - wa + n_wa - 1) // n_wa
    table = neighbours[:, :live]
    beyond = table - nodes
    segment, within = beyond // (n_wa * BOUND), beyond % (n_wa * BOUND)
    same = within // BOUND == wa
    row = within % BOUND
    side = jnp.where(same, 0, BOUND) + row
    inner = (segment == 2) == (core == 0)
    away = jnp.where(inner, live + BOUND, live + BOUND + n_wa * BOUND) + side
    home = jnp.where(same, row, live + row)
    index = jnp.where(table < nodes, table, jnp.where(segment == 0, home, away))
    valid = jnp.arange(FANOUT, dtype=jnp.int32)[:, None] < degrees[None, :live]
    index = jnp.where(valid, index, -1)
    inverse = (1.0 / (degrees[:live].astype(F32) + 1.0))[:, None]
    at = jnp.stack([live_count, core, lo, hi, wa]).astype(jnp.int32)

    adjacency = counts(index, (live + (1 + 2 * n_wa) * BOUND) // TILE, [inverse, at])
    partner, late_leading, *planes = tie([partner, leading, *planes], [far(adjacency)])
    sheet = jnp.concatenate([sheet, *planes])
    half_sheet, row_sheet = swap_wa(sheet), swap_lo(sheet)
    inner_same, inner_other = swap_core(late_leading), swap_core(partner)
    plane_same = swap_outer(late_leading, 1)
    part = gather(adjacency, features, (partner, inner_same, inner_other), live, [])
    half_sheet, row_same, plane_same = tie([half_sheet, row_same, plane_same], [far(part)])
    outer_same = jnp.where((blk // 2 % 2 == 0) == (core == 1), row_same, plane_same)
    outer_other = swap_wa(outer_same)
    cut = n_hi * 3 // 4
    row_tail, outer_other = tie([row_sheet[cut * share :], outer_other], [])
    late = list(tie([swap_lo(half_sheet[: cut * share]), swap_wa(row_tail)], []))
    pieces = [sheet, half_sheet, row_sheet]
    pieces = pieces + [swap_core(value) for value in pieces]
    matrix = place(at, pieces, [(k, 0) for k in (0, 1, 2, 4, 5, 6)], n_hi)
    output, grads, mixed, low, bias_sum, far_low, far_high, matrix = layer(
        at,
        part,
        adjacency,
        outer_same,
        outer_other,
        inverse,
        cotangent,
        late + [swap_core(value) for value in late],
        [(3, 0), (3, cut), (7, 0), (7, cut)],
        matrix,
        n_hi,
    )
    sent, token = weight_share(at, mixed, low, bias_sum, False, [])
    came = swap_core(sent)
    kept, bias_sum = weight_share(at, mixed, low, bias_sum, True, [token])

    far_low, far_high = swap_wa(far_low), swap_outer(far_high)
    a, a_sent, b, b_sent, bias_sum = share_rows(at, kept, came, bias_sum, share, [far_low, far_high])
    a_came, b_came = swap_wa(a_sent), swap_lo(b_sent)

    own_bound, inner_same_g, inner_other_g, outer_same_g = scatter_bound(adjacency, grads, [bias_sum])
    own_came, inner_came = swap_core(inner_other_g), swap_core(inner_same_g)
    split, tiles = live // TILE // 3, -(-nodes // TILE)
    grad_features, lead = grad_rows(adjacency, grads, matrix, nodes, 0, split, None, [far(own_bound)])
    outer_back, own_back = back(outer_same_g, far_low, own_bound, own_came, far_high, lead)
    outer_back = swap_outer(outer_back)
    a, a_sent, b, b_sent, bias_sum = fold(at, a, a_came, b, b_came, bias_sum, share, own_back)
    a_came, b_came = swap_lo(a_sent), swap_wa(b_sent)
    late = live // TILE * 5 // 6
    grad_features, token = grad_rows(
        adjacency, grads, matrix, nodes, split, late, grad_features, [bias_sum]
    )
    bias_sum, own, *rest = part_planes(
        at, a, a_came, b, b_came, bias_sum, share, n_hi, [token]
    )
    (own_back,) = tie([own_back], [own])
    returned = (inner_came, outer_back, swap_wa(own_back))
    rest = [rotate_hi(value, k + 1) for k, value in enumerate(rest)]
    grad_features, _ = grad_rows(adjacency, grads, matrix, nodes, late, tiles, grad_features, [bias_sum])
    grad_features, token = grad_lead(lead, returned, matrix, grad_features)
    mine, other = finish(at, bias_sum, own, rest, share, token)
    other = swap_core(other)
    first, second = jnp.where(core == 0, mine, other), jnp.where(core == 0, other, mine)
    grad_weight = jnp.concatenate([first[:share], second[:share]], axis=1)
    bias_row = jnp.concatenate([first[share], second[share]])
    grad_bias = lax.dynamic_slice_in_dim(bias_row, (blk * n_wa + wa) * share, share)
    return (output, grad_features, grad_weight, grad_bias)


def solution(mesh):
    return jax.shard_map(
        body,
        mesh=mesh,
        in_specs=(
            P(("blk", "wa"), None),
            P(("blk", "wa"), None),
            P(("blk", "wa")),
            P(None, ("blk", "wa")),
            P(("blk", "wa")),
            P("blk"),
            P(("blk", "wa"), None),
        ),
        out_specs=(
            P(("blk", "wa"), None),
            P(("blk", "wa"), None),
            P(("blk", "wa"), None),
            P(("blk", "wa")),
        ),
        check_vma=False,
    )
```
